512 devices in a mesh: lon: 16 (over x, z_hi, core), lat: 32 (over z_lo, y).
Axes of the slice: x: 4, y: 4, z: 16 (z_hi: 2, z_lo: 8; z = z_hi * 8 + z_lo), core: 2. Of those that a mesh axis runs over, the one named last changes fastest.
Arguments:
- features: bfloat16 [256, 1440, 128], P('lat', 'lon'), may hold values from -6 to 6
- queries: bfloat16 [256, 1440, 128], P('lat', 'lon'), may hold values from -200 to 200
- attn_keys: bfloat16 [256, 1440, 128], P('lat', 'lon'), may hold values from -4.5 to 4.5
- attn_values: bfloat16 [256, 1440, 128], P('lat', 'lon'), may hold values from -6 to 6
- cotangent: bfloat16 [256, 1440, 128], P('lat', 'lon'), may hold values from -6 to 6
- conv_near: bfloat16 [3, 3, 128, 128], replicated, may hold values from -0.1875 to 0.1875
- conv_wide: bfloat16 [3, 3, 128, 128], replicated, may hold values from -0.1875 to 0.1875
- proj_qkv: bfloat16 [128, 384], replicated, may hold values from -0.5 to 0.5
- proj_out: bfloat16 [128, 128], replicated, may hold values from -0.5 to 0.5
Outputs:
- feature_grad: bfloat16 [256, 1440, 128], P('lat', 'lon')
- conv_near_grad: float32 [3, 3, 128, 128], replicated
- conv_wide_grad: float32 [3, 3, 128, 128], replicated
- proj_qkv_grad: float32 [128, 384], replicated
- proj_out_grad: float32 [128, 128], replicated
The draws below stay inside these ranges and needn't reach their ends.
All inputs are finite; a program needn't handle non-finite values.
Results may differ from the reference program's by a relative error of at most 0.012.
Values may be sent and summed in bfloat16 or wider, within the bound.
No kernel may reach another device: no remote copies, remote signals or barrier semaphores. Data moves between devices by JAX's collectives and lax.ppermute only.
A program may use at most 64 MiB of HBM per device.

```python
import jax
import jax.numpy as jnp
from jax import lax

C = 128
HEADS = 8
LAT = 256
LON = 1440


def shared_normal(key):
    return jnp.clip(jax.random.normal(key, (LAT, LON, C), jnp.float32), -4.5, 4.5)


def draw_attn_keys(key, part):
    key_field = shared_normal(key)
    return key_field.astype(jnp.bfloat16)


def draw_queries(key, part):
    key = jax.random.fold_in(key, 7)
    first = jax.random.fold_in(key, 0)
    drawn = jnp.clip(jax.random.normal(first, (LAT, LON, C), jnp.float32), -4.5, 4.5)
    return drawn.astype(jnp.bfloat16)


def block_scale(key, shape, cuts, smallest, top_value):
    def one(position, shards_of):
        draws = jax.random.uniform(jax.random.fold_in(jax.random.fold_in(key, 6), position), (shards_of,), jnp.float32, smallest / len(cuts), top_value / len(cuts))
        return jnp.repeat(jnp.exp(draws), shape[position] // shards_of).reshape((-1,) + (1,) * (len(shape) - position - 1))

    factor_of = one(*cuts[0])
    for cut in cuts[1:]:
        factor_of = factor_of * one(*cut)
    return factor_of


def scatter_about(key, shape, deviation, bound, cuts=(), dtype=jnp.bfloat16):
    drawn = deviation * jax.random.normal(key, shape, jnp.float32)
    if cuts:
        drawn = drawn * block_scale(key, shape, cuts, -0.22, 0.18)
    return jnp.clip(drawn, -bound, bound).astype(dtype)


def setup_inputs(seed: int = 0) -> dict:
    splits = jax.random.split(jax.random.key(seed), 10)
    features = scatter_about(splits[0], (LAT, LON, C), 1.0, 6.0, ((0, 32), (1, 16)))
    queries = draw_queries(jax.random.fold_in(splits[9], 71), 0)
    attn_keys = draw_attn_keys(jax.random.fold_in(splits[9], 71), 0)
    attn_values = scatter_about(splits[3], (LAT, LON, C), 1.0, 6.0, ((0, 32), (1, 16)))
    cotangent = scatter_about(splits[4], (LAT, LON, C), 1.0, 6.0, ((0, 32), (1, 16)))
    conv_near = scatter_about(splits[5], (3, 3, C, C), (9 * C) ** -0.5, 0.1875)
    conv_wide = scatter_about(splits[6], (3, 3, C, C), (9 * C) ** -0.5, 0.1875)
    proj_qkv = scatter_about(splits[7], (C, 3 * C), C ** -0.5, 0.5)
    proj_out = scatter_about(splits[8], (C, C), C ** -0.5, 0.5)
    return {"features": features, "queries": queries, "attn_keys": attn_keys, "attn_values": attn_values, "cotangent": cotangent, "conv_near": conv_near, "conv_wide": conv_wide, "proj_qkv": proj_qkv, "proj_out": proj_out}


GELU_COEF = 0.7978845608028654
CUBIC_COEF = 0.044715


def gelu_value(pre_act):
    tanh_val = jnp.tanh(GELU_COEF * (pre_act + CUBIC_COEF * pre_act * pre_act * pre_act))
    return 0.5 * pre_act * (1.0 + tanh_val)


def gelu_slope(pre_act):
    tanh_val = jnp.tanh(GELU_COEF * (pre_act + CUBIC_COEF * pre_act * pre_act * pre_act))
    inner_d = GELU_COEF * (1.0 + 3.0 * CUBIC_COEF * pre_act * pre_act)
    return 0.5 * (1.0 + tanh_val) + 0.5 * pre_act * (1.0 - tanh_val * tanh_val) * inner_d


def contract_rows(left, right):
    return lax.dot_general(left, right, (((0,), (0,)), ((), ())), preferred_element_type=jnp.float32)


def conv_taps(padded, weight, spread, row_count, col_count):
    channels = padded.shape[-1]
    total_sum = jnp.zeros((row_count * col_count, weight.shape[-1]), jnp.float32)
    for row_tap in range(3):
        for col_tap in range(3):
            window = padded[row_tap * spread:row_tap * spread + row_count, col_tap * spread:col_tap * spread + col_count]
            total_sum = total_sum + jnp.dot(window.reshape(-1, channels), weight[row_tap, col_tap], preferred_element_type=jnp.float32)
    return total_sum.reshape(row_count, col_count, -1)


def conv_back(padded, weight, spread, row_count, col_count):
    channels = padded.shape[-1]
    total_sum = jnp.zeros((row_count * col_count, weight.shape[-2]), jnp.float32)
    for row_tap in range(3):
        for col_tap in range(3):
            row_at = (2 - row_tap) * spread
            col_at = (2 - col_tap) * spread
            window = padded[row_at:row_at + row_count, col_at:col_at + col_count]
            total_sum = total_sum + jnp.dot(window.reshape(-1, channels), weight[row_tap, col_tap].T, preferred_element_type=jnp.float32)
    return total_sum.reshape(row_count, col_count, -1)


def weight_terms(padded, gradient, spread, row_count, col_count):
    channels = padded.shape[-1]
    flat_grad = gradient.reshape(-1, gradient.shape[-1])
    tap_list = []
    for row_tap in range(3):
        for col_tap in range(3):
            window = padded[row_tap * spread:row_tap * spread + row_count, col_tap * spread:col_tap * spread + col_count]
            tap_list.append(contract_rows(window.reshape(-1, channels), flat_grad))
    return jnp.stack(tap_list).reshape(3, 3, channels, -1)


def attend_head(query_h, key_h, value_h, dout_h):
    scale = query_h.shape[-1] ** -0.5
    scores = jnp.dot(query_h, key_h.T, preferred_element_type=jnp.float32) * scale
    top_val = jnp.max(scores, axis=1, keepdims=True)
    raised = jnp.exp(scores - top_val)
    probs = raised / jnp.sum(raised, axis=1, keepdims=True)
    probs_low = probs.astype(jnp.bfloat16)
    mixed = jnp.dot(probs_low, value_h, preferred_element_type=jnp.float32).astype(jnp.bfloat16)
    prob_grad = jnp.dot(dout_h, value_h.T, preferred_element_type=jnp.float32)
    delta_sum = jnp.sum(dout_h.astype(jnp.float32) * mixed.astype(jnp.float32), axis=1, keepdims=True)
    score_grad = (probs * (prob_grad - delta_sum) * scale).astype(jnp.bfloat16)
    query_grad = jnp.dot(score_grad, key_h, preferred_element_type=jnp.float32).astype(jnp.bfloat16)
    key_grad = contract_rows(score_grad, query_h).astype(jnp.bfloat16)
    value_grad = contract_rows(probs_low, dout_h).astype(jnp.bfloat16)
    return mixed, query_grad, key_grad, value_grad


def attend_row(query_row, key_row, value_row, dout_row):
    length, channels = query_row.shape

    def by_head(field):
        return field.reshape(length, HEADS, channels // HEADS).transpose(1, 0, 2)

    def merge_heads(field):
        return field.transpose(1, 0, 2).reshape(length, channels)

    results = lax.map(lambda pieces: attend_head(*pieces), (by_head(query_row), by_head(key_row), by_head(value_row), by_head(dout_row)))
    return tuple(merge_heads(field) for field in results)


def pad_grid(field, width):
    field = jnp.pad(field, ((width, width), (0, 0), (0, 0)))
    return jnp.concatenate([field[:, -width:], field, field[:, :width]], axis=1)


def reference(features, queries, attn_keys, attn_values, cotangent, conv_near, conv_wide, proj_qkv, proj_out):
    channels = features.shape[-1]
    factor = float(LAT * LON) ** -0.5
    pad_x = pad_grid(features, 1)
    pre_near = conv_taps(pad_x, conv_near, 1, LAT, LON)
    hidden_one = (features.astype(jnp.float32) + gelu_value(pre_near)).astype(jnp.bfloat16)
    pad_hidden = pad_grid(hidden_one, 4)
    pre_wide = conv_taps(pad_hidden, conv_wide, 4, LAT, LON)
    hidden_two = (hidden_one.astype(jnp.float32) + gelu_value(pre_wide)).astype(jnp.bfloat16)
    flat_cot = cotangent.reshape(-1, channels)
    out_grad = jnp.dot(flat_cot, proj_out.T, preferred_element_type=jnp.float32).astype(jnp.bfloat16).reshape(LAT, LON, channels)
    mixed, query_grad, key_grad, value_grad = lax.map(lambda pieces: attend_row(*pieces), (queries, attn_keys, attn_values, out_grad))
    proj_out_grad = contract_rows(mixed.reshape(-1, channels), flat_cot) * factor
    stacked = jnp.concatenate([query_grad, key_grad, value_grad], axis=-1).reshape(-1, 3 * channels)
    attn_grad = jnp.dot(stacked, proj_qkv.T, preferred_element_type=jnp.float32).astype(jnp.bfloat16).reshape(LAT, LON, channels)
    proj_qkv_grad = contract_rows(hidden_two.reshape(-1, channels), stacked) * factor
    outer_total = cotangent.astype(jnp.float32) + attn_grad.astype(jnp.float32)
    wide_grad = (outer_total * gelu_slope(pre_wide)).astype(jnp.bfloat16)
    near_total = outer_total + conv_back(pad_grid(wide_grad, 4), conv_wide, 4, LAT, LON)
    conv_wide_grad = weight_terms(pad_hidden, wide_grad, 4, LAT, LON) * factor
    near_grad = (near_total * gelu_slope(pre_near)).astype(jnp.bfloat16)
    feature_grad = (near_total + conv_back(pad_grid(near_grad, 1), conv_near, 1, LAT, LON)).astype(jnp.bfloat16)
    conv_near_grad = weight_terms(pad_x, near_grad, 1, LAT, LON) * factor
    return feature_grad, conv_near_grad, conv_wide_grad, proj_qkv_grad, proj_out_grad
```

```python
import jax
import jax.numpy as jnp
from jax import lax
from jax.sharding import Mesh, PartitionSpec as P

HEADS = 8
GELU_COEF = 0.7978845608028654
CUBIC_COEF = 0.044715

LON_AXES = ("x", "zh", "core")
LAT_AXES = ("zl", "y")
PLANE = ("x", "core")
SWAP = [(0, 1), (1, 0)]


def gelu_value(pre_act):
    tanh_val = jnp.tanh(GELU_COEF * (pre_act + CUBIC_COEF * pre_act * pre_act * pre_act))
    return 0.5 * pre_act * (1.0 + tanh_val)


def gelu_slope(pre_act):
    tanh_val = jnp.tanh(GELU_COEF * (pre_act + CUBIC_COEF * pre_act * pre_act * pre_act))
    inner_d = GELU_COEF * (1.0 + 3.0 * CUBIC_COEF * pre_act * pre_act)
    return 0.5 * (1.0 + tanh_val) + 0.5 * pre_act * (1.0 - tanh_val * tanh_val) * inner_d


def contract_rows(left, right):
    return lax.dot_general(
        left, right, (((0,), (0,)), ((), ())), preferred_element_type=jnp.float32
    )


def conv_taps(padded, weight, spread, row_count, col_count):
    channels = padded.shape[-1]
    total_sum = jnp.zeros((row_count * col_count, weight.shape[-1]), jnp.float32)
    for row_tap in range(3):
        for col_tap in range(3):
            window = padded[
                row_tap * spread : row_tap * spread + row_count,
                col_tap * spread : col_tap * spread + col_count,
            ]
            total_sum = total_sum + jnp.dot(
                window.reshape(-1, channels),
                weight[row_tap, col_tap],
                preferred_element_type=jnp.float32,
            )
    return total_sum.reshape(row_count, col_count, -1)


def conv_back(padded, weight, spread, row_count, col_count):
    channels = padded.shape[-1]
    total_sum = jnp.zeros((row_count * col_count, weight.shape[-2]), jnp.float32)
    for row_tap in range(3):
        for col_tap in range(3):
            row_at = (2 - row_tap) * spread
            col_at = (2 - col_tap) * spread
            window = padded[row_at : row_at + row_count, col_at : col_at + col_count]
            total_sum = total_sum + jnp.dot(
                window.reshape(-1, channels),
                weight[row_tap, col_tap].T,
                preferred_element_type=jnp.float32,
            )
    return total_sum.reshape(row_count, col_count, -1)


def weight_terms(padded, gradient, spread, row_count, col_count):
    channels = padded.shape[-1]
    flat_grad = gradient.reshape(-1, gradient.shape[-1])
    tap_list = []
    for row_tap in range(3):
        for col_tap in range(3):
            window = padded[
                row_tap * spread : row_tap * spread + row_count,
                col_tap * spread : col_tap * spread + col_count,
            ]
            tap_list.append(contract_rows(window.reshape(-1, channels), flat_grad))
    return jnp.stack(tap_list).reshape(9 * channels, -1)


def exchange_lon(block, width):
    ring = [(i, (i + 1) % 16) for i in range(16)]
    low = lax.ppermute(block[:, -width:], LON_AXES, ring)
    high = lax.ppermute(block[:, :width], LON_AXES, [(b, a) for a, b in ring])
    return low, high


def exchange_lat(bottom, top):
    chain = [(i, i + 1) for i in range(31)]
    low = lax.ppermute(bottom, LAT_AXES, chain)
    high = lax.ppermute(top, LAT_AXES, [(b, a) for a, b in chain])
    return low, high


def inside_rows(lat_at, row_count, width):
    at = lat_at * row_count + jnp.arange(row_count + 2 * width, dtype=jnp.int32) - width
    return ((at >= 0) & (at < 32 * row_count))[:, None, None]


def attend_head(query_h, dout_h, key_h, value_h):
    scale = query_h.shape[-1] ** (-0.5)
    scores = jnp.dot(query_h, key_h.T, preferred_element_type=jnp.float32) * scale
    top_val = jnp.max(scores, axis=1, keepdims=True)
    raised = jnp.exp(scores - top_val)
    probs = raised / jnp.sum(raised, axis=1, keepdims=True)
    probs_low = probs.astype(jnp.bfloat16)
    mixed = jnp.dot(probs_low, value_h, preferred_element_type=jnp.float32).astype(jnp.bfloat16)
    prob_grad = jnp.dot(dout_h, value_h.T, preferred_element_type=jnp.float32)
    delta_sum = jnp.sum(
        dout_h.astype(jnp.float32) * mixed.astype(jnp.float32), axis=1, keepdims=True
    )
    score_grad = (probs * (prob_grad - delta_sum) * scale).astype(jnp.bfloat16)
    query_grad = jnp.dot(score_grad, key_h, preferred_element_type=jnp.float32).astype(jnp.bfloat16)
    key_grad = contract_rows(score_grad, query_h).astype(jnp.bfloat16)
    value_grad = contract_rows(probs_low, dout_h).astype(jnp.bfloat16)
    return (mixed, query_grad, key_grad, value_grad)


def reduce_all(terms):
    rows, channels = terms.shape
    part = rows // 32
    piece = part * channels // 16
    band = lax.all_to_all(
        terms.reshape(32, part, channels), ("x", "y", "core"), 0, 0, tiled=True
    )
    band = band.astype(jnp.float32).sum(0).astype(jnp.bfloat16).reshape(16, piece)
    band = lax.all_to_all(band, ("zh", "zl"), 0, 0, tiled=True)
    band = band.astype(jnp.float32).sum(0).astype(jnp.bfloat16)
    band = lax.all_to_all(
        jnp.broadcast_to(band[None], (16, piece)), ("zh", "zl"), 0, 0, tiled=True
    ).reshape(part, channels)
    return lax.all_to_all(
        jnp.broadcast_to(band[None], (32, part, channels)), ("x", "y", "core"), 0, 0, tiled=True
    ).reshape(rows, channels)


def on_device(
    features, queries, attn_keys, attn_values, cotangent, conv_near, conv_wide, proj_qkv, proj_out
):
    rows, cols, channels = features.shape
    head_width = channels // HEADS
    factor = float(rows * cols * 512) ** (-0.5)
    lat_at = lax.axis_index(LAT_AXES)

    def to_rows(field):
        return lax.all_to_all(field, PLANE, 0, 0, tiled=True)

    def by_head(field):
        return field.reshape(-1, HEADS, head_width).transpose(1, 0, 2)

    def merge_heads(field):
        return field.transpose(1, 0, 2).reshape(-1, channels)

    kv_own = to_rows(jnp.concatenate([attn_keys, attn_values], axis=1))
    kv_far = lax.ppermute(kv_own, "zh", SWAP)
    qc_own = to_rows(jnp.concatenate([queries, cotangent], axis=1))

    low, high = exchange_lon(features, 10)
    cot_low, cot_high = exchange_lon(cotangent, 5)
    feat_x = jnp.concatenate([low, features, high], axis=1)
    cot_x = jnp.concatenate([cot_low, cotangent, cot_high], axis=1)
    low, high = exchange_lat(
        jnp.concatenate([feat_x[-5:], jnp.pad(cot_x[-1:], ((0, 0), (0, 10), (0, 0)))], axis=0),
        jnp.concatenate([feat_x[:5], jnp.pad(cot_x[:1], ((0, 0), (0, 10), (0, 0)))], axis=0),
    )
    feat_x = jnp.concatenate([low[:5], feat_x, high[:5]], axis=0)
    cot_near = jnp.concatenate([low[5:, 4:96], cot_x[:, 4:96], high[5:, 4:96]], axis=0)

    pre_near = conv_taps(feat_x, conv_near, 1, rows + 8, cols + 18)
    hidden_one = (feat_x[1:-1, 1:-1].astype(jnp.float32) + gelu_value(pre_near)).astype(
        jnp.bfloat16
    )
    hidden_one = jnp.where(inside_rows(lat_at, rows, 4), hidden_one, jnp.zeros_like(hidden_one))
    pre_wide = conv_taps(hidden_one, conv_wide, 4, rows, cols + 10)
    hidden_two = (
        hidden_one[4:-4, 9:-9].astype(jnp.float32) + gelu_value(pre_wide[:, 5:-5])
    ).astype(jnp.bfloat16)
    hid_own = to_rows(hidden_two)
    hid_far = lax.ppermute(hid_own, "zh", SWAP)

    row_q = qc_own[:, :cols].reshape(-1, channels)
    row_c = qc_own[:, cols:].reshape(-1, channels)
    row_k = jnp.concatenate([kv_own[:, :cols], kv_far[:, :cols]], axis=0).reshape(-1, channels)
    row_v = jnp.concatenate([kv_own[:, cols:], kv_far[:, cols:]], axis=0).reshape(-1, channels)
    out_grad = jnp.dot(row_c, proj_out.T, preferred_element_type=jnp.float32).astype(jnp.bfloat16)
    mixed, query_grad, key_grad, value_grad = lax.map(
        lambda pieces: attend_head(*pieces),
        (by_head(row_q), by_head(out_grad), by_head(row_k), by_head(row_v)),
    )
    mixed, query_grad = merge_heads(mixed), merge_heads(query_grad)
    key_grad, value_grad = merge_heads(key_grad), merge_heads(value_grad)
    half = rows * cols
    far_kv = jnp.concatenate([key_grad[half:], value_grad[half:]], axis=1)
    far_part = jnp.dot(far_kv, proj_qkv[:, channels:].T, preferred_element_type=jnp.float32)
    from_far = lax.ppermute(far_part.astype(jnp.bfloat16), "zh", SWAP)
    own_qkv = jnp.concatenate([query_grad, key_grad[:half], value_grad[:half]], axis=1)
    own_part = jnp.dot(own_qkv, proj_qkv.T, preferred_element_type=jnp.float32)
    attn_grad = (own_part + from_far.astype(jnp.float32)).astype(jnp.bfloat16)
    attn_grad = lax.all_to_all(
        attn_grad.reshape(rows, cols, channels), PLANE, 0, 0, tiled=True
    )
    out_term = contract_rows(mixed, row_c)
    hid_flat = hid_own.reshape(-1, channels)
    far_flat = hid_far.reshape(-1, channels)
    query_term = contract_rows(hid_flat, query_grad)
    kv_term = contract_rows(hid_flat, own_qkv[:, channels:]) + contract_rows(far_flat, far_kv)

    low, high = exchange_lon(attn_grad, 5)
    attn_x = jnp.concatenate([low, attn_grad, high], axis=1)
    outer_x = cot_x.astype(jnp.float32) + attn_x.astype(jnp.float32)
    wide_x = (outer_x * gelu_slope(pre_wide)).astype(jnp.bfloat16)
    low, high = exchange_lat(
        jnp.concatenate([wide_x[-5:], attn_x[-1:]], axis=0),
        jnp.concatenate([wide_x[:5], attn_x[:1]], axis=0),
    )
    wide_all = jnp.concatenate([low[:5], wide_x, high[:5]], axis=0)
    attn_near = jnp.concatenate([low[5:, 4:96], attn_x[:, 4:96], high[5:, 4:96]], axis=0)
    near_total = (cot_near.astype(jnp.float32) + attn_near.astype(jnp.float32)) + conv_back(
        wide_all, conv_wide, 4, rows + 2, cols + 2
    )
    near_grad = (near_total * gelu_slope(pre_near[3:-3, 8:-8])).astype(jnp.bfloat16)
    near_grad = jnp.where(inside_rows(lat_at, rows, 1), near_grad, jnp.zeros_like(near_grad))
    feature_grad = (
        near_total[1:-1, 1:-1] + conv_back(near_grad, conv_near, 1, rows, cols)
    ).astype(jnp.bfloat16)
    wide_term = weight_terms(hidden_one[:, 5:-5], wide_x[:, 5:-5], 4, rows, cols)
    near_term = weight_terms(feat_x[4:-4, 9:-9], near_grad[1:-1, 1:-1], 1, rows, cols)

    terms = jnp.concatenate(
        [near_term, wide_term, query_term, kv_term[:, :channels], kv_term[:, channels:], out_term]
    )
    sums = reduce_all((terms * factor).astype(jnp.bfloat16)).astype(jnp.float32)
    taps = 9 * channels
    near_sum = sums[:taps].reshape(3, 3, channels, channels)
    wide_sum = sums[taps : 2 * taps].reshape(3, 3, channels, channels)
    qkv_sum = jnp.concatenate(
        [sums[2 * taps + i * channels : 2 * taps + (i + 1) * channels] for i in range(3)], axis=1
    )
    out_sum = sums[2 * taps + 3 * channels :]
    return (feature_grad, near_sum, wide_sum, qkv_sum, out_sum)


def solution(mesh):
    grid = Mesh(mesh.devices.reshape(4, 2, 2, 8, 4), LON_AXES + LAT_AXES)
    field = P(LAT_AXES, LON_AXES, None)
    return jax.shard_map(
        on_device,
        mesh=grid,
        in_specs=(field,) * 5 + (P(),) * 4,
        out_specs=(field, P(), P(), P(), P()),
        check_vma=False,
    )
```

```python
import functools

import jax
import jax.numpy as jnp
from jax import lax
from jax.experimental import pallas as pl
from jax.experimental.pallas import tpu as pltpu
from jax.sharding import Mesh, PartitionSpec as P

HEADS = 8
COLS = 90
GROWN = 96
EDGE = 5
GELU_COEF = 0.7978845608028654
CUBIC_COEF = 0.044715

LON_AXES = ("x", "zh", "core")
LAT_AXES = ("zl", "y")
PLANE = ("x", "core")
SWAP = [(0, 1), (1, 0)]


def gelu_value(pre_act):
    tanh_val = jnp.tanh(GELU_COEF * (pre_act + CUBIC_COEF * pre_act * pre_act * pre_act))
    return 0.5 * pre_act * (1.0 + tanh_val)


def gelu_slope(pre_act):
    tanh_val = jnp.tanh(GELU_COEF * (pre_act + CUBIC_COEF * pre_act * pre_act * pre_act))
    inner_d = GELU_COEF * (1.0 + 3.0 * CUBIC_COEF * pre_act * pre_act)
    return 0.5 * (1.0 + tanh_val) + 0.5 * pre_act * (1.0 - tanh_val * tanh_val) * inner_d


def contract_rows(left, right):
    return lax.dot_general(
        left, right, (((0,), (0,)), ((), ())), preferred_element_type=jnp.float32
    )


def exchange_lon(left, right):
    at_zero = lax.axis_index("core") == 0
    inner = lax.ppermute(jnp.where(at_zero, right, left), "core", SWAP)
    pairs = [(i, (i + 1) % 16 if i % 2 else (i - 1) % 16) for i in range(16)]
    outer = lax.ppermute(jnp.where(at_zero, left, right), LON_AXES, pairs)
    return jnp.where(at_zero, outer, inner), jnp.where(at_zero, inner, outer)


def exchange_lat(bottom, top):
    chain = [(i, i + 1) for i in range(31)]
    low = lax.ppermute(bottom, LAT_AXES, chain)
    high = lax.ppermute(top, LAT_AXES, [(b, a) for a, b in chain])
    return low, high


def attend_rows(qc_ref, kv_ref, far_ref, proj_ref, qkv_ref, part_ref, away_ref, send_ref,
                term_ref, own_ref, farg_ref,
                out_s, keep_s, grad_s, key_s, value_s, query_s, mixed_s):
    blocks = qc_ref.shape[0]
    wide = qc_ref.shape[1] // 2
    rows = blocks * wide
    cols = 2 * rows
    channels = qc_ref.shape[2]
    width = channels // HEADS
    chunk = 256
    low = jnp.bfloat16

    def rows_of(ref, at):
        return ref[:, at : at + wide, :].reshape(rows, channels)

    out_s[...] = lax.dot_general(
        rows_of(qc_ref, wide), proj_ref[...], (((1,), (1,)), ((), ())),
        preferred_element_type=jnp.float32,
    ).astype(low)
    for ref in (key_s, value_s, query_s, mixed_s):
        ref[...] = jnp.zeros_like(ref)
    lane_k = lax.broadcasted_iota(jnp.int32, (cols, channels), 1)
    filler = lax.broadcasted_iota(jnp.int32, (cols, channels), 0) % wide >= COLS
    lane_q = lax.broadcasted_iota(jnp.int32, (chunk, channels), 1)

    def one_head(head, carry):
        first = (head * width + width) % channels
        here_k = lane_k // width == head
        here_q = lane_q // width == head
        keys = jnp.concatenate([rows_of(kv_ref, 0), rows_of(far_ref, 0)], axis=0)
        values = jnp.concatenate([rows_of(kv_ref, wide), rows_of(far_ref, wide)], axis=0)
        spare = jnp.where((lane_k == first) & filler, -1e30, 0.0)
        keys_h = jnp.where(here_k, keys.astype(jnp.float32), spare).astype(low)
        ones = jnp.where((lane_k == first) | (lane_k == first + 1), 1.0, 0.0)
        values_h = jnp.where(here_k, values.astype(jnp.float32), ones).astype(low)
        query_n, dout_n = [], []
        for i in range(rows // chunk):
            at = i * chunk
            query = rows_of(qc_ref, 0)[at : at + chunk].astype(jnp.float32) * 0.25
            query_h = jnp.where(here_q, query, jnp.where(lane_q == first, 1.0, 0.0)).astype(low)
            dout = jnp.where(here_q, out_s[at : at + chunk, :].astype(jnp.float32), 0.0)
            scores = lax.dot_general(
                query_h, keys_h, (((1,), (1,)), ((), ())), preferred_element_type=jnp.float32
            )
            top = jnp.max(scores, axis=1, keepdims=True)
            raised = jnp.exp(scores - top).astype(low)
            keep_s[at : at + chunk, :] = raised
            mixed = jnp.dot(raised, values_h, preferred_element_type=jnp.float32)
            total = jnp.sum(jnp.where(lane_q == first, mixed, 0.0), axis=1, keepdims=True)
            share = 1.0 / total
            mixed = jnp.where(here_q, mixed * share, 0.0)
            mixed_s[at : at + chunk, :] += mixed
            delta = jnp.sum(dout * mixed, axis=1, keepdims=True)
            high = delta.astype(low).astype(jnp.float32)
            dout_x = jnp.where(
                lane_q == first, -high, jnp.where(lane_q == first + 1, high - delta, dout)
            ).astype(low)
            prob_grad = lax.dot_general(
                dout_x, values_h, (((1,), (1,)), ((), ())), preferred_element_type=jnp.float32
            )
            score_grad = raised * prob_grad.astype(low)
            grad_s[at : at + chunk, :] = score_grad
            query_s[at : at + chunk, :] += (
                jnp.dot(score_grad, keys_h, preferred_element_type=jnp.float32) * (0.25 * share)
            )
            query_n.append((jnp.where(here_q, query, 0.0) * share).astype(low))
            dout_n.append((dout * share).astype(low))
        key_s[...] += lax.dot_general(
            grad_s[...], jnp.concatenate(query_n, axis=0), (((0,), (0,)), ((), ())),
            preferred_element_type=jnp.float32,
        )
        value_s[...] += lax.dot_general(
            keep_s[...], jnp.concatenate(dout_n, axis=0), (((0,), (0,)), ((), ())),
            preferred_element_type=jnp.float32,
        )
        return carry

    lax.fori_loop(0, HEADS, one_head, 0)
    own_ref[:, :channels] = query_s[...].astype(low)
    own_ref[:, channels : 2 * channels] = key_s[:rows, :].astype(low)
    own_ref[:, 2 * channels :] = value_s[:rows, :].astype(low)
    farg_ref[:, :channels] = key_s[rows:, :].astype(low)
    farg_ref[:, channels:] = value_s[rows:, :].astype(low)
    own_part = lax.dot_general(
        own_ref[...], qkv_ref[...], (((1,), (1,)), ((), ())), preferred_element_type=jnp.float32
    )
    far_part = lax.dot_general(
        farg_ref[...], qkv_ref[:, channels:], (((1,), (1,)), ((), ())),
        preferred_element_type=jnp.float32,
    )
    part_ref[...] = own_part.reshape(blocks, wide, channels)
    away_ref[...] = far_part.reshape(blocks, wide, channels)
    query_s[...] = far_part
    for block in range(blocks):
        edge = 0 if block % 2 == 0 else COLS - EDGE
        query_s[block * wide + COLS : block * wide + COLS + EDGE, :] = part_ref[
            block, edge : edge + EDGE, :
        ]
    send_ref[...] = query_s[...].astype(low).reshape(blocks, wide, channels)
    term_ref[...] = lax.dot_general(
        mixed_s[...].astype(low), rows_of(qc_ref, wide), (((0,), (0,)), ((), ())),
        preferred_element_type=jnp.float32,
    )


def attention(qc_own, kv_own, kv_far, proj_out, proj_qkv):
    blocks, double, channels = qc_own.shape
    wide = double // 2
    rows = blocks * wide
    low = jnp.bfloat16
    shapes = [
        ((blocks, wide, channels), jnp.float32),
        ((blocks, wide, channels), jnp.float32),
        ((blocks, wide, channels), low),
        ((channels, channels), jnp.float32),
        ((rows, 3 * channels), low),
        ((rows, 2 * channels), low),
    ]
    return pl.pallas_call(
        attend_rows,
        out_shape=[jax.ShapeDtypeStruct(s, t) for s, t in shapes],
        in_specs=[pl.BlockSpec(memory_space=pltpu.VMEM)] * 5,
        out_specs=[pl.BlockSpec(memory_space=pltpu.VMEM)] * 6,
        scratch_shapes=[
            pltpu.VMEM((rows, channels), low),
            pltpu.VMEM((rows, 2 * rows), low),
            pltpu.VMEM((rows, 2 * rows), low),
            pltpu.VMEM((2 * rows, channels), jnp.float32),
            pltpu.VMEM((2 * rows, channels), jnp.float32),
            pltpu.VMEM((rows, channels), jnp.float32),
            pltpu.VMEM((rows, channels), jnp.float32),
        ],
        compiler_params=pltpu.CompilerParams(vmem_limit_bytes=48 * 1024 * 1024),
        cost_estimate=pl.CostEstimate(
            flops=12 * rows * 2 * rows * channels * HEADS,
            bytes_accessed=16 * rows * channels,
            transcendentals=HEADS * rows * 2 * rows,
        ),
        name="attend_rows",
    )(qc_own, kv_own, kv_far, proj_out, proj_qkv)


def row_inside(lat_ref, shape, width):
    at = lat_ref[0] * 8 + lax.broadcasted_iota(jnp.int32, shape, 0) - width
    return (at >= 0) & (at < 256)


def three(ref, starts, count):
    return jnp.concatenate(
        [ref[:, at : at + count, :].astype(jnp.bfloat16) for at in starts], axis=2
    )


def forward_block(lat_ref, feat_ref, near_ref, wide_ref, two_ref, one_ref, nslope_ref, wslope_ref,
                  feat_s, one_s, wide_s):
    channels = feat_ref.shape[2]
    low = jnp.bfloat16
    cols = 112
    feat_s[...] = feat_ref[...].astype(jnp.float32)
    feat_3 = three(feat_s, (0, 1, 2), cols)
    total = jnp.zeros((16 * cols, channels), jnp.float32)
    for tap in range(3):
        weight = near_ref[tap].reshape(3 * channels, channels)
        total += jnp.dot(
            feat_3[tap : tap + 16].reshape(16 * cols, 3 * channels), weight,
            preferred_element_type=jnp.float32,
        )
    pre_near = total.reshape(16, cols, channels)
    nslope_ref[...] = gelu_slope(pre_near[3:13])
    one = (feat_s[1:17, 1 : 1 + cols, :] + gelu_value(pre_near)).astype(low)
    one = jnp.where(row_inside(lat_ref, one.shape, 4), one.astype(jnp.float32), 0.0)
    one_ref[...] = one.astype(low)
    one_s[...] = jnp.zeros_like(one_s)
    one_s[:, :cols, :] = one
    one_3 = three(one_s, (0, 4, 8), cols)
    total = jnp.zeros((8 * cols, channels), jnp.float32)
    for tap in range(3):
        weight = wide_ref[tap].reshape(3 * channels, channels)
        total += jnp.dot(
            one_3[4 * tap : 4 * tap + 8].reshape(8 * cols, 3 * channels), weight,
            preferred_element_type=jnp.float32,
        )
    pre_wide = total.reshape(8, cols, channels)
    wslope_ref[...] = gelu_slope(pre_wide)
    wide_s[...] = gelu_value(pre_wide)
    two = one_s[4:12, 9 : 9 + GROWN, :] + wide_s[:, EDGE : EDGE + GROWN, :]
    valid = lax.broadcasted_iota(jnp.int32, two.shape, 1) < COLS
    two_ref[...] = jnp.where(valid, two, 0.0).astype(low)


def forward(lat_at, feat_x, conv_near, conv_wide):
    channels = feat_x.shape[2]
    shapes = [
        ((8, GROWN, channels), jnp.bfloat16),
        ((16, 112, channels), jnp.bfloat16),
        ((10, 112, channels), jnp.float32),
        ((8, 112, channels), jnp.float32),
    ]
    return pl.pallas_call(
        forward_block,
        out_shape=[jax.ShapeDtypeStruct(s, t) for s, t in shapes],
        in_specs=[pl.BlockSpec(memory_space=pltpu.SMEM)]
        + [pl.BlockSpec(memory_space=pltpu.VMEM)] * 3,
        out_specs=[pl.BlockSpec(memory_space=pltpu.VMEM)] * 4,
        scratch_shapes=[
            pltpu.VMEM((18, 128, channels), jnp.float32),
            pltpu.VMEM((16, 128, channels), jnp.float32),
            pltpu.VMEM((8, 112, channels), jnp.float32),
        ],
        compiler_params=pltpu.CompilerParams(vmem_limit_bytes=40 * 1024 * 1024),
        cost_estimate=pl.CostEstimate(
            flops=6 * 10**9, bytes_accessed=4 * 10**6, transcendentals=2 * 10**5
        ),
        name="forward_block",
    )(lat_at, feat_x, conv_near, conv_wide)


def backward_block(lat_ref, wide_ref, attn_ref, cot_ref, nslope_ref, one_ref, feat_ref, near_ref,
                   dil_ref, out_ref, term_ref, wide_s, outer_s, slope_s, one_s, feat_s, total_s,
                   near_s, *, factor):
    channels = wide_ref.shape[2]
    low = jnp.bfloat16
    cols = GROWN

    def transposed(ref, tap):
        return jnp.concatenate([ref[tap, i] for i in range(3)], axis=1)

    wide_s[...] = wide_ref[...].astype(jnp.float32)
    outer_s[...] = cot_ref[...].astype(jnp.float32) + attn_ref[...].astype(jnp.float32)
    slope_s[...] = nslope_ref[...]
    one_s[...] = one_ref[...].astype(jnp.float32)
    feat_s[...] = feat_ref[...].astype(jnp.float32)
    wide_3 = three(wide_s, (8, 4, 0), cols)
    total = jnp.zeros((10 * cols, channels), jnp.float32)
    for tap in range(3):
        at = 8 - 4 * tap
        total += lax.dot_general(
            wide_3[at : at + 10].reshape(10 * cols, 3 * channels), transposed(dil_ref, tap),
            (((1,), (1,)), ((), ())), preferred_element_type=jnp.float32,
        )
    near_total = total.reshape(10, cols, channels) + outer_s[:, 4 : 4 + cols, :]
    near_grad = (near_total * slope_s[:, 8 : 8 + cols, :]).astype(low).astype(jnp.float32)
    near_grad = jnp.where(row_inside(lat_ref, near_grad.shape, 1), near_grad, 0.0)
    for ref, value in ((total_s, near_total), (near_s, near_grad)):
        ref[...] = jnp.zeros_like(ref)
        ref[:, :cols, :] = value
    near_3 = three(near_s, (2, 1, 0), cols)
    total = jnp.zeros((8 * cols, channels), jnp.float32)
    for tap in range(3):
        at = 2 - tap
        total += lax.dot_general(
            near_3[at : at + 8].reshape(8 * cols, 3 * channels), transposed(near_ref, tap),
            (((1,), (1,)), ((), ())), preferred_element_type=jnp.float32,
        )
    feature = (total.reshape(8, cols, channels) + total_s[1:9, 1 : 1 + cols, :]).astype(low)
    out_ref[...] = feature[:, :COLS, :]

    valid = lax.broadcasted_iota(jnp.int32, (8, cols, channels), 1) < COLS
    own_near = jnp.where(valid, near_s[1:9, 1 : 1 + cols, :], 0.0)
    own_near = own_near.astype(low).reshape(8 * cols, channels)
    own_wide = jnp.where(valid, wide_s[5:13, EDGE : EDGE + cols, :], 0.0)
    own_wide = own_wide.astype(low).reshape(8 * cols, channels)
    feat_3 = three(feat_s, (9, 10, 11), cols)
    one_3 = three(one_s, (5, 9, 13), cols)
    long = 3 * channels
    for tap in range(3):
        for left, right, at in (
            (feat_3[4 + tap : 12 + tap], own_near, tap * long),
            (one_3[4 * tap : 4 * tap + 8], own_wide, (3 + tap) * long),
        ):
            term = contract_rows(left.reshape(8 * cols, long), right)
            term_ref[at : at + long, :] = (term * factor).astype(low)


def backward(lat_at, wide_all, attn_near, cot_near, near_slope, hidden_one, feat_x, conv_near,
             conv_wide, factor):
    channels = feat_x.shape[2]
    low = jnp.bfloat16
    shapes = [((8, COLS, channels), low), ((18 * channels, channels), low)]
    grown = [(18, 112), (10, 112), (10, 112), (16, 112), (18, 128), (10, 112), (10, 112)]
    return pl.pallas_call(
        functools.partial(backward_block, factor=factor),
        out_shape=[jax.ShapeDtypeStruct(s, t) for s, t in shapes],
        in_specs=[pl.BlockSpec(memory_space=pltpu.SMEM)]
        + [pl.BlockSpec(memory_space=pltpu.VMEM)] * 8,
        out_specs=[pl.BlockSpec(memory_space=pltpu.VMEM)] * 2,
        scratch_shapes=[pltpu.VMEM(g + (channels,), jnp.float32) for g in grown],
        compiler_params=pltpu.CompilerParams(vmem_limit_bytes=44 * 1024 * 1024),
        cost_estimate=pl.CostEstimate(
            flops=6 * 10**9, bytes_accessed=4 * 10**6, transcendentals=0
        ),
        name="backward_block",
    )(lat_at, wide_all, attn_near, cot_near, near_slope, hidden_one, feat_x, conv_near, conv_wide)


def reduce_all(terms):
    rows, channels = terms.shape
    part = rows // 32
    piece = part * channels // 16
    band = lax.all_to_all(
        terms.reshape(32, part, channels), ("x", "y", "core"), 0, 0, tiled=True
    )
    band = band.astype(jnp.float32).sum(0).astype(jnp.bfloat16).reshape(16, piece)
    band = lax.all_to_all(band, ("zh", "zl"), 0, 0, tiled=True)
    band = band.astype(jnp.float32).sum(0).astype(jnp.bfloat16)
    band = lax.all_to_all(
        jnp.broadcast_to(band[None], (16, piece)), ("zh", "zl"), 0, 0, tiled=True
    ).reshape(part, channels)
    return lax.all_to_all(
        jnp.broadcast_to(band[None], (32, part, channels)), ("x", "y", "core"), 0, 0, tiled=True
    ).reshape(rows, channels)


def on_device(
    features, queries, attn_keys, attn_values, cotangent, conv_near, conv_wide, proj_qkv, proj_out
):
    rows, cols, channels = features.shape
    factor = float(rows * cols * 512) ** (-0.5)
    lat_at = lax.axis_index(LAT_AXES).astype(jnp.int32).reshape(1)
    half_at = lax.axis_index("zh")

    def to_rows(*fields):
        grown = [jnp.pad(f, ((0, 0), (0, GROWN - f.shape[1]), (0, 0))) for f in fields]
        return lax.all_to_all(jnp.concatenate(grown, axis=1), PLANE, 0, 0, tiled=True)

    kv_own = to_rows(attn_keys, attn_values)
    kv_far = lax.ppermute(kv_own, "zh", SWAP)

    features, cotangent, kv_own = lax.optimization_barrier((features, cotangent, kv_own))
    blank = jnp.zeros((rows, 1, channels), features.dtype)
    low, high = exchange_lon(
        jnp.concatenate([features[:, :10], cotangent[:, :EDGE], blank], axis=1),
        jnp.concatenate([features[:, -10:], cotangent[:, -EDGE:], blank], axis=1),
    )
    qc_own = to_rows(queries, cotangent)
    feat_x = jnp.concatenate(
        [low[:, :10], features, high[:, :10], jnp.zeros((rows, 18, channels), features.dtype)],
        axis=1,
    )
    cot_x = jnp.concatenate(
        [low[:, 10:15], cotangent, high[:, 10:15], jnp.zeros((rows, 28, channels), features.dtype)],
        axis=1,
    )
    low, high = exchange_lat(
        jnp.concatenate([feat_x[-5:], cot_x[-1:]], axis=0),
        jnp.concatenate([feat_x[:5], cot_x[:1]], axis=0),
    )
    feat_x = jnp.concatenate([low[:5], feat_x, high[:5]], axis=0)
    cot_near = jnp.concatenate([low[5:], cot_x, high[5:]], axis=0)[:, :112]

    feat_x, kv_far = lax.optimization_barrier((feat_x, kv_far))
    hidden_two, hidden_one, near_slope, wide_slope = forward(lat_at, feat_x, conv_near, conv_wide)
    hid_own = to_rows(hidden_two)
    hid_far = lax.ppermute(hid_own, "zh", SWAP)

    own_part, far_part, sent, out_term, own_qkv, far_kv = attention(
        qc_own, kv_own, kv_far, proj_out, proj_qkv
    )
    from_far = lax.ppermute(sent, "zh", SWAP)
    whole = (own_part + from_far.astype(jnp.float32)).astype(jnp.bfloat16)
    whole = whole.reshape(4, 2, GROWN, channels)
    away = far_part.reshape(4, 2, GROWN, channels)
    edge = from_far.reshape(4, 2, GROWN, channels)[:, :, COLS : COLS + EDGE].astype(jnp.float32)
    edge_low = (edge[:, 0] + away[:, 0, :EDGE]).astype(jnp.bfloat16)
    edge_high = (edge[:, 1] + away[:, 1, COLS - EDGE : COLS]).astype(jnp.bfloat16)
    left = jnp.where(half_at == 1, edge_high, jnp.roll(edge_high, 1, axis=0))
    right = jnp.where(half_at == 0, edge_low, jnp.roll(edge_low, -1, axis=0))
    left = jnp.stack([left, whole[:, 0, COLS - EDGE : COLS]], axis=1)
    right = jnp.stack([whole[:, 1, :EDGE], right], axis=1)
    blank = jnp.zeros((4, 2, 12, channels), jnp.bfloat16)
    attn_x = jnp.concatenate([left, whole[:, :, :COLS], right, blank], axis=2)
    attn_x = lax.all_to_all(attn_x.reshape(8, 112, channels), PLANE, 0, 0, tiled=True)
    hid_flat = hid_own.reshape(-1, channels)
    far_flat = hid_far.reshape(-1, channels)
    query_term = contract_rows(hid_flat, own_qkv[:, :channels])
    kv_term = contract_rows(hid_flat, own_qkv[:, channels:]) + contract_rows(far_flat, far_kv)

    outer_x = cot_x[:, :112].astype(jnp.float32) + attn_x.astype(jnp.float32)
    wide_x = (outer_x * wide_slope).astype(jnp.bfloat16)
    low, high = exchange_lat(
        jnp.concatenate([wide_x[-5:], attn_x[-1:]], axis=0),
        jnp.concatenate([wide_x[:5], attn_x[:1]], axis=0),
    )
    wide_all = jnp.concatenate([low[:5], wide_x, high[:5]], axis=0)
    attn_near = jnp.concatenate([low[5:], attn_x, high[5:]], axis=0)
    feature_grad, conv_terms = backward(
        lat_at, wide_all, attn_near, cot_near, near_slope, hidden_one, feat_x, conv_near,
        conv_wide, factor,
    )

    others = jnp.concatenate([query_term, kv_term[:, :channels], kv_term[:, channels:], out_term])
    terms = jnp.concatenate([conv_terms, (others * factor).astype(jnp.bfloat16)])
    sums = reduce_all(terms).astype(jnp.float32)
    taps = 9 * channels
    near_sum = sums[:taps].reshape(3, 3, channels, channels)
    wide_sum = sums[taps : 2 * taps].reshape(3, 3, channels, channels)
    qkv_sum = jnp.concatenate(
        [sums[2 * taps + i * channels : 2 * taps + (i + 1) * channels] for i in range(3)], axis=1
    )
    out_sum = sums[2 * taps + 3 * channels :]
    return (feature_grad, near_sum, wide_sum, qkv_sum, out_sum)


def solution(mesh):
    grid = Mesh(mesh.devices.reshape(4, 2, 2, 8, 4), LON_AXES + LAT_AXES)
    field = P(LAT_AXES, LON_AXES, None)
    return jax.shard_map(
        on_device,
        mesh=grid,
        in_specs=(field,) * 5 + (P(),) * 4,
        out_specs=(field, P(), P(), P(), P()),
        check_vma=False,
    )
```

```python
import functools

import jax
import jax.numpy as jnp
from jax import lax
from jax.experimental import pallas as pl
from jax.experimental.pallas import tpu as pltpu
from jax.sharding import Mesh, PartitionSpec as P

HEADS = 8
COLS = 90
GROWN = 96
EDGE = 5
CHUNK = 256
GELU_COEF = 0.7978845608028654
CUBIC_COEF = 0.044715

LON_AXES = ("x", "zh", "core")
LAT_AXES = ("zl", "y")
PLANE = ("x", "core")
SWAP = [(0, 1), (1, 0)]


def gelu_value(pre_act):
    tanh_val = jnp.tanh(GELU_COEF * (pre_act + CUBIC_COEF * pre_act * pre_act * pre_act))
    return 0.5 * pre_act * (1.0 + tanh_val)


def gelu_slope(pre_act):
    tanh_val = jnp.tanh(GELU_COEF * (pre_act + CUBIC_COEF * pre_act * pre_act * pre_act))
    inner_d = GELU_COEF * (1.0 + 3.0 * CUBIC_COEF * pre_act * pre_act)
    return 0.5 * (1.0 + tanh_val) + 0.5 * pre_act * (1.0 - tanh_val * tanh_val) * inner_d


def contract_rows(left, right):
    return lax.dot_general(
        left, right, (((0,), (0,)), ((), ())), preferred_element_type=jnp.float32
    )


def exchange_lon(left, right):
    at_zero = lax.axis_index("core") == 0
    inner = lax.ppermute(jnp.where(at_zero, right, left), "core", SWAP)
    pairs = [(i, (i + 1) % 16 if i % 2 else (i - 1) % 16) for i in range(16)]
    outer = lax.ppermute(jnp.where(at_zero, left, right), LON_AXES, pairs)
    return jnp.where(at_zero, outer, inner), jnp.where(at_zero, inner, outer)


def exchange_lat(bottom, top):
    chain = [(i, i + 1) for i in range(31)]
    low = lax.ppermute(bottom, LAT_AXES, chain)
    high = lax.ppermute(top, LAT_AXES, [(b, a) for a, b in chain])
    return low, high


def attend_rows(qc_ref, own_ref, far_ref, proj_ref, mixed_ref, grad_ref, away_ref,
                out_s, keep_s, grad_s, pair_s, value_s, key_g, value_g, query_g, mixed_g, *, heads):
    blocks, wide, channels = own_ref.shape
    rows = blocks * wide
    cols = 2 * rows
    width = channels // HEADS
    chunk = CHUNK
    low = jnp.bfloat16

    def rows_of(ref, at):
        return ref[:, at : at + wide, :].reshape(rows, channels)

    out_s[...] = lax.dot_general(
        rows_of(qc_ref, wide), proj_ref[...], (((1,), (1,)), ((), ())),
        preferred_element_type=jnp.float32,
    )
    pair = jnp.concatenate([rows_of(own_ref, 0), rows_of(far_ref, 0)], axis=0).astype(jnp.float32)
    pair_s[...] = pair
    value_s[...] = pltpu.roll(pair, channels // 2, 1)
    for ref in (key_g, value_g, query_g, mixed_g):
        ref[...] = jnp.zeros_like(ref)
    lane_k = lax.broadcasted_iota(jnp.int32, (cols, channels), 1)
    filler = lax.broadcasted_iota(jnp.int32, (cols, channels), 0) % wide >= COLS
    lane_q = lax.broadcasted_iota(jnp.int32, (chunk, channels), 1)

    def one_head(head, carry):
        first = (head * width + width) % channels
        here_k = lane_k // width == head
        here_q = lane_q // width == head
        spare = jnp.where((lane_k == first) & filler, -1e30, 0.0)
        keys_h = jnp.where(here_k, pair_s[...], spare).astype(low)
        ones = jnp.where((lane_k == first) | (lane_k == first + 1), 1.0, 0.0)
        values_h = jnp.where(here_k, value_s[...], ones).astype(low)
        query_n, dout_n = [], []
        for i in range(rows // chunk):
            at = i * chunk
            query = rows_of(qc_ref, 0)[at : at + chunk].astype(jnp.float32) * 0.25
            query_h = jnp.where(here_q, query, jnp.where(lane_q == first, 1.0, 0.0)).astype(low)
            dout = out_s[at : at + chunk, :].astype(low).astype(jnp.float32)
            dout = jnp.where(here_q, dout, 0.0)
            scores = lax.dot_general(
                query_h, keys_h, (((1,), (1,)), ((), ())), preferred_element_type=jnp.float32
            )
            top = jnp.max(scores, axis=1, keepdims=True)
            raised = jnp.exp(scores - top).astype(low)
            keep_s[at : at + chunk, :] = raised
            mixed = jnp.dot(raised, values_h, preferred_element_type=jnp.float32)
            total = jnp.sum(jnp.where(lane_q == first, mixed, 0.0), axis=1, keepdims=True)
            share = 1.0 / total
            mixed = jnp.where(here_q, mixed * share, 0.0)
            mixed_g[at : at + chunk, :] += mixed
            delta = jnp.sum(dout * mixed, axis=1, keepdims=True)
            high = delta.astype(low).astype(jnp.float32)
            dout_x = jnp.where(
                lane_q == first, -high, jnp.where(lane_q == first + 1, high - delta, dout)
            ).astype(low)
            prob_grad = lax.dot_general(
                dout_x, values_h, (((1,), (1,)), ((), ())), preferred_element_type=jnp.float32
            )
            score_grad = raised * prob_grad.astype(low)
            grad_s[at : at + chunk, :] = score_grad
            query_g[at : at + chunk, :] += (
                jnp.dot(score_grad, keys_h, preferred_element_type=jnp.float32) * (0.25 * share)
            )
            query_n.append((jnp.where(here_q, query, 0.0) * share).astype(low))
            dout_n.append((dout * share).astype(low))
        key_g[...] += lax.dot_general(
            grad_s[...], jnp.concatenate(query_n, axis=0), (((0,), (0,)), ((), ())),
            preferred_element_type=jnp.float32,
        )
        value_g[...] += lax.dot_general(
            keep_s[...], jnp.concatenate(dout_n, axis=0), (((0,), (0,)), ((), ())),
            preferred_element_type=jnp.float32,
        )
        return carry

    lax.fori_loop(heads[0], heads[1], one_head, 0)
    mixed_ref[...] = mixed_g[...].astype(low)
    grad_ref[:, :channels] = query_g[...].astype(low)
    grad_ref[:, channels : 2 * channels] = key_g[:rows, :].astype(low)
    grad_ref[:, 2 * channels :] = value_g[:rows, :].astype(low)
    away_ref[:, :channels] = key_g[rows:, :].astype(low)
    away_ref[:, channels:] = value_g[rows:, :].astype(low)


def attention(qc_own, kv_own, kv_far, proj_out, heads):
    blocks, wide, channels = kv_own.shape
    rows = blocks * wide
    low = jnp.bfloat16
    shapes = [(rows, channels), (rows, 3 * channels), (rows, 2 * channels)]
    return pl.pallas_call(
        functools.partial(attend_rows, heads=heads),
        out_shape=[jax.ShapeDtypeStruct(s, low) for s in shapes],
        in_specs=[pl.BlockSpec(memory_space=pltpu.VMEM)] * 4,
        out_specs=[pl.BlockSpec(memory_space=pltpu.VMEM)] * 3,
        scratch_shapes=[
            pltpu.VMEM((rows, channels), jnp.float32),
            pltpu.VMEM((rows, 2 * rows), low),
            pltpu.VMEM((rows, 2 * rows), low),
            pltpu.VMEM((2 * rows, channels), jnp.float32),
            pltpu.VMEM((2 * rows, channels), jnp.float32),
            pltpu.VMEM((2 * rows, channels), jnp.float32),
            pltpu.VMEM((2 * rows, channels), jnp.float32),
            pltpu.VMEM((rows, channels), jnp.float32),
            pltpu.VMEM((rows, channels), jnp.float32),
        ],
        compiler_params=pltpu.CompilerParams(vmem_limit_bytes=48 * 1024 * 1024),
        cost_estimate=pl.CostEstimate(
            flops=12 * rows * 2 * rows * channels * (heads[1] - heads[0]),
            bytes_accessed=16 * rows * channels,
            transcendentals=(heads[1] - heads[0]) * rows * 2 * rows,
        ),
        name="attend_rows",
    )(qc_own, kv_own, kv_far, proj_out)


def gather_parts(first_refs, second_refs, cot_ref, qkv_ref, part_ref, away_ref, send_ref, term_ref,
                 all_ref, far_ref, send_s):
    channels = cot_ref.shape[2]
    blocks, wide = cot_ref.shape[0], cot_ref.shape[1] // 2
    rows = blocks * wide
    low = jnp.bfloat16
    mixed, own, far = (a[...] + b[...] for a, b in zip(first_refs, second_refs))
    all_ref[...] = own
    far_ref[...] = far
    own_part = lax.dot_general(
        own, qkv_ref[...], (((1,), (1,)), ((), ())), preferred_element_type=jnp.float32
    )
    far_part = lax.dot_general(
        far, qkv_ref[:, channels:], (((1,), (1,)), ((), ())), preferred_element_type=jnp.float32
    )
    part_ref[...] = own_part.reshape(blocks, wide, channels)
    away_ref[...] = far_part.reshape(blocks, wide, channels)
    send_s[...] = far_part.reshape(blocks, wide, channels)
    for block in range(blocks):
        edge = 0 if block % 2 == 0 else COLS - EDGE
        send_s[block, COLS : COLS + EDGE, :] = part_ref[block, edge : edge + EDGE, :]
    send_ref[...] = send_s[...].astype(low)
    cot = cot_ref[:, wide:, :].reshape(rows, channels)
    term_ref[...] = contract_rows(mixed, cot)


def combine(first, second, qc_own, proj_qkv):
    blocks, double, channels = qc_own.shape
    wide = double // 2
    rows = blocks * wide
    low = jnp.bfloat16
    shapes = [
        ((blocks, wide, channels), jnp.float32),
        ((blocks, wide, channels), jnp.float32),
        ((blocks, wide, channels), low),
        ((channels, channels), jnp.float32),
        ((rows, 3 * channels), low),
        ((rows, 2 * channels), low),
    ]

    def body(*refs):
        gather_parts(refs[:3], refs[3:6], *refs[6:])

    return pl.pallas_call(
        body,
        out_shape=[jax.ShapeDtypeStruct(s, t) for s, t in shapes],
        in_specs=[pl.BlockSpec(memory_space=pltpu.VMEM)] * 8,
        out_specs=[pl.BlockSpec(memory_space=pltpu.VMEM)] * 6,
        scratch_shapes=[pltpu.VMEM((blocks, wide, channels), jnp.float32)],
        compiler_params=pltpu.CompilerParams(vmem_limit_bytes=24 * 1024 * 1024),
        cost_estimate=pl.CostEstimate(
            flops=12 * rows * channels * channels, bytes_accessed=5 * 10**6, transcendentals=0
        ),
        name="combine",
    )(*first, *second, qc_own, proj_qkv)


def row_inside(lat_ref, shape, width):
    at = lat_ref[0] * 8 + lax.broadcasted_iota(jnp.int32, shape, 0) - width
    return (at >= 0) & (at < 256)


def three(ref, starts, count):
    return jnp.concatenate(
        [ref[:, at : at + count, :].astype(jnp.bfloat16) for at in starts], axis=2
    )


def forward_block(lat_ref, feat_ref, near_ref, wide_ref, two_ref, one_ref, nslope_ref, wslope_ref,
                  feat_s, one_s, wide_s):
    channels = feat_ref.shape[2]
    low = jnp.bfloat16
    cols = 112
    feat_s[...] = feat_ref[...].astype(jnp.float32)
    feat_3 = three(feat_s, (0, 1, 2), cols)
    total = jnp.zeros((16 * cols, channels), jnp.float32)
    for tap in range(3):
        weight = near_ref[tap].reshape(3 * channels, channels)
        total += jnp.dot(
            feat_3[tap : tap + 16].reshape(16 * cols, 3 * channels), weight,
            preferred_element_type=jnp.float32,
        )
    pre_near = total.reshape(16, cols, channels)
    nslope_ref[...] = gelu_slope(pre_near[3:13])
    one = (feat_s[1:17, 1 : 1 + cols, :] + gelu_value(pre_near)).astype(low)
    one = jnp.where(row_inside(lat_ref, one.shape, 4), one.astype(jnp.float32), 0.0)
    one_ref[...] = one.astype(low)
    one_s[...] = jnp.zeros_like(one_s)
    one_s[:, :cols, :] = one
    one_3 = three(one_s, (0, 4, 8), cols)
    total = jnp.zeros((8 * cols, channels), jnp.float32)
    for tap in range(3):
        weight = wide_ref[tap].reshape(3 * channels, channels)
        total += jnp.dot(
            one_3[4 * tap : 4 * tap + 8].reshape(8 * cols, 3 * channels), weight,
            preferred_element_type=jnp.float32,
        )
    pre_wide = total.reshape(8, cols, channels)
    wslope_ref[...] = gelu_slope(pre_wide)
    wide_s[...] = gelu_value(pre_wide)
    two = one_s[4:12, 9 : 9 + GROWN, :] + wide_s[:, EDGE : EDGE + GROWN, :]
    valid = lax.broadcasted_iota(jnp.int32, two.shape, 1) < COLS
    two_ref[...] = jnp.where(valid, two, 0.0).astype(low)


def forward(lat_at, feat_x, conv_near, conv_wide):
    channels = feat_x.shape[2]
    shapes = [
        ((8, GROWN, channels), jnp.bfloat16),
        ((16, 112, channels), jnp.bfloat16),
        ((10, 112, channels), jnp.float32),
        ((8, 112, channels), jnp.float32),
    ]
    return pl.pallas_call(
        forward_block,
        out_shape=[jax.ShapeDtypeStruct(s, t) for s, t in shapes],
        in_specs=[pl.BlockSpec(memory_space=pltpu.SMEM)]
        + [pl.BlockSpec(memory_space=pltpu.VMEM)] * 3,
        out_specs=[pl.BlockSpec(memory_space=pltpu.VMEM)] * 4,
        scratch_shapes=[
            pltpu.VMEM((18, 128, channels), jnp.float32),
            pltpu.VMEM((16, 128, channels), jnp.float32),
            pltpu.VMEM((8, 112, channels), jnp.float32),
        ],
        compiler_params=pltpu.CompilerParams(vmem_limit_bytes=40 * 1024 * 1024),
        cost_estimate=pl.CostEstimate(
            flops=6 * 10**9, bytes_accessed=4 * 10**6, transcendentals=2 * 10**5
        ),
        name="forward_block",
    )(lat_at, feat_x, conv_near, conv_wide)


def backward_block(lat_ref, wide_ref, attn_ref, cot_ref, nslope_ref, one_ref, feat_ref, near_ref,
                   dil_ref, out_ref, term_ref, wide_s, outer_s, slope_s, one_s, feat_s, total_s,
                   near_s, *, factor):
    channels = wide_ref.shape[2]
    low = jnp.bfloat16
    cols = GROWN

    def transposed(ref, tap):
        return jnp.concatenate([ref[tap, i] for i in range(3)], axis=1)

    wide_s[...] = wide_ref[...].astype(jnp.float32)
    outer_s[...] = cot_ref[...].astype(jnp.float32) + attn_ref[...].astype(jnp.float32)
    slope_s[...] = nslope_ref[...]
    one_s[...] = one_ref[...].astype(jnp.float32)
    feat_s[...] = feat_ref[...].astype(jnp.float32)
    wide_3 = three(wide_s, (8, 4, 0), cols)
    total = jnp.zeros((10 * cols, channels), jnp.float32)
    for tap in range(3):
        at = 8 - 4 * tap
        total += lax.dot_general(
            wide_3[at : at + 10].reshape(10 * cols, 3 * channels), transposed(dil_ref, tap),
            (((1,), (1,)), ((), ())), preferred_element_type=jnp.float32,
        )
    near_total = total.reshape(10, cols, channels) + outer_s[:, 4 : 4 + cols, :]
    near_grad = (near_total * slope_s[:, 8 : 8 + cols, :]).astype(low).astype(jnp.float32)
    near_grad = jnp.where(row_inside(lat_ref, near_grad.shape, 1), near_grad, 0.0)
    for ref, value in ((total_s, near_total), (near_s, near_grad)):
        ref[...] = jnp.zeros_like(ref)
        ref[:, :cols, :] = value
    near_3 = three(near_s, (2, 1, 0), cols)
    total = jnp.zeros((8 * cols, channels), jnp.float32)
    for tap in range(3):
        at = 2 - tap
        total += lax.dot_general(
            near_3[at : at + 8].reshape(8 * cols, 3 * channels), transposed(near_ref, tap),
            (((1,), (1,)), ((), ())), preferred_element_type=jnp.float32,
        )
    feature = (total.reshape(8, cols, channels) + total_s[1:9, 1 : 1 + cols, :]).astype(low)
    out_ref[...] = feature[:, :COLS, :]

    valid = lax.broadcasted_iota(jnp.int32, (8, cols, channels), 1) < COLS
    own_near = jnp.where(valid, near_s[1:9, 1 : 1 + cols, :], 0.0)
    own_near = own_near.astype(low).reshape(8 * cols, channels)
    own_wide = jnp.where(valid, wide_s[5:13, EDGE : EDGE + cols, :], 0.0)
    own_wide = own_wide.astype(low).reshape(8 * cols, channels)
    feat_3 = three(feat_s, (9, 10, 11), cols)
    one_3 = three(one_s, (5, 9, 13), cols)
    long = 3 * channels
    for tap in range(3):
        for left, right, at in (
            (feat_3[4 + tap : 12 + tap], own_near, tap * long),
            (one_3[4 * tap : 4 * tap + 8], own_wide, (3 + tap) * long),
        ):
            term = contract_rows(left.reshape(8 * cols, long), right)
            term_ref[at : at + long, :] = (term * factor).astype(low)


def backward(lat_at, wide_all, attn_near, cot_near, near_slope, hidden_one, feat_x, conv_near,
             conv_wide, factor):
    channels = feat_x.shape[2]
    low = jnp.bfloat16
    shapes = [((8, COLS, channels), low), ((18 * channels, channels), low)]
    grown = [(18, 112), (10, 112), (10, 112), (16, 112), (18, 128), (10, 112), (10, 112)]
    return pl.pallas_call(
        functools.partial(backward_block, factor=factor),
        out_shape=[jax.ShapeDtypeStruct(s, t) for s, t in shapes],
        in_specs=[pl.BlockSpec(memory_space=pltpu.SMEM)]
        + [pl.BlockSpec(memory_space=pltpu.VMEM)] * 8,
        out_specs=[pl.BlockSpec(memory_space=pltpu.VMEM)] * 2,
        scratch_shapes=[pltpu.VMEM(g + (channels,), jnp.float32) for g in grown],
        compiler_params=pltpu.CompilerParams(vmem_limit_bytes=44 * 1024 * 1024),
        cost_estimate=pl.CostEstimate(
            flops=6 * 10**9, bytes_accessed=4 * 10**6, transcendentals=0
        ),
        name="backward_block",
    )(lat_at, wide_all, attn_near, cot_near, near_slope, hidden_one, feat_x, conv_near, conv_wide)


def reduce_all(terms):
    rows, channels = terms.shape
    part = rows // 32
    piece = part * channels // 16
    band = lax.all_to_all(
        terms.reshape(32, part, channels), ("x", "y", "core"), 0, 0, tiled=True
    )
    band = band.astype(jnp.float32).sum(0).astype(jnp.bfloat16).reshape(16, piece)
    band = lax.all_to_all(band, ("zh", "zl"), 0, 0, tiled=True)
    band = band.astype(jnp.float32).sum(0).astype(jnp.bfloat16)
    band = lax.all_to_all(
        jnp.broadcast_to(band[None], (16, piece)), ("zh", "zl"), 0, 0, tiled=True
    ).reshape(part, channels)
    return lax.all_to_all(
        jnp.broadcast_to(band[None], (32, part, channels)), ("x", "y", "core"), 0, 0, tiled=True
    ).reshape(rows, channels)


def on_device(
    features, queries, attn_keys, attn_values, cotangent, conv_near, conv_wide, proj_qkv, proj_out
):
    rows, cols, channels = features.shape
    factor = float(rows * cols * 512) ** (-0.5)
    lat_at = lax.axis_index(LAT_AXES).astype(jnp.int32).reshape(1)
    half_at = lax.axis_index("zh")

    def to_rows(*fields):
        grown = [jnp.pad(f, ((0, 0), (0, GROWN - f.shape[1]), (0, 0))) for f in fields]
        return lax.all_to_all(jnp.concatenate(grown, axis=1), PLANE, 0, 0, tiled=True)

    side = channels // 2
    kv_own = to_rows(
        jnp.concatenate([attn_keys[..., :side], attn_values[..., :side]], axis=2),
        jnp.concatenate([attn_values[..., side:], attn_keys[..., side:]], axis=2),
    )
    kv_one, kv_two = kv_own[:, :GROWN], kv_own[:, GROWN:]
    far_one = lax.ppermute(kv_one, "zh", SWAP)
    far_two = lax.ppermute(kv_two, "zh", SWAP)

    features, cotangent, kv_one, kv_two = lax.optimization_barrier(
        (features, cotangent, kv_one, kv_two)
    )
    blank = jnp.zeros((rows, 1, channels), features.dtype)
    low, high = exchange_lon(
        jnp.concatenate([features[:, :10], cotangent[:, :EDGE], blank], axis=1),
        jnp.concatenate([features[:, -10:], cotangent[:, -EDGE:], blank], axis=1),
    )
    qc_own = to_rows(queries, cotangent)
    feat_x = jnp.concatenate(
        [low[:, :10], features, high[:, :10], jnp.zeros((rows, 18, channels), features.dtype)],
        axis=1,
    )
    cot_x = jnp.concatenate(
        [low[:, 10:15], cotangent, high[:, 10:15], jnp.zeros((rows, 28, channels), features.dtype)],
        axis=1,
    )
    feat_x, far_one = lax.optimization_barrier((feat_x, far_one))
    low, high = exchange_lat(
        jnp.concatenate([feat_x[-5:], cot_x[-1:]], axis=0),
        jnp.concatenate([feat_x[:5], cot_x[:1]], axis=0),
    )
    feat_x = jnp.concatenate([low[:5], feat_x, high[:5]], axis=0)
    cot_near = jnp.concatenate([low[5:], cot_x, high[5:]], axis=0)[:, :112]

    hidden_two, hidden_one, near_slope, wide_slope = forward(lat_at, feat_x, conv_near, conv_wide)
    hid_own = to_rows(hidden_two)
    hid_far = lax.ppermute(hid_own, "zh", SWAP)

    first = attention(qc_own, kv_one, far_one, proj_out, (0, HEADS // 2))
    second = attention(qc_own, kv_two, far_two, proj_out, (HEADS // 2, HEADS))
    own_part, far_part, sent, out_term, own_qkv, far_kv = combine(first, second, qc_own, proj_qkv)
    sent, hid_far = lax.optimization_barrier((sent, hid_far))
    from_far = lax.ppermute(sent, "zh", SWAP)
    whole = (own_part + from_far.astype(jnp.float32)).astype(jnp.bfloat16)
    whole = whole.reshape(4, 2, GROWN, channels)
    away = far_part.reshape(4, 2, GROWN, channels)
    edge = from_far.reshape(4, 2, GROWN, channels)[:, :, COLS : COLS + EDGE].astype(jnp.float32)
    edge_low = (edge[:, 0] + away[:, 0, :EDGE]).astype(jnp.bfloat16)
    edge_high = (edge[:, 1] + away[:, 1, COLS - EDGE : COLS]).astype(jnp.bfloat16)
    left = jnp.where(half_at == 1, edge_high, jnp.roll(edge_high, 1, axis=0))
    right = jnp.where(half_at == 0, edge_low, jnp.roll(edge_low, -1, axis=0))
    left = jnp.stack([left, whole[:, 0, COLS - EDGE : COLS]], axis=1)
    right = jnp.stack([whole[:, 1, :EDGE], right], axis=1)
    blank = jnp.zeros((4, 2, 12, channels), jnp.bfloat16)
    attn_x = jnp.concatenate([left, whole[:, :, :COLS], right, blank], axis=2)
    attn_x = lax.all_to_all(attn_x.reshape(8, 112, channels), PLANE, 0, 0, tiled=True)
    hid_flat = hid_own.reshape(-1, channels)
    far_flat = hid_far.reshape(-1, channels)
    query_term = contract_rows(hid_flat, own_qkv[:, :channels])
    kv_term = contract_rows(hid_flat, own_qkv[:, channels:]) + contract_rows(far_flat, far_kv)

    outer_x = cot_x[:, :112].astype(jnp.float32) + attn_x.astype(jnp.float32)
    wide_x = (outer_x * wide_slope).astype(jnp.bfloat16)
    low, high = exchange_lat(
        jnp.concatenate([wide_x[-5:], attn_x[-1:]], axis=0),
        jnp.concatenate([wide_x[:5], attn_x[:1]], axis=0),
    )
    wide_all = jnp.concatenate([low[:5], wide_x, high[:5]], axis=0)
    attn_near = jnp.concatenate([low[5:], attn_x, high[5:]], axis=0)
    feature_grad, conv_terms = backward(
        lat_at, wide_all, attn_near, cot_near, near_slope, hidden_one, feat_x, conv_near,
        conv_wide, factor,
    )

    others = jnp.concatenate([query_term, kv_term[:, :channels], kv_term[:, channels:], out_term])
    terms = jnp.concatenate([conv_terms, (others * factor).astype(jnp.bfloat16)])
    sums = reduce_all(terms).astype(jnp.float32)
    taps = 9 * channels
    near_sum = sums[:taps].reshape(3, 3, channels, channels)
    wide_sum = sums[taps : 2 * taps].reshape(3, 3, channels, channels)
    qkv_sum = jnp.concatenate(
        [sums[2 * taps + i * channels : 2 * taps + (i + 1) * channels] for i in range(3)], axis=1
    )
    out_sum = sums[2 * taps + 3 * channels :]
    return (feature_grad, near_sum, wide_sum, qkv_sum, out_sum)


def solution(mesh):
    grid = Mesh(mesh.devices.reshape(4, 2, 2, 8, 4), LON_AXES + LAT_AXES)
    field = P(LAT_AXES, LON_AXES, None)
    return jax.shard_map(
        on_device,
        mesh=grid,
        in_specs=(field,) * 5 + (P(),) * 4,
        out_specs=(field, P(), P(), P(), P()),
        check_vma=False,
    )
```

```python
import functools

import jax
import jax.numpy as jnp
from jax import lax
from jax.experimental import pallas as pl
from jax.experimental.pallas import tpu as pltpu
from jax.sharding import Mesh, PartitionSpec as P

HEADS = 8
COLS = 90
GROWN = 96
EDGE = 5
CHUNK = 256
GELU_COEF = 0.7978845608028654
CUBIC_COEF = 0.044715

LON_AXES = ("x", "zh", "core")
LAT_AXES = ("zl", "y")
PLANE = ("x", "core")
SWAP = [(0, 1), (1, 0)]


def gelu_value(pre_act):
    tanh_val = jnp.tanh(GELU_COEF * (pre_act + CUBIC_COEF * pre_act * pre_act * pre_act))
    return 0.5 * pre_act * (1.0 + tanh_val)


def gelu_slope(pre_act):
    tanh_val = jnp.tanh(GELU_COEF * (pre_act + CUBIC_COEF * pre_act * pre_act * pre_act))
    inner_d = GELU_COEF * (1.0 + 3.0 * CUBIC_COEF * pre_act * pre_act)
    return 0.5 * (1.0 + tanh_val) + 0.5 * pre_act * (1.0 - tanh_val * tanh_val) * inner_d


def contract_rows(left, right):
    return lax.dot_general(
        left, right, (((0,), (0,)), ((), ())), preferred_element_type=jnp.float32
    )


def exchange_lon(left, right):
    at_zero = lax.axis_index("core") == 0
    inner = lax.ppermute(jnp.where(at_zero, right, left), "core", SWAP)
    pairs = [(i, (i + 1) % 16 if i % 2 else (i - 1) % 16) for i in range(16)]
    outer = lax.ppermute(jnp.where(at_zero, left, right), LON_AXES, pairs)
    return jnp.where(at_zero, outer, inner), jnp.where(at_zero, inner, outer)


def exchange_lat(bottom, top):
    chain = [(i, i + 1) for i in range(31)]
    low = lax.ppermute(bottom, LAT_AXES, chain)
    high = lax.ppermute(top, LAT_AXES, [(b, a) for a, b in chain])
    return low, high


def attend_rows(qc_ref, own_ref, far_ref, proj_ref, mixed_ref, grad_ref, away_ref,
                out_s, keep_s, grad_s, pair_s, value_s, key_g, value_g, query_g, mixed_g, *, heads):
    blocks, wide, channels = own_ref.shape
    rows = blocks * wide
    cols = 2 * rows
    width = channels // HEADS
    chunk = CHUNK
    low = jnp.bfloat16

    def rows_of(ref, at):
        return ref[:, at : at + wide, :].reshape(rows, channels)

    out_s[...] = lax.dot_general(
        rows_of(qc_ref, wide), proj_ref[...], (((1,), (1,)), ((), ())),
        preferred_element_type=jnp.float32,
    )
    pair = jnp.concatenate([rows_of(own_ref, 0), rows_of(far_ref, 0)], axis=0).astype(jnp.float32)
    pair_s[...] = pair
    value_s[...] = pltpu.roll(pair, channels // 2, 1)
    for ref in (key_g, value_g, query_g, mixed_g):
        ref[...] = jnp.zeros_like(ref)
    lane_k = lax.broadcasted_iota(jnp.int32, (cols, channels), 1)
    filler = lax.broadcasted_iota(jnp.int32, (cols, channels), 0) % wide >= COLS
    lane_q = lax.broadcasted_iota(jnp.int32, (chunk, channels), 1)

    def one_head(head, carry):
        first = (head * width + width) % channels
        here_k = lane_k // width == head
        here_q = lane_q // width == head
        spare = jnp.where((lane_k == first) & filler, -1e30, 0.0)
        keys_h = jnp.where(here_k, pair_s[...], spare).astype(low)
        ones = jnp.where((lane_k == first) | (lane_k == first + 1), 1.0, 0.0)
        values_h = jnp.where(here_k, value_s[...], ones).astype(low)
        query_n, dout_n = [], []
        for i in range(rows // chunk):
            at = i * chunk
            query = rows_of(qc_ref, 0)[at : at + chunk].astype(jnp.float32) * 0.25
            query_h = jnp.where(here_q, query, jnp.where(lane_q == first, 1.0, 0.0)).astype(low)
            dout = out_s[at : at + chunk, :].astype(low).astype(jnp.float32)
            dout = jnp.where(here_q, dout, 0.0)
            scores = lax.dot_general(
                query_h, keys_h, (((1,), (1,)), ((), ())), preferred_element_type=jnp.float32
            )
            top = jnp.max(scores, axis=1, keepdims=True)
            raised = jnp.exp(scores - top).astype(low)
            keep_s[at : at + chunk, :] = raised
            mixed = jnp.dot(raised, values_h, preferred_element_type=jnp.float32)
            total = jnp.sum(jnp.where(lane_q == first, mixed, 0.0), axis=1, keepdims=True)
            share = 1.0 / total
            mixed = jnp.where(here_q, mixed * share, 0.0)
            mixed_g[at : at + chunk, :] += mixed
            delta = jnp.sum(dout * mixed, axis=1, keepdims=True)
            high = delta.astype(low).astype(jnp.float32)
            dout_x = jnp.where(
                lane_q == first, -high, jnp.where(lane_q == first + 1, high - delta, dout)
            ).astype(low)
            prob_grad = lax.dot_general(
                dout_x, values_h, (((1,), (1,)), ((), ())), preferred_element_type=jnp.float32
            )
            score_grad = raised * prob_grad.astype(low)
            grad_s[at : at + chunk, :] = score_grad
            query_g[at : at + chunk, :] += (
                jnp.dot(score_grad, keys_h, preferred_element_type=jnp.float32) * (0.25 * share)
            )
            query_n.append((jnp.where(here_q, query, 0.0) * share).astype(low))
            dout_n.append((dout * share).astype(low))
        key_g[...] += lax.dot_general(
            grad_s[...], jnp.concatenate(query_n, axis=0), (((0,), (0,)), ((), ())),
            preferred_element_type=jnp.float32,
        )
        value_g[...] += lax.dot_general(
            keep_s[...], jnp.concatenate(dout_n, axis=0), (((0,), (0,)), ((), ())),
            preferred_element_type=jnp.float32,
        )
        return carry

    lax.fori_loop(heads[0], heads[1], one_head, 0)
    mixed_ref[...] = mixed_g[...].astype(low)
    grad_ref[:, :channels] = query_g[...].astype(low)
    grad_ref[:, channels : 2 * channels] = key_g[:rows, :].astype(low)
    grad_ref[:, 2 * channels :] = value_g[:rows, :].astype(low)
    away_ref[:, :channels] = key_g[rows:, :].astype(low)
    away_ref[:, channels:] = value_g[rows:, :].astype(low)


def attention(qc_own, kv_own, kv_far, proj_out, heads):
    blocks, wide, channels = kv_own.shape
    rows = blocks * wide
    low = jnp.bfloat16
    shapes = [(rows, channels), (rows, 3 * channels), (rows, 2 * channels)]
    return pl.pallas_call(
        functools.partial(attend_rows, heads=heads),
        out_shape=[jax.ShapeDtypeStruct(s, low) for s in shapes],
        in_specs=[pl.BlockSpec(memory_space=pltpu.VMEM)] * 4,
        out_specs=[pl.BlockSpec(memory_space=pltpu.VMEM)] * 3,
        scratch_shapes=[
            pltpu.VMEM((rows, channels), jnp.float32),
            pltpu.VMEM((rows, 2 * rows), low),
            pltpu.VMEM((rows, 2 * rows), low),
            pltpu.VMEM((2 * rows, channels), jnp.float32),
            pltpu.VMEM((2 * rows, channels), jnp.float32),
            pltpu.VMEM((2 * rows, channels), jnp.float32),
            pltpu.VMEM((2 * rows, channels), jnp.float32),
            pltpu.VMEM((rows, channels), jnp.float32),
            pltpu.VMEM((rows, channels), jnp.float32),
        ],
        compiler_params=pltpu.CompilerParams(vmem_limit_bytes=48 * 1024 * 1024),
        cost_estimate=pl.CostEstimate(
            flops=12 * rows * 2 * rows * channels * (heads[1] - heads[0]),
            bytes_accessed=16 * rows * channels,
            transcendentals=(heads[1] - heads[0]) * rows * 2 * rows,
        ),
        name="attend_rows",
    )(qc_own, kv_own, kv_far, proj_out)


def gather_parts(first_refs, second_refs, cot_ref, qkv_ref, part_ref, away_ref, send_ref, term_ref,
                 all_ref, far_ref, send_s):
    channels = cot_ref.shape[2]
    blocks, wide = cot_ref.shape[0], cot_ref.shape[1] // 2
    rows = blocks * wide
    low = jnp.bfloat16
    mixed, own, far = (a[...] + b[...] for a, b in zip(first_refs, second_refs))
    all_ref[...] = own
    far_ref[...] = far
    own_part = lax.dot_general(
        own, qkv_ref[...], (((1,), (1,)), ((), ())), preferred_element_type=jnp.float32
    )
    far_part = lax.dot_general(
        far, qkv_ref[:, channels:], (((1,), (1,)), ((), ())), preferred_element_type=jnp.float32
    )
    part_ref[...] = own_part.reshape(blocks, wide, channels)
    away_ref[...] = far_part.reshape(blocks, wide, channels)
    send_s[...] = far_part.reshape(blocks, wide, channels)
    for block in range(blocks):
        edge = 0 if block % 2 == 0 else COLS - EDGE
        send_s[block, COLS : COLS + EDGE, :] = part_ref[block, edge : edge + EDGE, :]
    send_ref[...] = send_s[...].astype(low)
    cot = cot_ref[:, wide:, :].reshape(rows, channels)
    term_ref[...] = contract_rows(mixed, cot)


def combine(first, second, qc_own, proj_qkv):
    blocks, double, channels = qc_own.shape
    wide = double // 2
    rows = blocks * wide
    low = jnp.bfloat16
    shapes = [
        ((blocks, wide, channels), jnp.float32),
        ((blocks, wide, channels), jnp.float32),
        ((blocks, wide, channels), low),
        ((channels, channels), jnp.float32),
        ((rows, 3 * channels), low),
        ((rows, 2 * channels), low),
    ]

    def body(*refs):
        gather_parts(refs[:3], refs[3:6], *refs[6:])

    return pl.pallas_call(
        body,
        out_shape=[jax.ShapeDtypeStruct(s, t) for s, t in shapes],
        in_specs=[pl.BlockSpec(memory_space=pltpu.VMEM)] * 8,
        out_specs=[pl.BlockSpec(memory_space=pltpu.VMEM)] * 6,
        scratch_shapes=[pltpu.VMEM((blocks, wide, channels), jnp.float32)],
        compiler_params=pltpu.CompilerParams(vmem_limit_bytes=24 * 1024 * 1024),
        cost_estimate=pl.CostEstimate(
            flops=12 * rows * channels * channels, bytes_accessed=5 * 10**6, transcendentals=0
        ),
        name="combine",
    )(*first, *second, qc_own, proj_qkv)


def row_inside(lat_ref, shape, width):
    at = lat_ref[0] * 8 + lax.broadcasted_iota(jnp.int32, shape, 0) - width
    return (at >= 0) & (at < 256)


def three(ref, starts, count):
    return jnp.concatenate(
        [ref[:, at : at + count, :].astype(jnp.bfloat16) for at in starts], axis=2
    )


def forward_block(lat_ref, feat_ref, near_ref, wide_ref, two_ref, one_ref, nslope_ref, wslope_ref,
                  feat_s, one_s, wide_s):
    channels = feat_ref.shape[2]
    low = jnp.bfloat16
    cols = 112
    feat_s[...] = feat_ref[...].astype(jnp.float32)
    feat_3 = three(feat_s, (0, 1, 2), cols)
    total = jnp.zeros((16 * cols, channels), jnp.float32)
    for tap in range(3):
        weight = near_ref[tap].reshape(3 * channels, channels)
        total += jnp.dot(
            feat_3[tap : tap + 16].reshape(16 * cols, 3 * channels), weight,
            preferred_element_type=jnp.float32,
        )
    pre_near = total.reshape(16, cols, channels)
    nslope_ref[...] = gelu_slope(pre_near[3:13])
    one = (feat_s[1:17, 1 : 1 + cols, :] + gelu_value(pre_near)).astype(low)
    one = jnp.where(row_inside(lat_ref, one.shape, 4), one.astype(jnp.float32), 0.0)
    one_ref[...] = one.astype(low)
    one_s[...] = jnp.zeros_like(one_s)
    one_s[:, :cols, :] = one
    one_3 = three(one_s, (0, 4, 8), cols)
    total = jnp.zeros((8 * cols, channels), jnp.float32)
    for tap in range(3):
        weight = wide_ref[tap].reshape(3 * channels, channels)
        total += jnp.dot(
            one_3[4 * tap : 4 * tap + 8].reshape(8 * cols, 3 * channels), weight,
            preferred_element_type=jnp.float32,
        )
    pre_wide = total.reshape(8, cols, channels)
    wslope_ref[...] = gelu_slope(pre_wide)
    wide_s[...] = gelu_value(pre_wide)
    two = one_s[4:12, 9 : 9 + GROWN, :] + wide_s[:, EDGE : EDGE + GROWN, :]
    valid = lax.broadcasted_iota(jnp.int32, two.shape, 1) < COLS
    two_ref[...] = jnp.where(valid, two, 0.0).astype(low)


def forward(lat_at, feat_x, conv_near, conv_wide):
    channels = feat_x.shape[2]
    shapes = [
        ((8, GROWN, channels), jnp.bfloat16),
        ((16, 112, channels), jnp.bfloat16),
        ((10, 112, channels), jnp.float32),
        ((8, 112, channels), jnp.float32),
    ]
    return pl.pallas_call(
        forward_block,
        out_shape=[jax.ShapeDtypeStruct(s, t) for s, t in shapes],
        in_specs=[pl.BlockSpec(memory_space=pltpu.SMEM)]
        + [pl.BlockSpec(memory_space=pltpu.VMEM)] * 3,
        out_specs=[pl.BlockSpec(memory_space=pltpu.VMEM)] * 4,
        scratch_shapes=[
            pltpu.VMEM((18, 128, channels), jnp.float32),
            pltpu.VMEM((16, 128, channels), jnp.float32),
            pltpu.VMEM((8, 112, channels), jnp.float32),
        ],
        compiler_params=pltpu.CompilerParams(vmem_limit_bytes=40 * 1024 * 1024),
        cost_estimate=pl.CostEstimate(
            flops=6 * 10**9, bytes_accessed=4 * 10**6, transcendentals=2 * 10**5
        ),
        name="forward_block",
    )(lat_at, feat_x, conv_near, conv_wide)


def backward_block(lat_ref, wide_ref, attn_ref, cot_ref, nslope_ref, one_ref, feat_ref, near_ref,
                   dil_ref, out_ref, term_ref, wide_s, outer_s, slope_s, one_s, feat_s, total_s,
                   near_s, *, factor):
    channels = wide_ref.shape[2]
    low = jnp.bfloat16
    cols = GROWN

    def transposed(ref, tap):
        return jnp.concatenate([ref[tap, i] for i in range(3)], axis=1)

    wide_s[...] = wide_ref[...].astype(jnp.float32)
    outer_s[...] = cot_ref[...].astype(jnp.float32) + attn_ref[...].astype(jnp.float32)
    slope_s[...] = nslope_ref[...]
    one_s[...] = one_ref[...].astype(jnp.float32)
    feat_s[...] = feat_ref[...].astype(jnp.float32)
    wide_3 = three(wide_s, (8, 4, 0), cols)
    total = jnp.zeros((10 * cols, channels), jnp.float32)
    for tap in range(3):
        at = 8 - 4 * tap
        total += lax.dot_general(
            wide_3[at : at + 10].reshape(10 * cols, 3 * channels), transposed(dil_ref, tap),
            (((1,), (1,)), ((), ())), preferred_element_type=jnp.float32,
        )
    near_total = total.reshape(10, cols, channels) + outer_s[:, 4 : 4 + cols, :]
    near_grad = (near_total * slope_s[:, 8 : 8 + cols, :]).astype(low).astype(jnp.float32)
    near_grad = jnp.where(row_inside(lat_ref, near_grad.shape, 1), near_grad, 0.0)
    for ref, value in ((total_s, near_total), (near_s, near_grad)):
        ref[...] = jnp.zeros_like(ref)
        ref[:, :cols, :] = value
    near_3 = three(near_s, (2, 1, 0), cols)
    total = jnp.zeros((8 * cols, channels), jnp.float32)
    for tap in range(3):
        at = 2 - tap
        total += lax.dot_general(
            near_3[at : at + 8].reshape(8 * cols, 3 * channels), transposed(near_ref, tap),
            (((1,), (1,)), ((), ())), preferred_element_type=jnp.float32,
        )
    feature = (total.reshape(8, cols, channels) + total_s[1:9, 1 : 1 + cols, :]).astype(low)
    out_ref[...] = feature[:, :COLS, :]

    valid = lax.broadcasted_iota(jnp.int32, (8, cols, channels), 1) < COLS
    own_near = jnp.where(valid, near_s[1:9, 1 : 1 + cols, :], 0.0)
    own_near = own_near.astype(low).reshape(8 * cols, channels)
    own_wide = jnp.where(valid, wide_s[5:13, EDGE : EDGE + cols, :], 0.0)
    own_wide = own_wide.astype(low).reshape(8 * cols, channels)
    feat_3 = three(feat_s, (9, 10, 11), cols)
    one_3 = three(one_s, (5, 9, 13), cols)
    long = 3 * channels
    for tap in range(3):
        for left, right, at in (
            (feat_3[4 + tap : 12 + tap], own_near, tap * long),
            (one_3[4 * tap : 4 * tap + 8], own_wide, (3 + tap) * long),
        ):
            term = contract_rows(left.reshape(8 * cols, long), right)
            term_ref[at : at + long, :] = (term * factor).astype(low)


def backward(lat_at, wide_all, attn_near, cot_near, near_slope, hidden_one, feat_x, conv_near,
             conv_wide, factor):
    channels = feat_x.shape[2]
    low = jnp.bfloat16
    shapes = [((8, COLS, channels), low), ((18 * channels, channels), low)]
    grown = [(18, 112), (10, 112), (10, 112), (16, 112), (18, 128), (10, 112), (10, 112)]
    return pl.pallas_call(
        functools.partial(backward_block, factor=factor),
        out_shape=[jax.ShapeDtypeStruct(s, t) for s, t in shapes],
        in_specs=[pl.BlockSpec(memory_space=pltpu.SMEM)]
        + [pl.BlockSpec(memory_space=pltpu.VMEM)] * 8,
        out_specs=[pl.BlockSpec(memory_space=pltpu.VMEM)] * 2,
        scratch_shapes=[pltpu.VMEM(g + (channels,), jnp.float32) for g in grown],
        compiler_params=pltpu.CompilerParams(vmem_limit_bytes=44 * 1024 * 1024),
        cost_estimate=pl.CostEstimate(
            flops=6 * 10**9, bytes_accessed=4 * 10**6, transcendentals=0
        ),
        name="backward_block",
    )(lat_at, wide_all, attn_near, cot_near, near_slope, hidden_one, feat_x, conv_near, conv_wide)


def reduce_all(terms):
    rows, channels = terms.shape
    part = rows // 32
    piece = part * channels // 16
    band = lax.all_to_all(
        terms.reshape(32, part, channels), ("x", "y", "core"), 0, 0, tiled=True
    )
    band = band.astype(jnp.float32).sum(0).astype(jnp.bfloat16).reshape(16, piece)
    band = lax.all_to_all(band, ("zh", "zl"), 0, 0, tiled=True)
    band = band.astype(jnp.float32).sum(0).astype(jnp.bfloat16)
    band = lax.all_to_all(
        jnp.broadcast_to(band[None], (16, piece)), ("zh", "zl"), 0, 0, tiled=True
    ).reshape(part, channels)
    return lax.all_to_all(
        jnp.broadcast_to(band[None], (32, part, channels)), ("x", "y", "core"), 0, 0, tiled=True
    ).reshape(rows, channels)


def on_device(
    features, queries, attn_keys, attn_values, cotangent, conv_near, conv_wide, proj_qkv, proj_out
):
    rows, cols, channels = features.shape
    factor = float(rows * cols * 512) ** (-0.5)
    lat_at = lax.axis_index(LAT_AXES).astype(jnp.int32).reshape(1)
    half_at = lax.axis_index("zh")

    def to_rows(*fields):
        grown = [jnp.pad(f, ((0, 0), (0, GROWN - f.shape[1]), (0, 0))) for f in fields]
        return lax.all_to_all(jnp.concatenate(grown, axis=1), PLANE, 0, 0, tiled=True)

    blank = jnp.zeros((rows, 1, channels), features.dtype)
    low, high = exchange_lon(
        jnp.concatenate([features[:, :10], cotangent[:, :EDGE], blank], axis=1),
        jnp.concatenate([features[:, -10:], cotangent[:, -EDGE:], blank], axis=1),
    )
    low, high, attn_keys, attn_values = lax.optimization_barrier(
        (low, high, attn_keys, attn_values)
    )

    side = channels // 2
    kv_own = to_rows(
        jnp.concatenate([attn_keys[..., :side], attn_values[..., :side]], axis=2),
        jnp.concatenate([attn_values[..., side:], attn_keys[..., side:]], axis=2),
    )

    feat_x = jnp.concatenate(
        [low[:, :10], features, high[:, :10], jnp.zeros((rows, 18, channels), features.dtype)],
        axis=1,
    )
    cot_x = jnp.concatenate(
        [low[:, 10:15], cotangent, high[:, 10:15], jnp.zeros((rows, 28, channels), features.dtype)],
        axis=1,
    )
    low, high = exchange_lat(
        jnp.concatenate([feat_x[-5:], cot_x[-1:]], axis=0),
        jnp.concatenate([feat_x[:5], cot_x[:1]], axis=0),
    )
    low, high, kv_own, queries = lax.optimization_barrier((low, high, kv_own, queries))
    kv_one, kv_two = kv_own[:, :GROWN], kv_own[:, GROWN:]
    far_one = lax.ppermute(kv_one, "zh", SWAP)
    far_two = lax.ppermute(kv_two, "zh", SWAP)
    qc_own = to_rows(queries, cotangent)
    feat_x = jnp.concatenate([low[:5], feat_x, high[:5]], axis=0)
    cot_near = jnp.concatenate([low[5:], cot_x, high[5:]], axis=0)[:, :112]

    hidden_two, hidden_one, near_slope, wide_slope = forward(lat_at, feat_x, conv_near, conv_wide)
    hid_far = lax.ppermute(hidden_two, "zh", SWAP)
    far_one, hidden_two = lax.optimization_barrier((far_one, hidden_two))

    first = attention(qc_own, kv_one, far_one, proj_out, (0, HEADS // 2))
    first, kv_two = lax.optimization_barrier((first, kv_two))
    second = attention(qc_own, kv_two, far_two, proj_out, (HEADS // 2, HEADS))
    own_part, far_part, sent, out_term, own_qkv, far_kv = combine(first, second, qc_own, proj_qkv)
    sent, hid_far = lax.optimization_barrier((sent, hid_far))
    hid_rows = to_rows(hidden_two, hid_far)
    from_far = lax.ppermute(sent, "zh", SWAP)
    whole = (own_part + from_far.astype(jnp.float32)).astype(jnp.bfloat16)
    whole = whole.reshape(4, 2, GROWN, channels)
    away = far_part.reshape(4, 2, GROWN, channels)
    edge = from_far.reshape(4, 2, GROWN, channels)[:, :, COLS : COLS + EDGE].astype(jnp.float32)
    edge_low = (edge[:, 0] + away[:, 0, :EDGE]).astype(jnp.bfloat16)
    edge_high = (edge[:, 1] + away[:, 1, COLS - EDGE : COLS]).astype(jnp.bfloat16)
    left = jnp.where(half_at == 1, edge_high, jnp.roll(edge_high, 1, axis=0))
    right = jnp.where(half_at == 0, edge_low, jnp.roll(edge_low, -1, axis=0))
    left = jnp.stack([left, whole[:, 0, COLS - EDGE : COLS]], axis=1)
    right = jnp.stack([whole[:, 1, :EDGE], right], axis=1)
    blank = jnp.zeros((4, 2, 12, channels), jnp.bfloat16)
    attn_x = jnp.concatenate([left, whole[:, :, :COLS], right, blank], axis=2)
    attn_x = lax.all_to_all(attn_x.reshape(8, 112, channels), PLANE, 0, 0, tiled=True)
    hid_flat = hid_rows[:, :GROWN].reshape(-1, channels)
    far_flat = hid_rows[:, GROWN:].reshape(-1, channels)
    query_term = contract_rows(hid_flat, own_qkv[:, :channels])
    kv_term = contract_rows(hid_flat, own_qkv[:, channels:]) + contract_rows(far_flat, far_kv)

    outer_x = cot_x[:, :112].astype(jnp.float32) + attn_x.astype(jnp.float32)
    wide_x = (outer_x * wide_slope).astype(jnp.bfloat16)
    low, high = exchange_lat(
        jnp.concatenate([wide_x[-5:], attn_x[-1:]], axis=0),
        jnp.concatenate([wide_x[:5], attn_x[:1]], axis=0),
    )
    wide_all = jnp.concatenate([low[:5], wide_x, high[:5]], axis=0)
    attn_near = jnp.concatenate([low[5:], attn_x, high[5:]], axis=0)
    feature_grad, conv_terms = backward(
        lat_at, wide_all, attn_near, cot_near, near_slope, hidden_one, feat_x, conv_near,
        conv_wide, factor,
    )

    others = jnp.concatenate([query_term, kv_term[:, :channels], kv_term[:, channels:], out_term])
    terms = jnp.concatenate([conv_terms, (others * factor).astype(jnp.bfloat16)])
    sums = reduce_all(terms).astype(jnp.float32)
    taps = 9 * channels
    near_sum = sums[:taps].reshape(3, 3, channels, channels)
    wide_sum = sums[taps : 2 * taps].reshape(3, 3, channels, channels)
    qkv_sum = jnp.concatenate(
        [sums[2 * taps + i * channels : 2 * taps + (i + 1) * channels] for i in range(3)], axis=1
    )
    out_sum = sums[2 * taps + 3 * channels :]
    return (feature_grad, near_sum, wide_sum, qkv_sum, out_sum)


def solution(mesh):
    grid = Mesh(mesh.devices.reshape(4, 2, 2, 8, 4), LON_AXES + LAT_AXES)
    field = P(LAT_AXES, LON_AXES, None)
    return jax.shard_map(
        on_device,
        mesh=grid,
        in_specs=(field,) * 5 + (P(),) * 4,
        out_specs=(field, P(), P(), P(), P()),
        check_vma=False,
    )
```

```python
import functools

import jax
import jax.numpy as jnp
from jax import lax
from jax.experimental import pallas as pl
from jax.experimental.pallas import tpu as pltpu
from jax.sharding import Mesh, PartitionSpec as P

HEADS = 8
COLS = 90
GROWN = 96
EDGE = 5
CHUNK = 256
GELU_COEF = 0.7978845608028654
CUBIC_COEF = 0.044715

LON_AXES = ("x", "zh", "core")
LAT_AXES = ("zl", "y")
PLANE = ("x", "core")
SWAP = [(0, 1), (1, 0)]


def gelu_value(pre_act):
    tanh_val = jnp.tanh(GELU_COEF * (pre_act + CUBIC_COEF * pre_act * pre_act * pre_act))
    return 0.5 * pre_act * (1.0 + tanh_val)


def gelu_slope(pre_act):
    tanh_val = jnp.tanh(GELU_COEF * (pre_act + CUBIC_COEF * pre_act * pre_act * pre_act))
    inner_d = GELU_COEF * (1.0 + 3.0 * CUBIC_COEF * pre_act * pre_act)
    return 0.5 * (1.0 + tanh_val) + 0.5 * pre_act * (1.0 - tanh_val * tanh_val) * inner_d


def contract_rows(left, right):
    return lax.dot_general(
        left, right, (((0,), (0,)), ((), ())), preferred_element_type=jnp.float32
    )


def exchange_lon(left, right):
    at_zero = lax.axis_index("core") == 0
    inner = lax.ppermute(jnp.where(at_zero, right, left), "core", SWAP)
    pairs = [(i, (i + 1) % 16 if i % 2 else (i - 1) % 16) for i in range(16)]
    outer = lax.ppermute(jnp.where(at_zero, left, right), LON_AXES, pairs)
    return jnp.where(at_zero, outer, inner), jnp.where(at_zero, inner, outer)


def exchange_lat(bottom, top):
    chain = [(i, i + 1) for i in range(31)]
    low = lax.ppermute(bottom, LAT_AXES, chain)
    high = lax.ppermute(top, LAT_AXES, [(b, a) for a, b in chain])
    return low, high


def attend_rows(*refs, heads, last):
    qc_ref, own_ref, far_ref, proj_ref = refs[:4]
    out_s, keep_s, grad_s, pair_s, value_s, key_g, value_g, query_g, mixed_g = refs[-9:]
    blocks, wide, channels = own_ref.shape
    rows = blocks * wide
    cols = 2 * rows
    width = channels // HEADS
    chunk = CHUNK
    low = jnp.bfloat16

    def rows_of(ref, at):
        return ref[:, at : at + wide, :].reshape(rows, channels)

    out_s[...] = lax.dot_general(
        rows_of(qc_ref, wide), proj_ref[...], (((1,), (1,)), ((), ())),
        preferred_element_type=jnp.float32,
    )
    pair = jnp.concatenate([rows_of(own_ref, 0), rows_of(far_ref, 0)], axis=0).astype(jnp.float32)
    pair_s[...] = pair
    value_s[...] = pltpu.roll(pair, channels // 2, 1)
    for ref in (key_g, value_g, query_g, mixed_g):
        ref[...] = jnp.zeros_like(ref)
    lane_k = lax.broadcasted_iota(jnp.int32, (cols, channels), 1)
    filler = lax.broadcasted_iota(jnp.int32, (cols, channels), 0) % wide >= COLS
    lane_q = lax.broadcasted_iota(jnp.int32, (chunk, channels), 1)

    def one_head(head, carry):
        first = (head * width + width) % channels
        here_k = lane_k // width == head
        here_q = lane_q // width == head
        spare = jnp.where((lane_k == first) & filler, -1e30, 0.0)
        keys_h = jnp.where(here_k, pair_s[...], spare).astype(low)
        ones = jnp.where((lane_k == first) | (lane_k == first + 1), 1.0, 0.0)
        values_h = jnp.where(here_k, value_s[...], ones).astype(low)
        spots = [slice(at, at + chunk) for at in range(0, rows, chunk)]
        queries, douts, shares, query_n, dout_n = [], [], [], [], []
        for spot in spots:
            query = rows_of(qc_ref, 0)[spot].astype(jnp.float32) * 0.25
            query_h = jnp.where(here_q, query, jnp.where(lane_q == first, 1.0, 0.0)).astype(low)
            queries.append(jnp.where(here_q, query, 0.0))
            scores = lax.dot_general(
                query_h, keys_h, (((1,), (1,)), ((), ())), preferred_element_type=jnp.float32
            )
            top = jnp.max(scores, axis=1, keepdims=True)
            keep_s[spot, :] = jnp.exp(scores - top).astype(low)
        for spot in spots:
            dout = out_s[spot, :].astype(low).astype(jnp.float32)
            dout = jnp.where(here_q, dout, 0.0)
            mixed = jnp.dot(keep_s[spot, :], values_h, preferred_element_type=jnp.float32)
            total = jnp.sum(jnp.where(lane_q == first, mixed, 0.0), axis=1, keepdims=True)
            share = 1.0 / total
            mixed = jnp.where(here_q, mixed * share, 0.0)
            mixed_g[spot, :] += mixed
            delta = jnp.sum(dout * mixed, axis=1, keepdims=True)
            high = delta.astype(low).astype(jnp.float32)
            douts.append(
                jnp.where(
                    lane_q == first, -high, jnp.where(lane_q == first + 1, high - delta, dout)
                ).astype(low)
            )
            shares.append(share)
            dout_n.append((dout * share).astype(low))
        value_g[...] += lax.dot_general(
            keep_s[...], jnp.concatenate(dout_n, axis=0), (((0,), (0,)), ((), ())),
            preferred_element_type=jnp.float32,
        )
        for spot, dout_x in zip(spots, douts):
            prob_grad = lax.dot_general(
                dout_x, values_h, (((1,), (1,)), ((), ())), preferred_element_type=jnp.float32
            )
            grad_s[spot, :] = keep_s[spot, :] * prob_grad.astype(low)
        for spot, query, share in zip(spots, queries, shares):
            query_g[spot, :] += (
                jnp.dot(grad_s[spot, :], keys_h, preferred_element_type=jnp.float32)
                * (0.25 * share)
            )
            query_n.append((query * share).astype(low))
        key_g[...] += lax.dot_general(
            grad_s[...], jnp.concatenate(query_n, axis=0), (((0,), (0,)), ((), ())),
            preferred_element_type=jnp.float32,
        )
        return carry

    lax.fori_loop(heads[0], heads[1], one_head, 0)
    mixed = mixed_g[...].astype(low)
    grads = [query_g[...].astype(low)]
    grads += [ref[:rows, :].astype(low) for ref in (key_g, value_g)]
    aways = [ref[rows:, :].astype(low) for ref in (key_g, value_g)]
    if not last:
        mixed_ref, grad_ref, away_ref = refs[4:7]
        mixed_ref[...] = mixed
        grad_ref[...] = jnp.concatenate(grads, axis=1)
        away_ref[...] = jnp.concatenate(aways, axis=1)
        return
    mixed_ref, grad_ref, away_ref, qkv_ref = refs[4:8]
    part_ref, apart_ref, send_ref, term_ref, all_ref, far_all_ref = refs[8:14]
    own = jnp.concatenate(grads, axis=1) + grad_ref[...]
    far = jnp.concatenate(aways, axis=1) + away_ref[...]
    all_ref[...] = own
    far_all_ref[...] = far
    own_part = lax.dot_general(
        own, qkv_ref[...], (((1,), (1,)), ((), ())), preferred_element_type=jnp.float32
    )
    far_part = lax.dot_general(
        far, qkv_ref[:, channels:], (((1,), (1,)), ((), ())), preferred_element_type=jnp.float32
    )
    part_ref[...] = own_part.reshape(blocks, wide, channels)
    apart_ref[...] = jnp.zeros_like(apart_ref)
    query_g[...] = far_part
    for block in range(blocks):
        edge = 0 if block % 2 == 0 else COLS - EDGE
        at = block * wide + COLS
        apart_ref[block, :EDGE, :] = query_g[at - COLS + edge : at - COLS + edge + EDGE, :]
        query_g[at : at + EDGE, :] = part_ref[block, edge : edge + EDGE, :]
    send_ref[...] = query_g[...].astype(low).reshape(blocks, wide, channels)
    term_ref[...] = contract_rows(mixed + mixed_ref[...], rows_of(qc_ref, wide))


def attention(qc_own, kv_own, kv_far, proj_out, heads, first=None, proj_qkv=None):
    blocks, wide, channels = kv_own.shape
    rows = blocks * wide
    low = jnp.bfloat16
    operands = [qc_own, kv_own, kv_far, proj_out]
    shapes = [((rows, channels), low), ((rows, 3 * channels), low), ((rows, 2 * channels), low)]
    if first is not None:
        operands += [*first, proj_qkv]
        shapes = [
            ((blocks, wide, channels), jnp.float32),
            ((blocks, 8, channels), jnp.float32),
            ((blocks, wide, channels), low),
            ((channels, channels), jnp.float32),
        ] + shapes[1:]
    return pl.pallas_call(
        functools.partial(attend_rows, heads=heads, last=first is not None),
        out_shape=[jax.ShapeDtypeStruct(s, t) for s, t in shapes],
        in_specs=[pl.BlockSpec(memory_space=pltpu.VMEM)] * len(operands),
        out_specs=[pl.BlockSpec(memory_space=pltpu.VMEM)] * len(shapes),
        scratch_shapes=[
            pltpu.VMEM((rows, channels), jnp.float32),
            pltpu.VMEM((rows, 2 * rows), low),
            pltpu.VMEM((rows, 2 * rows), low),
            pltpu.VMEM((2 * rows, channels), jnp.float32),
            pltpu.VMEM((2 * rows, channels), jnp.float32),
            pltpu.VMEM((2 * rows, channels), jnp.float32),
            pltpu.VMEM((2 * rows, channels), jnp.float32),
            pltpu.VMEM((rows, channels), jnp.float32),
            pltpu.VMEM((rows, channels), jnp.float32),
        ],
        compiler_params=pltpu.CompilerParams(vmem_limit_bytes=48 * 1024 * 1024),
        cost_estimate=pl.CostEstimate(
            flops=12 * rows * 2 * rows * channels * (heads[1] - heads[0]),
            bytes_accessed=16 * rows * channels,
            transcendentals=(heads[1] - heads[0]) * rows * 2 * rows,
        ),
        name="attend_rows",
    )(*operands)


def row_inside(lat_ref, shape, width):
    at = lat_ref[0] * 8 + lax.broadcasted_iota(jnp.int32, shape, 0) - width
    return (at >= 0) & (at < 256)


def three(ref, starts, count):
    return jnp.concatenate(
        [ref[:, at : at + count, :].astype(jnp.bfloat16) for at in starts], axis=2
    )


def forward_block(lat_ref, feat_ref, near_ref, wide_ref, two_ref, one_ref, nslope_ref, wslope_ref,
                  feat_s, one_s, wide_s):
    channels = feat_ref.shape[2]
    low = jnp.bfloat16
    cols = 112
    feat_s[...] = feat_ref[...].astype(jnp.float32)
    feat_3 = three(feat_s, (0, 1, 2), cols)
    total = jnp.zeros((16 * cols, channels), jnp.float32)
    for tap in range(3):
        weight = near_ref[tap].reshape(3 * channels, channels)
        total += jnp.dot(
            feat_3[tap : tap + 16].reshape(16 * cols, 3 * channels), weight,
            preferred_element_type=jnp.float32,
        )
    pre_near = total.reshape(16, cols, channels)
    nslope_ref[...] = gelu_slope(pre_near[3:13])
    one = (feat_s[1:17, 1 : 1 + cols, :] + gelu_value(pre_near)).astype(low)
    one = jnp.where(row_inside(lat_ref, one.shape, 4), one.astype(jnp.float32), 0.0)
    one_ref[...] = one.astype(low)
    one_s[...] = jnp.zeros_like(one_s)
    one_s[:, :cols, :] = one
    one_3 = three(one_s, (0, 4, 8), cols)
    total = jnp.zeros((8 * cols, channels), jnp.float32)
    for tap in range(3):
        weight = wide_ref[tap].reshape(3 * channels, channels)
        total += jnp.dot(
            one_3[4 * tap : 4 * tap + 8].reshape(8 * cols, 3 * channels), weight,
            preferred_element_type=jnp.float32,
        )
    pre_wide = total.reshape(8, cols, channels)
    wslope_ref[...] = gelu_slope(pre_wide)
    wide_s[...] = gelu_value(pre_wide)
    two = one_s[4:12, 9 : 9 + GROWN, :] + wide_s[:, EDGE : EDGE + GROWN, :]
    valid = lax.broadcasted_iota(jnp.int32, two.shape, 1) < COLS
    two_ref[...] = jnp.where(valid, two, 0.0).astype(low)


def forward(lat_at, feat_x, conv_near, conv_wide):
    channels = feat_x.shape[2]
    shapes = [
        ((8, GROWN, channels), jnp.bfloat16),
        ((16, 112, channels), jnp.bfloat16),
        ((10, 112, channels), jnp.float32),
        ((8, 112, channels), jnp.float32),
    ]
    return pl.pallas_call(
        forward_block,
        out_shape=[jax.ShapeDtypeStruct(s, t) for s, t in shapes],
        in_specs=[pl.BlockSpec(memory_space=pltpu.SMEM)]
        + [pl.BlockSpec(memory_space=pltpu.VMEM)] * 3,
        out_specs=[pl.BlockSpec(memory_space=pltpu.VMEM)] * 4,
        scratch_shapes=[
            pltpu.VMEM((18, 128, channels), jnp.float32),
            pltpu.VMEM((16, 128, channels), jnp.float32),
            pltpu.VMEM((8, 112, channels), jnp.float32),
        ],
        compiler_params=pltpu.CompilerParams(vmem_limit_bytes=40 * 1024 * 1024),
        cost_estimate=pl.CostEstimate(
            flops=6 * 10**9, bytes_accessed=4 * 10**6, transcendentals=2 * 10**5
        ),
        name="forward_block",
    )(lat_at, feat_x, conv_near, conv_wide)


def backward_block(lat_ref, wide_ref, attn_ref, cot_ref, nslope_ref, one_ref, feat_ref, near_ref,
                   dil_ref, out_ref, term_ref, wide_s, outer_s, slope_s, one_s, feat_s, total_s,
                   near_s, *, factor):
    channels = wide_ref.shape[2]
    low = jnp.bfloat16
    cols = GROWN

    def transposed(ref, tap):
        return jnp.concatenate([ref[tap, i] for i in range(3)], axis=1)

    wide_s[...] = wide_ref[...].astype(jnp.float32)
    outer_s[...] = cot_ref[...].astype(jnp.float32) + attn_ref[...].astype(jnp.float32)
    slope_s[...] = nslope_ref[...]
    one_s[...] = one_ref[...].astype(jnp.float32)
    feat_s[...] = feat_ref[...].astype(jnp.float32)
    wide_3 = three(wide_s, (8, 4, 0), cols)
    total = jnp.zeros((10 * cols, channels), jnp.float32)
    for tap in range(3):
        at = 8 - 4 * tap
        total += lax.dot_general(
            wide_3[at : at + 10].reshape(10 * cols, 3 * channels), transposed(dil_ref, tap),
            (((1,), (1,)), ((), ())), preferred_element_type=jnp.float32,
        )
    near_total = total.reshape(10, cols, channels) + outer_s[:, 4 : 4 + cols, :]
    near_grad = (near_total * slope_s[:, 8 : 8 + cols, :]).astype(low).astype(jnp.float32)
    near_grad = jnp.where(row_inside(lat_ref, near_grad.shape, 1), near_grad, 0.0)
    for ref, value in ((total_s, near_total), (near_s, near_grad)):
        ref[...] = jnp.zeros_like(ref)
        ref[:, :cols, :] = value
    near_3 = three(near_s, (2, 1, 0), cols)
    total = jnp.zeros((8 * cols, channels), jnp.float32)
    for tap in range(3):
        at = 2 - tap
        total += lax.dot_general(
            near_3[at : at + 8].reshape(8 * cols, 3 * channels), transposed(near_ref, tap),
            (((1,), (1,)), ((), ())), preferred_element_type=jnp.float32,
        )
    feature = (total.reshape(8, cols, channels) + total_s[1:9, 1 : 1 + cols, :]).astype(low)
    out_ref[...] = feature[:, :COLS, :]

    valid = lax.broadcasted_iota(jnp.int32, (8, cols, channels), 1) < COLS
    own_near = jnp.where(valid, near_s[1:9, 1 : 1 + cols, :], 0.0)
    own_near = own_near.astype(low).reshape(8 * cols, channels)
    own_wide = jnp.where(valid, wide_s[5:13, EDGE : EDGE + cols, :], 0.0)
    own_wide = own_wide.astype(low).reshape(8 * cols, channels)
    feat_3 = three(feat_s, (9, 10, 11), cols)
    one_3 = three(one_s, (5, 9, 13), cols)
    long = 3 * channels
    for tap in range(3):
        for left, right, at in (
            (feat_3[4 + tap : 12 + tap], own_near, tap * long),
            (one_3[4 * tap : 4 * tap + 8], own_wide, (3 + tap) * long),
        ):
            term = contract_rows(left.reshape(8 * cols, long), right)
            term_ref[at : at + long, :] = (term * factor).astype(low)


def backward(lat_at, wide_all, attn_near, cot_near, near_slope, hidden_one, feat_x, conv_near,
             conv_wide, factor):
    channels = feat_x.shape[2]
    low = jnp.bfloat16
    shapes = [((8, COLS, channels), low), ((18 * channels, channels), low)]
    grown = [(18, 112), (10, 112), (10, 112), (16, 112), (18, 128), (10, 112), (10, 112)]
    return pl.pallas_call(
        functools.partial(backward_block, factor=factor),
        out_shape=[jax.ShapeDtypeStruct(s, t) for s, t in shapes],
        in_specs=[pl.BlockSpec(memory_space=pltpu.SMEM)]
        + [pl.BlockSpec(memory_space=pltpu.VMEM)] * 8,
        out_specs=[pl.BlockSpec(memory_space=pltpu.VMEM)] * 2,
        scratch_shapes=[pltpu.VMEM(g + (channels,), jnp.float32) for g in grown],
        compiler_params=pltpu.CompilerParams(vmem_limit_bytes=44 * 1024 * 1024),
        cost_estimate=pl.CostEstimate(
            flops=6 * 10**9, bytes_accessed=4 * 10**6, transcendentals=0
        ),
        name="backward_block",
    )(lat_at, wide_all, attn_near, cot_near, near_slope, hidden_one, feat_x, conv_near, conv_wide)


def reduce_all(terms):
    rows, channels = terms.shape
    part = rows // 32
    piece = part * channels // 16
    band = lax.all_to_all(
        terms.reshape(32, part, channels), ("x", "y", "core"), 0, 0, tiled=True
    )
    band = band.astype(jnp.float32).sum(0).astype(jnp.bfloat16).reshape(16, piece)
    band = lax.all_to_all(band, ("zh", "zl"), 0, 0, tiled=True)
    band = band.astype(jnp.float32).sum(0).astype(jnp.bfloat16)
    band = lax.all_to_all(
        jnp.broadcast_to(band[None], (16, piece)), ("zh", "zl"), 0, 0, tiled=True
    ).reshape(part, channels)
    return lax.all_to_all(
        jnp.broadcast_to(band[None], (32, part, channels)), ("x", "y", "core"), 0, 0, tiled=True
    ).reshape(rows, channels)


def on_device(
    features, queries, attn_keys, attn_values, cotangent, conv_near, conv_wide, proj_qkv, proj_out
):
    rows, cols, channels = features.shape
    factor = float(rows * cols * 512) ** (-0.5)
    lat_at = lax.axis_index(LAT_AXES).astype(jnp.int32).reshape(1)
    half_at = lax.axis_index("zh")

    def to_rows(*fields):
        grown = [jnp.pad(f, ((0, 0), (0, GROWN - f.shape[1]), (0, 0))) for f in fields]
        return lax.all_to_all(jnp.concatenate(grown, axis=1), PLANE, 0, 0, tiled=True)

    blank = jnp.zeros((rows, 1, channels), features.dtype)
    low, high = exchange_lon(
        jnp.concatenate([features[:, :10], cotangent[:, :EDGE], blank], axis=1),
        jnp.concatenate([features[:, -10:], cotangent[:, -EDGE:], blank], axis=1),
    )
    low, high, attn_keys, attn_values = lax.optimization_barrier(
        (low, high, attn_keys, attn_values)
    )

    side = channels // 2
    kv_own = to_rows(
        jnp.concatenate([attn_keys[..., :side], attn_values[..., :side]], axis=2),
        jnp.concatenate([attn_values[..., side:], attn_keys[..., side:]], axis=2),
    )

    feat_x = jnp.concatenate(
        [low[:, :10], features, high[:, :10], jnp.zeros((rows, 18, channels), features.dtype)],
        axis=1,
    )
    cot_x = jnp.concatenate(
        [low[:, 10:15], cotangent, high[:, 10:15], jnp.zeros((rows, 28, channels), features.dtype)],
        axis=1,
    )
    low, high = exchange_lat(
        jnp.concatenate([feat_x[-5:], cot_x[-1:]], axis=0),
        jnp.concatenate([feat_x[:5], cot_x[:1]], axis=0),
    )
    low, high, kv_own, queries = lax.optimization_barrier((low, high, kv_own, queries))
    kv_one, kv_two = kv_own[:, :GROWN], kv_own[:, GROWN:]
    far_one = lax.ppermute(kv_one, "zh", SWAP)
    far_two = lax.ppermute(kv_two, "zh", SWAP)
    qc_own = to_rows(queries, cotangent)
    feat_x = jnp.concatenate([low[:5], feat_x, high[:5]], axis=0)
    cot_near = jnp.concatenate([low[5:], cot_x, high[5:]], axis=0)[:, :112]

    hidden_two, hidden_one, near_slope, wide_slope = forward(lat_at, feat_x, conv_near, conv_wide)
    hid_far = lax.ppermute(hidden_two, "zh", SWAP)
    far_one, hidden_two = lax.optimization_barrier((far_one, hidden_two))

    half = HEADS // 2
    first = attention(qc_own, kv_one, far_one, proj_out, (0, half))
    first, kv_two = lax.optimization_barrier((first, kv_two))
    own_part, far_edge, sent, out_term, own_qkv, far_kv = attention(
        qc_own, kv_two, far_two, proj_out, (half, HEADS), first, proj_qkv
    )
    sent, hid_far = lax.optimization_barrier((sent, hid_far))
    hid_rows = to_rows(hidden_two, hid_far)
    from_far = lax.ppermute(sent, "zh", SWAP)
    whole = (own_part + from_far.astype(jnp.float32)).astype(jnp.bfloat16)
    whole = whole.reshape(4, 2, GROWN, channels)
    edge = from_far.reshape(4, 2, GROWN, channels)[:, :, COLS : COLS + EDGE].astype(jnp.float32)
    edge = (edge + far_edge.reshape(4, 2, 8, channels)[:, :, :EDGE]).astype(jnp.bfloat16)
    edge_low, edge_high = edge[:, 0], edge[:, 1]
    left = jnp.where(half_at == 1, edge_high, jnp.roll(edge_high, 1, axis=0))
    right = jnp.where(half_at == 0, edge_low, jnp.roll(edge_low, -1, axis=0))
    left = jnp.stack([left, whole[:, 0, COLS - EDGE : COLS]], axis=1)
    right = jnp.stack([whole[:, 1, :EDGE], right], axis=1)
    blank = jnp.zeros((4, 2, 12, channels), jnp.bfloat16)
    attn_x = jnp.concatenate([left, whole[:, :, :COLS], right, blank], axis=2)
    attn_x = lax.all_to_all(attn_x.reshape(8, 112, channels), PLANE, 0, 0, tiled=True)
    hid_flat = hid_rows[:, :GROWN].reshape(-1, channels)
    far_flat = hid_rows[:, GROWN:].reshape(-1, channels)
    query_term = contract_rows(hid_flat, own_qkv[:, :channels])
    kv_term = contract_rows(hid_flat, own_qkv[:, channels:]) + contract_rows(far_flat, far_kv)

    outer_x = cot_x[:, :112].astype(jnp.float32) + attn_x.astype(jnp.float32)
    wide_x = (outer_x * wide_slope).astype(jnp.bfloat16)
    low, high = exchange_lat(
        jnp.concatenate([wide_x[-5:], attn_x[-1:]], axis=0),
        jnp.concatenate([wide_x[:5], attn_x[:1]], axis=0),
    )
    wide_all = jnp.concatenate([low[:5], wide_x, high[:5]], axis=0)
    attn_near = jnp.concatenate([low[5:], attn_x, high[5:]], axis=0)
    feature_grad, conv_terms = backward(
        lat_at, wide_all, attn_near, cot_near, near_slope, hidden_one, feat_x, conv_near,
        conv_wide, factor,
    )

    others = jnp.concatenate([query_term, kv_term[:, :channels], kv_term[:, channels:], out_term])
    terms = jnp.concatenate([conv_terms, (others * factor).astype(jnp.bfloat16)])
    sums = reduce_all(terms).astype(jnp.float32)
    taps = 9 * channels
    near_sum = sums[:taps].reshape(3, 3, channels, channels)
    wide_sum = sums[taps : 2 * taps].reshape(3, 3, channels, channels)
    qkv_sum = jnp.concatenate(
        [sums[2 * taps + i * channels : 2 * taps + (i + 1) * channels] for i in range(3)], axis=1
    )
    out_sum = sums[2 * taps + 3 * channels :]
    return (feature_grad, near_sum, wide_sum, qkv_sum, out_sum)


def solution(mesh):
    grid = Mesh(mesh.devices.reshape(4, 2, 2, 8, 4), LON_AXES + LAT_AXES)
    field = P(LAT_AXES, LON_AXES, None)
    return jax.shard_map(
        on_device,
        mesh=grid,
        in_specs=(field,) * 5 + (P(),) * 4,
        out_specs=(field, P(), P(), P(), P()),
        check_vma=False,
    )
```

```python
import functools

import jax
import jax.numpy as jnp
from jax import lax
from jax.experimental import pallas as pl
from jax.experimental.pallas import tpu as pltpu
from jax.sharding import Mesh, PartitionSpec as P

HEADS = 8
COLS = 90
GROWN = 96
EDGE = 5
CHUNK = 256
GELU_COEF = 0.7978845608028654
CUBIC_COEF = 0.044715

LON_AXES = ("x", "zh", "core")
LAT_AXES = ("zl", "y")
PLANE = ("x", "core")
SWAP = [(0, 1), (1, 0)]


def gelu_value(pre_act):
    tanh_val = jnp.tanh(GELU_COEF * (pre_act + CUBIC_COEF * pre_act * pre_act * pre_act))
    return 0.5 * pre_act * (1.0 + tanh_val)


def gelu_slope(pre_act):
    tanh_val = jnp.tanh(GELU_COEF * (pre_act + CUBIC_COEF * pre_act * pre_act * pre_act))
    inner_d = GELU_COEF * (1.0 + 3.0 * CUBIC_COEF * pre_act * pre_act)
    return 0.5 * (1.0 + tanh_val) + 0.5 * pre_act * (1.0 - tanh_val * tanh_val) * inner_d


def contract_rows(left, right):
    return lax.dot_general(
        left, right, (((0,), (0,)), ((), ())), preferred_element_type=jnp.float32
    )


def exchange_lon(left, right):
    at_zero = lax.axis_index("core") == 0
    inner = lax.ppermute(jnp.where(at_zero, right, left), "core", SWAP)
    pairs = [(i, (i + 1) % 16 if i % 2 else (i - 1) % 16) for i in range(16)]
    outer = lax.ppermute(jnp.where(at_zero, left, right), LON_AXES, pairs)
    return jnp.where(at_zero, outer, inner), jnp.where(at_zero, inner, outer)


def exchange_lat(bottom, top):
    chain = [(i, i + 1) for i in range(31)]
    low = lax.ppermute(bottom, LAT_AXES, chain)
    high = lax.ppermute(top, LAT_AXES, [(b, a) for a, b in chain])
    return low, high


def attend_rows(*refs, heads, last):
    own_ref, far_ref, proj_ref = refs[:3]
    out_s, keep_s, grad_s, pair_s, value_s, key_g, value_g, query_g, mixed_g = refs[-9:]
    blocks, wide, channels = far_ref.shape
    rows = blocks * wide
    cols = 2 * rows
    pair_at, query_at, cot_at = (wide if last else 0), 2 * wide, 3 * wide
    width = channels // HEADS
    chunk = CHUNK
    low = jnp.bfloat16

    def rows_of(ref, at):
        return ref[:, at : at + wide, :].reshape(rows, channels)

    out_s[...] = lax.dot_general(
        rows_of(own_ref, cot_at), proj_ref[...], (((1,), (1,)), ((), ())),
        preferred_element_type=jnp.float32,
    )
    pair = jnp.concatenate([rows_of(own_ref, pair_at), rows_of(far_ref, 0)], axis=0).astype(jnp.float32)
    pair_s[...] = pair
    value_s[...] = pltpu.roll(pair, channels // 2, 1)
    for ref in (key_g, value_g, query_g, mixed_g):
        ref[...] = jnp.zeros_like(ref)
    lane_k = lax.broadcasted_iota(jnp.int32, (cols, channels), 1)
    filler = lax.broadcasted_iota(jnp.int32, (cols, channels), 0) % wide >= COLS
    lane_q = lax.broadcasted_iota(jnp.int32, (chunk, channels), 1)

    def one_head(head, carry):
        first = (head * width + width) % channels
        here_k = lane_k // width == head
        here_q = lane_q // width == head
        spare = jnp.where((lane_k == first) & filler, -1e30, 0.0)
        keys_h = jnp.where(here_k, pair_s[...], spare).astype(low)
        ones = jnp.where((lane_k == first) | (lane_k == first + 1), 1.0, 0.0)
        values_h = jnp.where(here_k, value_s[...], ones).astype(low)
        spots = [slice(at, at + chunk) for at in range(0, rows, chunk)]
        queries, douts, shares, query_n, dout_n = [], [], [], [], []
        for spot in spots:
            query = rows_of(own_ref, query_at)[spot].astype(jnp.float32) * 0.25
            query_h = jnp.where(here_q, query, jnp.where(lane_q == first, 1.0, 0.0)).astype(low)
            queries.append(jnp.where(here_q, query, 0.0))
            scores = lax.dot_general(
                query_h, keys_h, (((1,), (1,)), ((), ())), preferred_element_type=jnp.float32
            )
            top = jnp.max(scores, axis=1, keepdims=True)
            keep_s[spot, :] = jnp.exp(scores - top).astype(low)
        for spot in spots:
            dout = out_s[spot, :].astype(low).astype(jnp.float32)
            dout = jnp.where(here_q, dout, 0.0)
            mixed = jnp.dot(keep_s[spot, :], values_h, preferred_element_type=jnp.float32)
            total = jnp.sum(jnp.where(lane_q == first, mixed, 0.0), axis=1, keepdims=True)
            share = 1.0 / total
            mixed = jnp.where(here_q, mixed * share, 0.0)
            mixed_g[spot, :] += mixed
            delta = jnp.sum(dout * mixed, axis=1, keepdims=True)
            high = delta.astype(low).astype(jnp.float32)
            douts.append(
                jnp.where(
                    lane_q == first, -high, jnp.where(lane_q == first + 1, high - delta, dout)
                ).astype(low)
            )
            shares.append(share)
            dout_n.append((dout * share).astype(low))
        value_g[...] += lax.dot_general(
            keep_s[...], jnp.concatenate(dout_n, axis=0), (((0,), (0,)), ((), ())),
            preferred_element_type=jnp.float32,
        )
        for spot, dout_x in zip(spots, douts):
            prob_grad = lax.dot_general(
                dout_x, values_h, (((1,), (1,)), ((), ())), preferred_element_type=jnp.float32
            )
            grad_s[spot, :] = keep_s[spot, :] * prob_grad.astype(low)
        for spot, query, share in zip(spots, queries, shares):
            query_g[spot, :] += (
                jnp.dot(grad_s[spot, :], keys_h, preferred_element_type=jnp.float32)
                * (0.25 * share)
            )
            query_n.append((query * share).astype(low))
        key_g[...] += lax.dot_general(
            grad_s[...], jnp.concatenate(query_n, axis=0), (((0,), (0,)), ((), ())),
            preferred_element_type=jnp.float32,
        )
        return carry

    lax.fori_loop(heads[0], heads[1], one_head, 0)
    mixed = mixed_g[...].astype(low)
    grads = [query_g[...].astype(low)]
    grads += [ref[:rows, :].astype(low) for ref in (key_g, value_g)]
    aways = [ref[rows:, :].astype(low) for ref in (key_g, value_g)]
    if not last:
        mixed_ref, grad_ref, away_ref = refs[3:6]
        mixed_ref[...] = mixed
        grad_ref[...] = jnp.concatenate(grads, axis=1)
        away_ref[...] = jnp.concatenate(aways, axis=1)
        return
    mixed_ref, grad_ref, away_ref, qkv_ref = refs[3:7]
    part_ref, apart_ref, send_ref, term_ref, all_ref, far_all_ref = refs[7:13]
    own = jnp.concatenate(grads, axis=1) + grad_ref[...]
    far = jnp.concatenate(aways, axis=1) + away_ref[...]
    all_ref[...] = own
    far_all_ref[...] = far
    own_part = lax.dot_general(
        own, qkv_ref[...], (((1,), (1,)), ((), ())), preferred_element_type=jnp.float32
    )
    far_part = lax.dot_general(
        far, qkv_ref[:, channels:], (((1,), (1,)), ((), ())), preferred_element_type=jnp.float32
    )
    part_ref[...] = own_part.reshape(blocks, wide, channels)
    apart_ref[...] = jnp.zeros_like(apart_ref)
    query_g[...] = far_part
    for block in range(blocks):
        edge = 0 if block % 2 == 0 else COLS - EDGE
        at = block * wide + COLS
        apart_ref[block, :EDGE, :] = query_g[at - COLS + edge : at - COLS + edge + EDGE, :]
        query_g[at : at + EDGE, :] = part_ref[block, edge : edge + EDGE, :]
    send_ref[...] = query_g[...].astype(low).reshape(blocks, wide, channels)
    term_ref[...] = contract_rows(mixed + mixed_ref[...], rows_of(own_ref, cot_at))


def attention(own_rows, kv_far, proj_out, heads, first=None, proj_qkv=None):
    blocks, wide, channels = kv_far.shape
    rows = blocks * wide
    low = jnp.bfloat16
    operands = [own_rows, kv_far, proj_out]
    shapes = [((rows, channels), low), ((rows, 3 * channels), low), ((rows, 2 * channels), low)]
    if first is not None:
        operands += [*first, proj_qkv]
        shapes = [
            ((blocks, wide, channels), jnp.float32),
            ((blocks, 8, channels), jnp.float32),
            ((blocks, wide, channels), low),
            ((channels, channels), jnp.float32),
        ] + shapes[1:]
    return pl.pallas_call(
        functools.partial(attend_rows, heads=heads, last=first is not None),
        out_shape=[jax.ShapeDtypeStruct(s, t) for s, t in shapes],
        in_specs=[pl.BlockSpec(memory_space=pltpu.VMEM)] * len(operands),
        out_specs=[pl.BlockSpec(memory_space=pltpu.VMEM)] * len(shapes),
        scratch_shapes=[
            pltpu.VMEM((rows, channels), jnp.float32),
            pltpu.VMEM((rows, 2 * rows), low),
            pltpu.VMEM((rows, 2 * rows), low),
            pltpu.VMEM((2 * rows, channels), jnp.float32),
            pltpu.VMEM((2 * rows, channels), jnp.float32),
            pltpu.VMEM((2 * rows, channels), jnp.float32),
            pltpu.VMEM((2 * rows, channels), jnp.float32),
            pltpu.VMEM((rows, channels), jnp.float32),
            pltpu.VMEM((rows, channels), jnp.float32),
        ],
        compiler_params=pltpu.CompilerParams(vmem_limit_bytes=48 * 1024 * 1024),
        cost_estimate=pl.CostEstimate(
            flops=12 * rows * 2 * rows * channels * (heads[1] - heads[0]),
            bytes_accessed=16 * rows * channels,
            transcendentals=(heads[1] - heads[0]) * rows * 2 * rows,
        ),
        name="attend_rows",
    )(*operands)


def row_inside(lat_ref, shape, width):
    at = lat_ref[0] * 8 + lax.broadcasted_iota(jnp.int32, shape, 0) - width
    return (at >= 0) & (at < 256)


def three(ref, starts, count):
    return jnp.concatenate(
        [ref[:, at : at + count, :].astype(jnp.bfloat16) for at in starts], axis=2
    )


def forward_block(lat_ref, feat_ref, near_ref, wide_ref, two_ref, one_ref, nslope_ref, wslope_ref,
                  feat_s, one_s, wide_s):
    channels = feat_ref.shape[2]
    low = jnp.bfloat16
    cols = 112
    feat_s[...] = feat_ref[...].astype(jnp.float32)
    feat_3 = three(feat_s, (0, 1, 2), cols)
    total = jnp.zeros((16 * cols, channels), jnp.float32)
    for tap in range(3):
        weight = near_ref[tap].reshape(3 * channels, channels)
        total += jnp.dot(
            feat_3[tap : tap + 16].reshape(16 * cols, 3 * channels), weight,
            preferred_element_type=jnp.float32,
        )
    pre_near = total.reshape(16, cols, channels)
    nslope_ref[...] = gelu_slope(pre_near[3:13])
    one = (feat_s[1:17, 1 : 1 + cols, :] + gelu_value(pre_near)).astype(low)
    one = jnp.where(row_inside(lat_ref, one.shape, 4), one.astype(jnp.float32), 0.0)
    one_ref[...] = one.astype(low)
    one_s[...] = jnp.zeros_like(one_s)
    one_s[:, :cols, :] = one
    one_3 = three(one_s, (0, 4, 8), cols)
    total = jnp.zeros((8 * cols, channels), jnp.float32)
    for tap in range(3):
        weight = wide_ref[tap].reshape(3 * channels, channels)
        total += jnp.dot(
            one_3[4 * tap : 4 * tap + 8].reshape(8 * cols, 3 * channels), weight,
            preferred_element_type=jnp.float32,
        )
    pre_wide = total.reshape(8, cols, channels)
    wslope_ref[...] = gelu_slope(pre_wide)
    wide_s[...] = gelu_value(pre_wide)
    two = one_s[4:12, 9 : 9 + GROWN, :] + wide_s[:, EDGE : EDGE + GROWN, :]
    valid = lax.broadcasted_iota(jnp.int32, two.shape, 1) < COLS
    two_ref[...] = jnp.where(valid, two, 0.0).astype(low)


def forward(lat_at, feat_x, conv_near, conv_wide):
    channels = feat_x.shape[2]
    shapes = [
        ((8, GROWN, channels), jnp.bfloat16),
        ((16, 112, channels), jnp.bfloat16),
        ((10, 112, channels), jnp.float32),
        ((8, 112, channels), jnp.float32),
    ]
    return pl.pallas_call(
        forward_block,
        out_shape=[jax.ShapeDtypeStruct(s, t) for s, t in shapes],
        in_specs=[pl.BlockSpec(memory_space=pltpu.SMEM)]
        + [pl.BlockSpec(memory_space=pltpu.VMEM)] * 3,
        out_specs=[pl.BlockSpec(memory_space=pltpu.VMEM)] * 4,
        scratch_shapes=[
            pltpu.VMEM((18, 128, channels), jnp.float32),
            pltpu.VMEM((16, 128, channels), jnp.float32),
            pltpu.VMEM((8, 112, channels), jnp.float32),
        ],
        compiler_params=pltpu.CompilerParams(vmem_limit_bytes=40 * 1024 * 1024),
        cost_estimate=pl.CostEstimate(
            flops=6 * 10**9, bytes_accessed=4 * 10**6, transcendentals=2 * 10**5
        ),
        name="forward_block",
    )(lat_at, feat_x, conv_near, conv_wide)


def backward_block(lat_ref, wide_ref, attn_ref, cot_ref, nslope_ref, one_ref, feat_ref, near_ref,
                   dil_ref, out_ref, term_ref, wide_s, outer_s, slope_s, one_s, feat_s, total_s,
                   near_s, *, factor):
    channels = wide_ref.shape[2]
    low = jnp.bfloat16
    cols = GROWN

    def transposed(ref, tap):
        return jnp.concatenate([ref[tap, i] for i in range(3)], axis=1)

    wide_s[...] = wide_ref[...].astype(jnp.float32)
    outer_s[...] = cot_ref[...].astype(jnp.float32) + attn_ref[...].astype(jnp.float32)
    slope_s[...] = nslope_ref[...]
    one_s[...] = one_ref[...].astype(jnp.float32)
    feat_s[...] = feat_ref[...].astype(jnp.float32)
    wide_3 = three(wide_s, (8, 4, 0), cols)
    total = jnp.zeros((10 * cols, channels), jnp.float32)
    for tap in range(3):
        at = 8 - 4 * tap
        total += lax.dot_general(
            wide_3[at : at + 10].reshape(10 * cols, 3 * channels), transposed(dil_ref, tap),
            (((1,), (1,)), ((), ())), preferred_element_type=jnp.float32,
        )
    near_total = total.reshape(10, cols, channels) + outer_s[:, 4 : 4 + cols, :]
    near_grad = (near_total * slope_s[:, 8 : 8 + cols, :]).astype(low).astype(jnp.float32)
    near_grad = jnp.where(row_inside(lat_ref, near_grad.shape, 1), near_grad, 0.0)
    for ref, value in ((total_s, near_total), (near_s, near_grad)):
        ref[...] = jnp.zeros_like(ref)
        ref[:, :cols, :] = value
    near_3 = three(near_s, (2, 1, 0), cols)
    total = jnp.zeros((8 * cols, channels), jnp.float32)
    for tap in range(3):
        at = 2 - tap
        total += lax.dot_general(
            near_3[at : at + 8].reshape(8 * cols, 3 * channels), transposed(near_ref, tap),
            (((1,), (1,)), ((), ())), preferred_element_type=jnp.float32,
        )
    feature = (total.reshape(8, cols, channels) + total_s[1:9, 1 : 1 + cols, :]).astype(low)
    out_ref[...] = feature[:, :COLS, :]

    valid = lax.broadcasted_iota(jnp.int32, (8, cols, channels), 1) < COLS
    own_near = jnp.where(valid, near_s[1:9, 1 : 1 + cols, :], 0.0)
    own_near = own_near.astype(low).reshape(8 * cols, channels)
    own_wide = jnp.where(valid, wide_s[5:13, EDGE : EDGE + cols, :], 0.0)
    own_wide = own_wide.astype(low).reshape(8 * cols, channels)
    feat_3 = three(feat_s, (9, 10, 11), cols)
    one_3 = three(one_s, (5, 9, 13), cols)
    long = 3 * channels
    for tap in range(3):
        for left, right, at in (
            (feat_3[4 + tap : 12 + tap], own_near, tap * long),
            (one_3[4 * tap : 4 * tap + 8], own_wide, (3 + tap) * long),
        ):
            term = contract_rows(left.reshape(8 * cols, long), right)
            term_ref[at : at + long, :] = (term * factor).astype(low)


def backward(lat_at, wide_all, attn_near, cot_near, near_slope, hidden_one, feat_x, conv_near,
             conv_wide, factor):
    channels = feat_x.shape[2]
    low = jnp.bfloat16
    shapes = [((8, COLS, channels), low), ((18 * channels, channels), low)]
    grown = [(18, 112), (10, 112), (10, 112), (16, 112), (18, 128), (10, 112), (10, 112)]
    return pl.pallas_call(
        functools.partial(backward_block, factor=factor),
        out_shape=[jax.ShapeDtypeStruct(s, t) for s, t in shapes],
        in_specs=[pl.BlockSpec(memory_space=pltpu.SMEM)]
        + [pl.BlockSpec(memory_space=pltpu.VMEM)] * 8,
        out_specs=[pl.BlockSpec(memory_space=pltpu.VMEM)] * 2,
        scratch_shapes=[pltpu.VMEM(g + (channels,), jnp.float32) for g in grown],
        compiler_params=pltpu.CompilerParams(vmem_limit_bytes=44 * 1024 * 1024),
        cost_estimate=pl.CostEstimate(
            flops=6 * 10**9, bytes_accessed=4 * 10**6, transcendentals=0
        ),
        name="backward_block",
    )(lat_at, wide_all, attn_near, cot_near, near_slope, hidden_one, feat_x, conv_near, conv_wide)


def reduce_all(terms):
    rows, channels = terms.shape
    part = rows // 32
    piece = part * channels // 16
    band = lax.all_to_all(
        terms.reshape(32, part, channels), ("x", "y", "core"), 0, 0, tiled=True
    )
    band = band.astype(jnp.float32).sum(0).astype(jnp.bfloat16).reshape(16, piece)
    band = lax.all_to_all(band, ("zh", "zl"), 0, 0, tiled=True)
    band = band.astype(jnp.float32).sum(0).astype(jnp.bfloat16)
    band = lax.all_to_all(
        jnp.broadcast_to(band[None], (16, piece)), ("zh", "zl"), 0, 0, tiled=True
    ).reshape(part, channels)
    return lax.all_to_all(
        jnp.broadcast_to(band[None], (32, part, channels)), ("x", "y", "core"), 0, 0, tiled=True
    ).reshape(rows, channels)


def on_device(
    features, queries, attn_keys, attn_values, cotangent, conv_near, conv_wide, proj_qkv, proj_out
):
    rows, cols, channels = features.shape
    factor = float(rows * cols * 512) ** (-0.5)
    lat_at = lax.axis_index(LAT_AXES).astype(jnp.int32).reshape(1)
    half_at = lax.axis_index("zh")

    def to_rows(*fields):
        grown = [jnp.pad(f, ((0, 0), (0, GROWN - f.shape[1]), (0, 0))) for f in fields]
        return lax.all_to_all(jnp.concatenate(grown, axis=1), PLANE, 0, 0, tiled=True)

    blank = jnp.zeros((rows, 1, channels), features.dtype)
    low, high = exchange_lon(
        jnp.concatenate([features[:, :10], cotangent[:, :EDGE], blank], axis=1),
        jnp.concatenate([features[:, -10:], cotangent[:, -EDGE:], blank], axis=1),
    )
    low, high, attn_keys, attn_values = lax.optimization_barrier(
        (low, high, attn_keys, attn_values)
    )

    side = channels // 2
    own_rows = to_rows(
        jnp.concatenate([attn_keys[..., :side], attn_values[..., :side]], axis=2),
        jnp.concatenate([attn_values[..., side:], attn_keys[..., side:]], axis=2),
        queries,
        cotangent,
    )

    feat_x = jnp.concatenate(
        [low[:, :10], features, high[:, :10], jnp.zeros((rows, 18, channels), features.dtype)],
        axis=1,
    )
    cot_x = jnp.concatenate(
        [low[:, 10:15], cotangent, high[:, 10:15], jnp.zeros((rows, 28, channels), features.dtype)],
        axis=1,
    )
    low, high = exchange_lat(
        jnp.concatenate([feat_x[-5:], cot_x[-1:]], axis=0),
        jnp.concatenate([feat_x[:5], cot_x[:1]], axis=0),
    )
    low, high, own_rows = lax.optimization_barrier((low, high, own_rows))
    far_one = lax.ppermute(own_rows[:, :GROWN], "zh", SWAP)
    far_two = lax.ppermute(own_rows[:, GROWN : 2 * GROWN], "zh", SWAP)
    feat_x = jnp.concatenate([low[:5], feat_x, high[:5]], axis=0)
    cot_near = jnp.concatenate([low[5:], cot_x, high[5:]], axis=0)[:, :112]

    hidden_two, hidden_one, near_slope, wide_slope = forward(lat_at, feat_x, conv_near, conv_wide)
    hid_far = lax.ppermute(hidden_two, "zh", SWAP)
    far_one, hidden_two = lax.optimization_barrier((far_one, hidden_two))

    half = HEADS // 2
    first = attention(own_rows, far_one, proj_out, (0, half))
    first, proj_out = lax.optimization_barrier((first, proj_out))
    own_part, far_edge, sent, out_term, own_qkv, far_kv = attention(
        own_rows, far_two, proj_out, (half, HEADS), first, proj_qkv
    )
    sent, hid_far = lax.optimization_barrier((sent, hid_far))
    hid_rows = to_rows(hidden_two, hid_far)
    from_far = lax.ppermute(sent, "zh", SWAP)
    whole = (own_part + from_far.astype(jnp.float32)).astype(jnp.bfloat16)
    whole = whole.reshape(4, 2, GROWN, channels)
    edge = from_far.reshape(4, 2, GROWN, channels)[:, :, COLS : COLS + EDGE].astype(jnp.float32)
    edge = (edge + far_edge.reshape(4, 2, 8, channels)[:, :, :EDGE]).astype(jnp.bfloat16)
    edge_low, edge_high = edge[:, 0], edge[:, 1]
    left = jnp.where(half_at == 1, edge_high, jnp.roll(edge_high, 1, axis=0))
    right = jnp.where(half_at == 0, edge_low, jnp.roll(edge_low, -1, axis=0))
    left = jnp.stack([left, whole[:, 0, COLS - EDGE : COLS]], axis=1)
    right = jnp.stack([whole[:, 1, :EDGE], right], axis=1)
    blank = jnp.zeros((4, 2, 12, channels), jnp.bfloat16)
    attn_x = jnp.concatenate([left, whole[:, :, :COLS], right, blank], axis=2)
    attn_x = lax.all_to_all(attn_x.reshape(8, 112, channels), PLANE, 0, 0, tiled=True)
    hid_flat = hid_rows[:, :GROWN].reshape(-1, channels)
    far_flat = hid_rows[:, GROWN:].reshape(-1, channels)
    query_term = contract_rows(hid_flat, own_qkv[:, :channels])
    kv_term = contract_rows(hid_flat, own_qkv[:, channels:]) + contract_rows(far_flat, far_kv)

    outer_x = cot_x[:, :112].astype(jnp.float32) + attn_x.astype(jnp.float32)
    wide_x = (outer_x * wide_slope).astype(jnp.bfloat16)
    low, high = exchange_lat(
        jnp.concatenate([wide_x[-5:], attn_x[-1:]], axis=0),
        jnp.concatenate([wide_x[:5], attn_x[:1]], axis=0),
    )
    wide_all = jnp.concatenate([low[:5], wide_x, high[:5]], axis=0)
    attn_near = jnp.concatenate([low[5:], attn_x, high[5:]], axis=0)
    feature_grad, conv_terms = backward(
        lat_at, wide_all, attn_near, cot_near, near_slope, hidden_one, feat_x, conv_near,
        conv_wide, factor,
    )

    others = jnp.concatenate([query_term, kv_term[:, :channels], kv_term[:, channels:], out_term])
    terms = jnp.concatenate([conv_terms, (others * factor).astype(jnp.bfloat16)])
    sums = reduce_all(terms).astype(jnp.float32)
    taps = 9 * channels
    near_sum = sums[:taps].reshape(3, 3, channels, channels)
    wide_sum = sums[taps : 2 * taps].reshape(3, 3, channels, channels)
    qkv_sum = jnp.concatenate(
        [sums[2 * taps + i * channels : 2 * taps + (i + 1) * channels] for i in range(3)], axis=1
    )
    out_sum = sums[2 * taps + 3 * channels :]
    return (feature_grad, near_sum, wide_sum, qkv_sum, out_sum)


def solution(mesh):
    grid = Mesh(mesh.devices.reshape(4, 2, 2, 8, 4), LON_AXES + LAT_AXES)
    field = P(LAT_AXES, LON_AXES, None)
    return jax.shard_map(
        on_device,
        mesh=grid,
        in_specs=(field,) * 5 + (P(),) * 4,
        out_specs=(field, P(), P(), P(), P()),
        check_vma=False,
    )
```

```python
import functools

import jax
import jax.numpy as jnp
from jax import lax
from jax.experimental import pallas as pl
from jax.experimental.pallas import tpu as pltpu
from jax.sharding import Mesh, PartitionSpec as P

HEADS = 8
COLS = 90
GROWN = 96
EDGE = 5
CHUNK = 256
GELU_COEF = 0.7978845608028654
CUBIC_COEF = 0.044715

LON_AXES = ("x", "zh", "core")
LAT_AXES = ("zl", "y")
PLANE = ("x", "core")
SWAP = [(0, 1), (1, 0)]


def gelu_value(pre_act):
    tanh_val = jnp.tanh(GELU_COEF * (pre_act + CUBIC_COEF * pre_act * pre_act * pre_act))
    return 0.5 * pre_act * (1.0 + tanh_val)


def gelu_slope(pre_act):
    tanh_val = jnp.tanh(GELU_COEF * (pre_act + CUBIC_COEF * pre_act * pre_act * pre_act))
    inner_d = GELU_COEF * (1.0 + 3.0 * CUBIC_COEF * pre_act * pre_act)
    return 0.5 * (1.0 + tanh_val) + 0.5 * pre_act * (1.0 - tanh_val * tanh_val) * inner_d


def contract_rows(left, right):
    return lax.dot_general(
        left, right, (((0,), (0,)), ((), ())), preferred_element_type=jnp.float32
    )


def exchange_lon(left, right):
    at_zero = lax.axis_index("core") == 0
    inner = lax.ppermute(jnp.where(at_zero, right, left), "core", SWAP)
    pairs = [(i, (i + 1) % 16 if i % 2 else (i - 1) % 16) for i in range(16)]
    outer = lax.ppermute(jnp.where(at_zero, left, right), LON_AXES, pairs)
    return jnp.where(at_zero, outer, inner), jnp.where(at_zero, inner, outer)


def exchange_lat(bottom, top):
    chain = [(i, i + 1) for i in range(31)]
    low = lax.ppermute(bottom, LAT_AXES, chain)
    high = lax.ppermute(top, LAT_AXES, [(b, a) for a, b in chain])
    return low, high


def attend_rows(*refs, heads, last):
    own_ref, far_ref, proj_ref = refs[:3]
    out_s, keep_s, grad_s, pair_s, value_s, key_g, value_g, query_g, mixed_g = refs[-9:]
    blocks, wide, channels = far_ref.shape
    rows = blocks * wide
    cols = 2 * rows
    pair_at, query_at, cot_at = (wide if last else 0), 2 * wide, 3 * wide
    width = channels // HEADS
    chunk = CHUNK
    low = jnp.bfloat16

    def rows_of(ref, at):
        return ref[:, at : at + wide, :].reshape(rows, channels)

    out_s[...] = lax.dot_general(
        rows_of(own_ref, cot_at), proj_ref[...], (((1,), (1,)), ((), ())),
        preferred_element_type=jnp.float32,
    )
    pair = jnp.concatenate([rows_of(own_ref, pair_at), rows_of(far_ref, 0)], axis=0).astype(jnp.float32)
    pair_s[...] = pair
    value_s[...] = pltpu.roll(pair, channels // 2, 1)
    for ref in (key_g, value_g, query_g, mixed_g):
        ref[...] = jnp.zeros_like(ref)
    lane_k = lax.broadcasted_iota(jnp.int32, (cols, channels), 1)
    filler = lax.broadcasted_iota(jnp.int32, (cols, channels), 0) % wide >= COLS
    lane_q = lax.broadcasted_iota(jnp.int32, (chunk, channels), 1)

    def one_head(head, carry):
        first = (head * width + width) % channels
        here_k = lane_k // width == head
        here_q = lane_q // width == head
        spare = jnp.where((lane_k == first) & filler, -1e30, 0.0)
        keys_h = jnp.where(here_k, pair_s[...], spare).astype(low)
        ones = jnp.where((lane_k == first) | (lane_k == first + 1), 1.0, 0.0)
        values_h = jnp.where(here_k, value_s[...], ones).astype(low)
        spots = [slice(at, at + chunk) for at in range(0, rows, chunk)]
        queries, douts, shares, query_n, dout_n = [], [], [], [], []
        for spot in spots:
            query = rows_of(own_ref, query_at)[spot].astype(jnp.float32) * 0.25
            query_h = jnp.where(here_q, query, jnp.where(lane_q == first, 1.0, 0.0)).astype(low)
            queries.append(jnp.where(here_q, query, 0.0))
            scores = lax.dot_general(
                query_h, keys_h, (((1,), (1,)), ((), ())), preferred_element_type=jnp.float32
            )
            top = jnp.max(scores, axis=1, keepdims=True)
            keep_s[spot, :] = jnp.exp(scores - top).astype(low)
        for spot in spots:
            dout = out_s[spot, :].astype(low).astype(jnp.float32)
            dout = jnp.where(here_q, dout, 0.0)
            mixed = jnp.dot(keep_s[spot, :], values_h, preferred_element_type=jnp.float32)
            total = jnp.sum(jnp.where(lane_q == first, mixed, 0.0), axis=1, keepdims=True)
            share = 1.0 / total
            mixed = jnp.where(here_q, mixed * share, 0.0)
            mixed_g[spot, :] += mixed
            delta = jnp.sum(dout * mixed, axis=1, keepdims=True)
            high = delta.astype(low).astype(jnp.float32)
            douts.append(
                jnp.where(
                    lane_q == first, -high, jnp.where(lane_q == first + 1, high - delta, dout)
                ).astype(low)
            )
            shares.append(share)
            dout_n.append((dout * share).astype(low))
        value_g[...] += lax.dot_general(
            keep_s[...], jnp.concatenate(dout_n, axis=0), (((0,), (0,)), ((), ())),
            preferred_element_type=jnp.float32,
        )
        for spot, dout_x in zip(spots, douts):
            prob_grad = lax.dot_general(
                dout_x, values_h, (((1,), (1,)), ((), ())), preferred_element_type=jnp.float32
            )
            grad_s[spot, :] = keep_s[spot, :] * prob_grad.astype(low)
        for spot, query, share in zip(spots, queries, shares):
            query_g[spot, :] += (
                jnp.dot(grad_s[spot, :], keys_h, preferred_element_type=jnp.float32)
                * (0.25 * share)
            )
            query_n.append((query * share).astype(low))
        key_g[...] += lax.dot_general(
            grad_s[...], jnp.concatenate(query_n, axis=0), (((0,), (0,)), ((), ())),
            preferred_element_type=jnp.float32,
        )
        return carry

    lax.fori_loop(heads[0], heads[1], one_head, 0)
    mixed = mixed_g[...].astype(low)
    grads = [query_g[...].astype(low)]
    grads += [ref[:rows, :].astype(low) for ref in (key_g, value_g)]
    aways = [ref[rows:, :].astype(low) for ref in (key_g, value_g)]
    if not last:
        mixed_ref, grad_ref, away_ref = refs[3:6]
        mixed_ref[...] = mixed
        grad_ref[...] = jnp.concatenate(grads, axis=1)
        away_ref[...] = jnp.concatenate(aways, axis=1)
        return
    mixed_ref, grad_ref, away_ref, qkv_ref = refs[3:7]
    part_ref, apart_ref, send_ref, term_ref, all_ref, far_all_ref = refs[7:13]
    own = jnp.concatenate(grads, axis=1) + grad_ref[...]
    far = jnp.concatenate(aways, axis=1) + away_ref[...]
    all_ref[...] = own
    far_all_ref[...] = far
    own_part = lax.dot_general(
        own, qkv_ref[...], (((1,), (1,)), ((), ())), preferred_element_type=jnp.float32
    )
    far_part = lax.dot_general(
        far, qkv_ref[:, channels:], (((1,), (1,)), ((), ())), preferred_element_type=jnp.float32
    )
    part_ref[...] = own_part.reshape(blocks, wide, channels)
    apart_ref[...] = jnp.zeros_like(apart_ref)
    query_g[...] = far_part
    for block in range(blocks):
        edge = 0 if block % 2 == 0 else COLS - EDGE
        at = block * wide + COLS
        apart_ref[block, :EDGE, :] = query_g[at - COLS + edge : at - COLS + edge + EDGE, :]
        query_g[at : at + EDGE, :] = part_ref[block, edge : edge + EDGE, :]
    send_ref[...] = query_g[...].astype(low).reshape(blocks, wide, channels)
    term_ref[...] = contract_rows(mixed + mixed_ref[...], rows_of(own_ref, cot_at))


def attention(own_rows, kv_far, proj_out, heads, first=None, proj_qkv=None):
    blocks, wide, channels = kv_far.shape
    rows = blocks * wide
    low = jnp.bfloat16
    operands = [own_rows, kv_far, proj_out]
    shapes = [((rows, channels), low), ((rows, 3 * channels), low), ((rows, 2 * channels), low)]
    if first is not None:
        operands += [*first, proj_qkv]
        shapes = [
            ((blocks, wide, channels), jnp.float32),
            ((blocks, 8, channels), jnp.float32),
            ((blocks, wide, channels), low),
            ((channels, channels), jnp.float32),
        ] + shapes[1:]
    return pl.pallas_call(
        functools.partial(attend_rows, heads=heads, last=first is not None),
        out_shape=[jax.ShapeDtypeStruct(s, t) for s, t in shapes],
        in_specs=[pl.BlockSpec(memory_space=pltpu.VMEM)] * len(operands),
        out_specs=[pl.BlockSpec(memory_space=pltpu.VMEM)] * len(shapes),
        scratch_shapes=[
            pltpu.VMEM((rows, channels), jnp.float32),
            pltpu.VMEM((rows, 2 * rows), low),
            pltpu.VMEM((rows, 2 * rows), low),
            pltpu.VMEM((2 * rows, channels), jnp.float32),
            pltpu.VMEM((2 * rows, channels), jnp.float32),
            pltpu.VMEM((2 * rows, channels), jnp.float32),
            pltpu.VMEM((2 * rows, channels), jnp.float32),
            pltpu.VMEM((rows, channels), jnp.float32),
            pltpu.VMEM((rows, channels), jnp.float32),
        ],
        compiler_params=pltpu.CompilerParams(vmem_limit_bytes=48 * 1024 * 1024),
        cost_estimate=pl.CostEstimate(
            flops=12 * rows * 2 * rows * channels * (heads[1] - heads[0]),
            bytes_accessed=16 * rows * channels,
            transcendentals=(heads[1] - heads[0]) * rows * 2 * rows,
        ),
        name="attend_rows",
    )(*operands)


def row_inside(lat_ref, shape, width):
    at = lat_ref[0] * 8 + lax.broadcasted_iota(jnp.int32, shape, 0) - width
    return (at >= 0) & (at < 256)


def three(ref, starts, count):
    return jnp.concatenate(
        [ref[:, at : at + count, :].astype(jnp.bfloat16) for at in starts], axis=2
    )


def forward_block(lat_ref, feat_ref, near_ref, wide_ref, two_ref, one_ref, nslope_ref, wslope_ref,
                  feat_s, one_s, wide_s):
    channels = feat_ref.shape[2]
    low = jnp.bfloat16
    cols = 112
    feat_s[...] = feat_ref[...].astype(jnp.float32)
    feat_3 = three(feat_s, (0, 1, 2), cols)
    total = jnp.zeros((16 * cols, channels), jnp.float32)
    for tap in range(3):
        weight = near_ref[tap].reshape(3 * channels, channels)
        total += jnp.dot(
            feat_3[tap : tap + 16].reshape(16 * cols, 3 * channels), weight,
            preferred_element_type=jnp.float32,
        )
    pre_near = total.reshape(16, cols, channels)
    nslope_ref[...] = gelu_slope(pre_near[3:13])
    one = (feat_s[1:17, 1 : 1 + cols, :] + gelu_value(pre_near)).astype(low)
    one = jnp.where(row_inside(lat_ref, one.shape, 4), one.astype(jnp.float32), 0.0)
    one_ref[...] = one.astype(low)
    one_s[...] = jnp.zeros_like(one_s)
    one_s[:, :cols, :] = one
    one_3 = three(one_s, (0, 4, 8), cols)
    total = jnp.zeros((8 * cols, channels), jnp.float32)
    for tap in range(3):
        weight = wide_ref[tap].reshape(3 * channels, channels)
        total += jnp.dot(
            one_3[4 * tap : 4 * tap + 8].reshape(8 * cols, 3 * channels), weight,
            preferred_element_type=jnp.float32,
        )
    pre_wide = total.reshape(8, cols, channels)
    wslope_ref[...] = gelu_slope(pre_wide)
    wide_s[...] = gelu_value(pre_wide)
    two = one_s[4:12, 9 : 9 + GROWN, :] + wide_s[:, EDGE : EDGE + GROWN, :]
    valid = lax.broadcasted_iota(jnp.int32, two.shape, 1) < COLS
    two_ref[...] = jnp.where(valid, two, 0.0).astype(low)


def forward(lat_at, feat_x, conv_near, conv_wide):
    channels = feat_x.shape[2]
    shapes = [
        ((8, GROWN, channels), jnp.bfloat16),
        ((16, 112, channels), jnp.bfloat16),
        ((10, 112, channels), jnp.float32),
        ((8, 112, channels), jnp.float32),
    ]
    return pl.pallas_call(
        forward_block,
        out_shape=[jax.ShapeDtypeStruct(s, t) for s, t in shapes],
        in_specs=[pl.BlockSpec(memory_space=pltpu.SMEM)]
        + [pl.BlockSpec(memory_space=pltpu.VMEM)] * 3,
        out_specs=[pl.BlockSpec(memory_space=pltpu.VMEM)] * 4,
        scratch_shapes=[
            pltpu.VMEM((18, 128, channels), jnp.float32),
            pltpu.VMEM((16, 128, channels), jnp.float32),
            pltpu.VMEM((8, 112, channels), jnp.float32),
        ],
        compiler_params=pltpu.CompilerParams(vmem_limit_bytes=40 * 1024 * 1024),
        cost_estimate=pl.CostEstimate(
            flops=6 * 10**9, bytes_accessed=4 * 10**6, transcendentals=2 * 10**5
        ),
        name="forward_block",
    )(lat_at, feat_x, conv_near, conv_wide)


def backward_block(lat_ref, wide_ref, attn_ref, cot_ref, nslope_ref, one_ref, feat_ref, near_ref,
                   dil_ref, out_ref, term_ref, wide_s, outer_s, slope_s, one_s, feat_s, total_s,
                   near_s, *, factor):
    channels = wide_ref.shape[2]
    low = jnp.bfloat16
    cols = GROWN

    def transposed(ref, tap):
        return jnp.concatenate([ref[tap, i] for i in range(3)], axis=1)

    wide_s[...] = wide_ref[...].astype(jnp.float32)
    outer_s[...] = cot_ref[...].astype(jnp.float32) + attn_ref[...].astype(jnp.float32)
    slope_s[...] = nslope_ref[...]
    one_s[...] = one_ref[...].astype(jnp.float32)
    feat_s[...] = feat_ref[...].astype(jnp.float32)
    wide_3 = three(wide_s, (8, 4, 0), cols)
    total = jnp.zeros((10 * cols, channels), jnp.float32)
    for tap in range(3):
        at = 8 - 4 * tap
        total += lax.dot_general(
            wide_3[at : at + 10].reshape(10 * cols, 3 * channels), transposed(dil_ref, tap),
            (((1,), (1,)), ((), ())), preferred_element_type=jnp.float32,
        )
    near_total = total.reshape(10, cols, channels) + outer_s[:, 4 : 4 + cols, :]
    near_grad = (near_total * slope_s[:, 8 : 8 + cols, :]).astype(low).astype(jnp.float32)
    near_grad = jnp.where(row_inside(lat_ref, near_grad.shape, 1), near_grad, 0.0)
    for ref, value in ((total_s, near_total), (near_s, near_grad)):
        ref[...] = jnp.zeros_like(ref)
        ref[:, :cols, :] = value
    near_3 = three(near_s, (2, 1, 0), cols)
    total = jnp.zeros((8 * cols, channels), jnp.float32)
    for tap in range(3):
        at = 2 - tap
        total += lax.dot_general(
            near_3[at : at + 8].reshape(8 * cols, 3 * channels), transposed(near_ref, tap),
            (((1,), (1,)), ((), ())), preferred_element_type=jnp.float32,
        )
    feature = (total.reshape(8, cols, channels) + total_s[1:9, 1 : 1 + cols, :]).astype(low)
    out_ref[...] = feature[:, :COLS, :]

    valid = lax.broadcasted_iota(jnp.int32, (8, cols, channels), 1) < COLS
    own_near = jnp.where(valid, near_s[1:9, 1 : 1 + cols, :], 0.0)
    own_near = own_near.astype(low).reshape(8 * cols, channels)
    own_wide = jnp.where(valid, wide_s[5:13, EDGE : EDGE + cols, :], 0.0)
    own_wide = own_wide.astype(low).reshape(8 * cols, channels)
    feat_3 = three(feat_s, (9, 10, 11), cols)
    one_3 = three(one_s, (5, 9, 13), cols)
    long = 3 * channels
    for tap in range(3):
        for left, right, at in (
            (feat_3[4 + tap : 12 + tap], own_near, tap * long),
            (one_3[4 * tap : 4 * tap + 8], own_wide, (3 + tap) * long),
        ):
            term = contract_rows(left.reshape(8 * cols, long), right)
            term_ref[at : at + long, :] = (term * factor).astype(low)


def backward(lat_at, wide_all, attn_near, cot_near, near_slope, hidden_one, feat_x, conv_near,
             conv_wide, factor):
    channels = feat_x.shape[2]
    low = jnp.bfloat16
    shapes = [((8, COLS, channels), low), ((18 * channels, channels), low)]
    grown = [(18, 112), (10, 112), (10, 112), (16, 112), (18, 128), (10, 112), (10, 112)]
    return pl.pallas_call(
        functools.partial(backward_block, factor=factor),
        out_shape=[jax.ShapeDtypeStruct(s, t) for s, t in shapes],
        in_specs=[pl.BlockSpec(memory_space=pltpu.SMEM)]
        + [pl.BlockSpec(memory_space=pltpu.VMEM)] * 8,
        out_specs=[pl.BlockSpec(memory_space=pltpu.VMEM)] * 2,
        scratch_shapes=[pltpu.VMEM(g + (channels,), jnp.float32) for g in grown],
        compiler_params=pltpu.CompilerParams(vmem_limit_bytes=44 * 1024 * 1024),
        cost_estimate=pl.CostEstimate(
            flops=6 * 10**9, bytes_accessed=4 * 10**6, transcendentals=0
        ),
        name="backward_block",
    )(lat_at, wide_all, attn_near, cot_near, near_slope, hidden_one, feat_x, conv_near, conv_wide)


def reduce_all(terms):
    rows, channels = terms.shape
    part = rows // 32
    piece = part * channels // 16
    band = lax.all_to_all(
        terms.reshape(32, part, channels), ("x", "y", "core"), 0, 0, tiled=True
    )
    band = band.astype(jnp.float32).sum(0).astype(jnp.bfloat16).reshape(16, piece)
    band = lax.all_to_all(band, ("zh", "zl"), 0, 0, tiled=True)
    band = band.astype(jnp.float32).sum(0).astype(jnp.bfloat16)
    band = lax.all_to_all(
        jnp.broadcast_to(band[None], (16, piece)), ("zh", "zl"), 0, 0, tiled=True
    ).reshape(part, channels)
    return lax.all_to_all(
        jnp.broadcast_to(band[None], (32, part, channels)), ("x", "y", "core"), 0, 0, tiled=True
    ).reshape(rows, channels)


def on_device(
    features, queries, attn_keys, attn_values, cotangent, conv_near, conv_wide, proj_qkv, proj_out
):
    rows, cols, channels = features.shape
    factor = float(rows * cols * 512) ** (-0.5)
    lat_at = lax.axis_index(LAT_AXES).astype(jnp.int32).reshape(1)
    half_at = lax.axis_index("zh")

    def to_rows(*fields):
        grown = [jnp.pad(f, ((0, 0), (0, GROWN - f.shape[1]), (0, 0))) for f in fields]
        return lax.all_to_all(jnp.concatenate(grown, axis=1), PLANE, 0, 0, tiled=True)

    blank = jnp.zeros((rows, 1, channels), features.dtype)
    low, high = exchange_lon(
        jnp.concatenate([features[:, :10], cotangent[:, :EDGE], blank], axis=1),
        jnp.concatenate([features[:, -10:], cotangent[:, -EDGE:], blank], axis=1),
    )
    low, high, attn_keys, attn_values = lax.optimization_barrier(
        (low, high, attn_keys, attn_values)
    )

    side = channels // 2
    own_rows = to_rows(
        jnp.concatenate([attn_keys[..., :side], attn_values[..., :side]], axis=2),
        jnp.concatenate([attn_values[..., side:], attn_keys[..., side:]], axis=2),
        queries,
        cotangent,
    )

    feat_x = jnp.concatenate(
        [low[:, :10], features, high[:, :10], jnp.zeros((rows, 18, channels), features.dtype)],
        axis=1,
    )
    cot_x = jnp.concatenate(
        [low[:, 10:15], cotangent, high[:, 10:15], jnp.zeros((rows, 28, channels), features.dtype)],
        axis=1,
    )
    low, high = exchange_lat(
        jnp.concatenate([feat_x[-5:], cot_x[-1:]], axis=0),
        jnp.concatenate([feat_x[:5], cot_x[:1]], axis=0),
    )
    low, high, own_rows = lax.optimization_barrier((low, high, own_rows))
    far_one = lax.ppermute(own_rows[:, :GROWN], "zh", SWAP)
    far_two = lax.ppermute(own_rows[:, GROWN : 2 * GROWN], "zh", SWAP)
    feat_x = jnp.concatenate([low[:5], feat_x, high[:5]], axis=0)
    cot_near = jnp.concatenate([low[5:], cot_x, high[5:]], axis=0)[:, :112]

    hidden_two, hidden_one, near_slope, wide_slope = forward(lat_at, feat_x, conv_near, conv_wide)
    hid_far = lax.ppermute(hidden_two, "zh", SWAP)
    far_one, hidden_two = lax.optimization_barrier((far_one, hidden_two))

    half = HEADS // 2
    first = attention(own_rows, far_one, proj_out, (0, half))
    first, proj_out = lax.optimization_barrier((first, proj_out))
    own_part, far_edge, sent, out_term, own_qkv, far_kv = attention(
        own_rows, far_two, proj_out, (half, HEADS), first, proj_qkv
    )
    from_far = lax.ppermute(sent, "zh", SWAP)
    from_far, hid_far = lax.optimization_barrier((from_far, hid_far))
    whole = (own_part + from_far.astype(jnp.float32)).astype(jnp.bfloat16)
    whole = whole.reshape(4, 2, GROWN, channels)
    edge = from_far.reshape(4, 2, GROWN, channels)[:, :, COLS : COLS + EDGE].astype(jnp.float32)
    edge = (edge + far_edge.reshape(4, 2, 8, channels)[:, :, :EDGE]).astype(jnp.bfloat16)
    edge_low, edge_high = edge[:, 0], edge[:, 1]
    left = jnp.where(half_at == 1, edge_high, jnp.roll(edge_high, 1, axis=0))
    right = jnp.where(half_at == 0, edge_low, jnp.roll(edge_low, -1, axis=0))
    left = jnp.stack([left, whole[:, 0, COLS - EDGE : COLS]], axis=1)
    right = jnp.stack([whole[:, 1, :EDGE], right], axis=1)
    blank = jnp.zeros((4, 2, 12, channels), jnp.bfloat16)
    attn_x = jnp.concatenate([left, whole[:, :, :COLS], right, blank], axis=2)
    attn_x = lax.all_to_all(attn_x.reshape(8, 112, channels), PLANE, 0, 0, tiled=True)
    hid_rows = to_rows(hidden_two, hid_far)
    hid_flat = hid_rows[:, :GROWN].reshape(-1, channels)
    far_flat = hid_rows[:, GROWN:].reshape(-1, channels)
    query_term = contract_rows(hid_flat, own_qkv[:, :channels])
    kv_term = contract_rows(hid_flat, own_qkv[:, channels:]) + contract_rows(far_flat, far_kv)

    outer_x = cot_x[:, :112].astype(jnp.float32) + attn_x.astype(jnp.float32)
    wide_x = (outer_x * wide_slope).astype(jnp.bfloat16)
    low, high = exchange_lat(
        jnp.concatenate([wide_x[-5:], attn_x[-1:]], axis=0),
        jnp.concatenate([wide_x[:5], attn_x[:1]], axis=0),
    )
    wide_all = jnp.concatenate([low[:5], wide_x, high[:5]], axis=0)
    attn_near = jnp.concatenate([low[5:], attn_x, high[5:]], axis=0)
    feature_grad, conv_terms = backward(
        lat_at, wide_all, attn_near, cot_near, near_slope, hidden_one, feat_x, conv_near,
        conv_wide, factor,
    )

    others = jnp.concatenate([query_term, kv_term[:, :channels], kv_term[:, channels:], out_term])
    terms = jnp.concatenate([conv_terms, (others * factor).astype(jnp.bfloat16)])
    sums = reduce_all(terms).astype(jnp.float32)
    taps = 9 * channels
    near_sum = sums[:taps].reshape(3, 3, channels, channels)
    wide_sum = sums[taps : 2 * taps].reshape(3, 3, channels, channels)
    qkv_sum = jnp.concatenate(
        [sums[2 * taps + i * channels : 2 * taps + (i + 1) * channels] for i in range(3)], axis=1
    )
    out_sum = sums[2 * taps + 3 * channels :]
    return (feature_grad, near_sum, wide_sum, qkv_sum, out_sum)


def solution(mesh):
    grid = Mesh(mesh.devices.reshape(4, 2, 2, 8, 4), LON_AXES + LAT_AXES)
    field = P(LAT_AXES, LON_AXES, None)
    return jax.shard_map(
        on_device,
        mesh=grid,
        in_specs=(field,) * 5 + (P(),) * 4,
        out_specs=(field, P(), P(), P(), P()),
        check_vma=False,
    )
```

```python
import functools

import jax
import jax.numpy as jnp
from jax import lax
from jax.experimental import pallas as pl
from jax.experimental.pallas import tpu as pltpu
from jax.sharding import Mesh, PartitionSpec as P

HEADS = 8
COLS = 90
GROWN = 96
EDGE = 5
CHUNK = 256
GELU_COEF = 0.7978845608028654
CUBIC_COEF = 0.044715

LON_AXES = ("x", "zh", "core")
LAT_AXES = ("zl", "y")
PLANE = ("x", "core")
SWAP = [(0, 1), (1, 0)]


def gelu_value(pre_act):
    tanh_val = jnp.tanh(GELU_COEF * (pre_act + CUBIC_COEF * pre_act * pre_act * pre_act))
    return 0.5 * pre_act * (1.0 + tanh_val)


def gelu_slope(pre_act):
    tanh_val = jnp.tanh(GELU_COEF * (pre_act + CUBIC_COEF * pre_act * pre_act * pre_act))
    inner_d = GELU_COEF * (1.0 + 3.0 * CUBIC_COEF * pre_act * pre_act)
    return 0.5 * (1.0 + tanh_val) + 0.5 * pre_act * (1.0 - tanh_val * tanh_val) * inner_d


def contract_rows(left, right):
    return lax.dot_general(
        left, right, (((0,), (0,)), ((), ())), preferred_element_type=jnp.float32
    )


def exchange_lon(left, right):
    at_zero = lax.axis_index("core") == 0
    inner = lax.ppermute(jnp.where(at_zero, right, left), "core", SWAP)
    pairs = [(i, (i + 1) % 16 if i % 2 else (i - 1) % 16) for i in range(16)]
    outer = lax.ppermute(jnp.where(at_zero, left, right), LON_AXES, pairs)
    return jnp.where(at_zero, outer, inner), jnp.where(at_zero, inner, outer)


def exchange_lat(bottom, top):
    chain = [(i, i + 1) for i in range(31)]
    low = lax.ppermute(bottom, LAT_AXES, chain)
    high = lax.ppermute(top, LAT_AXES, [(b, a) for a, b in chain])
    return low, high


def attend_rows(*refs, heads, last):
    own_ref, far_ref, proj_ref = refs[:3]
    out_s, keep_s, grad_s, pair_s, value_s, key_g, value_g, query_g, mixed_g = refs[-9:]
    blocks, wide, channels = far_ref.shape
    rows = blocks * wide
    cols = 2 * rows
    pair_at, query_at, cot_at = (wide if last else 0), 2 * wide, 3 * wide
    width = channels // HEADS
    chunk = CHUNK
    low = jnp.bfloat16

    def rows_of(ref, at):
        return ref[:, at : at + wide, :].reshape(rows, channels)

    out_s[...] = lax.dot_general(
        rows_of(own_ref, cot_at), proj_ref[...], (((1,), (1,)), ((), ())),
        preferred_element_type=jnp.float32,
    )
    pair = jnp.concatenate([rows_of(own_ref, pair_at), rows_of(far_ref, 0)], axis=0).astype(jnp.float32)
    pair_s[...] = pair
    value_s[...] = pltpu.roll(pair, channels // 2, 1)
    for ref in (key_g, value_g, query_g, mixed_g):
        ref[...] = jnp.zeros_like(ref)
    lane_k = lax.broadcasted_iota(jnp.int32, (cols, channels), 1)
    filler = lax.broadcasted_iota(jnp.int32, (cols, channels), 0) % wide >= COLS
    lane_q = lax.broadcasted_iota(jnp.int32, (chunk, channels), 1)

    def one_head(head, carry):
        first = (head * width + width) % channels
        here_k = lane_k // width == head
        here_q = lane_q // width == head
        spare = jnp.where((lane_k == first) & filler, -1e30, 0.0)
        keys_h = jnp.where(here_k, pair_s[...], spare).astype(low)
        ones = jnp.where((lane_k == first) | (lane_k == first + 1), 1.0, 0.0)
        values_h = jnp.where(here_k, value_s[...], ones).astype(low)
        spots = [slice(at, at + chunk) for at in range(0, rows, chunk)]
        queries, douts, shares, query_n, dout_n = [], [], [], [], []
        for spot in spots:
            query = rows_of(own_ref, query_at)[spot].astype(jnp.float32) * 0.25
            query_h = jnp.where(here_q, query, jnp.where(lane_q == first, 1.0, 0.0)).astype(low)
            queries.append(jnp.where(here_q, query, 0.0))
            scores = lax.dot_general(
                query_h, keys_h, (((1,), (1,)), ((), ())), preferred_element_type=jnp.float32
            )
            top = jnp.max(scores, axis=1, keepdims=True)
            keep_s[spot, :] = jnp.exp(scores - top).astype(low)
        for spot in spots:
            dout = out_s[spot, :].astype(low).astype(jnp.float32)
            dout = jnp.where(here_q, dout, 0.0)
            mixed = jnp.dot(keep_s[spot, :], values_h, preferred_element_type=jnp.float32)
            total = jnp.sum(jnp.where(lane_q == first, mixed, 0.0), axis=1, keepdims=True)
            share = 1.0 / total
            mixed = jnp.where(here_q, mixed * share, 0.0)
            mixed_g[spot, :] += mixed
            delta = jnp.sum(dout * mixed, axis=1, keepdims=True)
            high = delta.astype(low).astype(jnp.float32)
            douts.append(
                jnp.where(
                    lane_q == first, -high, jnp.where(lane_q == first + 1, high - delta, dout)
                ).astype(low)
            )
            shares.append(share)
            dout_n.append((dout * share).astype(low))
        value_g[...] += lax.dot_general(
            keep_s[...], jnp.concatenate(dout_n, axis=0), (((0,), (0,)), ((), ())),
            preferred_element_type=jnp.float32,
        )
        for spot, dout_x in zip(spots, douts):
            prob_grad = lax.dot_general(
                dout_x, values_h, (((1,), (1,)), ((), ())), preferred_element_type=jnp.float32
            )
            grad_s[spot, :] = keep_s[spot, :] * prob_grad.astype(low)
        for spot, query, share in zip(spots, queries, shares):
            query_g[spot, :] += (
                jnp.dot(grad_s[spot, :], keys_h, preferred_element_type=jnp.float32)
                * (0.25 * share)
            )
            query_n.append((query * share).astype(low))
        key_g[...] += lax.dot_general(
            grad_s[...], jnp.concatenate(query_n, axis=0), (((0,), (0,)), ((), ())),
            preferred_element_type=jnp.float32,
        )
        return carry

    lax.fori_loop(heads[0], heads[1], one_head, 0)
    mixed = mixed_g[...].astype(low)
    grads = [query_g[...].astype(low)]
    grads += [ref[:rows, :].astype(low) for ref in (key_g, value_g)]
    aways = [ref[rows:, :].astype(low) for ref in (key_g, value_g)]
    if not last:
        mixed_ref, grad_ref, away_ref = refs[3:6]
        mixed_ref[...] = mixed
        grad_ref[...] = jnp.concatenate(grads, axis=1)
        away_ref[...] = jnp.concatenate(aways, axis=1)
        return
    mixed_ref, grad_ref, away_ref, qkv_ref = refs[3:7]
    part_ref, apart_ref, send_ref, term_ref, all_ref, far_all_ref = refs[7:13]
    own = jnp.concatenate(grads, axis=1) + grad_ref[...]
    far = jnp.concatenate(aways, axis=1) + away_ref[...]
    all_ref[...] = own
    far_all_ref[...] = far
    own_part = lax.dot_general(
        own, qkv_ref[...], (((1,), (1,)), ((), ())), preferred_element_type=jnp.float32
    )
    far_part = lax.dot_general(
        far, qkv_ref[:, channels:], (((1,), (1,)), ((), ())), preferred_element_type=jnp.float32
    )
    part_ref[...] = own_part.reshape(blocks, wide, channels)
    apart_ref[...] = jnp.zeros_like(apart_ref)
    query_g[...] = far_part
    for block in range(blocks):
        edge = 0 if block % 2 == 0 else COLS - EDGE
        at = block * wide + COLS
        apart_ref[block, :EDGE, :] = query_g[at - COLS + edge : at - COLS + edge + EDGE, :]
        query_g[at : at + EDGE, :] = part_ref[block, edge : edge + EDGE, :]
    send_ref[...] = query_g[...].astype(low).reshape(blocks, wide, channels)
    term_ref[...] = contract_rows(mixed + mixed_ref[...], rows_of(own_ref, cot_at))


def attention(own_rows, kv_far, proj_out, heads, first=None, proj_qkv=None):
    blocks, wide, channels = kv_far.shape
    rows = blocks * wide
    low = jnp.bfloat16
    operands = [own_rows, kv_far, proj_out]
    shapes = [((rows, channels), low), ((rows, 3 * channels), low), ((rows, 2 * channels), low)]
    if first is not None:
        operands += [*first, proj_qkv]
        shapes = [
            ((blocks, wide, channels), jnp.float32),
            ((blocks, 8, channels), jnp.float32),
            ((blocks, wide, channels), low),
            ((channels, channels), jnp.float32),
        ] + shapes[1:]
    return pl.pallas_call(
        functools.partial(attend_rows, heads=heads, last=first is not None),
        out_shape=[jax.ShapeDtypeStruct(s, t) for s, t in shapes],
        in_specs=[pl.BlockSpec(memory_space=pltpu.VMEM)] * len(operands),
        out_specs=[pl.BlockSpec(memory_space=pltpu.VMEM)] * len(shapes),
        scratch_shapes=[
            pltpu.VMEM((rows, channels), jnp.float32),
            pltpu.VMEM((rows, 2 * rows), low),
            pltpu.VMEM((rows, 2 * rows), low),
            pltpu.VMEM((2 * rows, channels), jnp.float32),
            pltpu.VMEM((2 * rows, channels), jnp.float32),
            pltpu.VMEM((2 * rows, channels), jnp.float32),
            pltpu.VMEM((2 * rows, channels), jnp.float32),
            pltpu.VMEM((rows, channels), jnp.float32),
            pltpu.VMEM((rows, channels), jnp.float32),
        ],
        compiler_params=pltpu.CompilerParams(vmem_limit_bytes=48 * 1024 * 1024),
        cost_estimate=pl.CostEstimate(
            flops=12 * rows * 2 * rows * channels * (heads[1] - heads[0]),
            bytes_accessed=16 * rows * channels,
            transcendentals=(heads[1] - heads[0]) * rows * 2 * rows,
        ),
        name="attend_rows",
    )(*operands)


def row_inside(lat_ref, shape, width):
    at = lat_ref[0] * 8 + lax.broadcasted_iota(jnp.int32, shape, 0) - width
    return (at >= 0) & (at < 256)


def three(ref, starts, count):
    return jnp.concatenate(
        [ref[:, at : at + count, :].astype(jnp.bfloat16) for at in starts], axis=2
    )


def forward_block(lat_ref, feat_ref, near_ref, wide_ref, two_ref, one_ref, nslope_ref, wslope_ref,
                  feat_s, one_s, wide_s):
    channels = feat_ref.shape[2]
    low = jnp.bfloat16
    cols = 112
    feat_s[...] = feat_ref[...].astype(jnp.float32)
    feat_3 = three(feat_s, (0, 1, 2), cols)
    total = jnp.zeros((16 * cols, channels), jnp.float32)
    for tap in range(3):
        weight = near_ref[tap].reshape(3 * channels, channels)
        total += jnp.dot(
            feat_3[tap : tap + 16].reshape(16 * cols, 3 * channels), weight,
            preferred_element_type=jnp.float32,
        )
    pre_near = total.reshape(16, cols, channels)
    nslope_ref[...] = gelu_slope(pre_near[3:13])
    one = (feat_s[1:17, 1 : 1 + cols, :] + gelu_value(pre_near)).astype(low)
    one = jnp.where(row_inside(lat_ref, one.shape, 4), one.astype(jnp.float32), 0.0)
    one_ref[...] = one.astype(low)
    one_s[...] = jnp.zeros_like(one_s)
    one_s[:, :cols, :] = one
    one_3 = three(one_s, (0, 4, 8), cols)
    total = jnp.zeros((8 * cols, channels), jnp.float32)
    for tap in range(3):
        weight = wide_ref[tap].reshape(3 * channels, channels)
        total += jnp.dot(
            one_3[4 * tap : 4 * tap + 8].reshape(8 * cols, 3 * channels), weight,
            preferred_element_type=jnp.float32,
        )
    pre_wide = total.reshape(8, cols, channels)
    wslope_ref[...] = gelu_slope(pre_wide)
    wide_s[...] = gelu_value(pre_wide)
    two = one_s[4:12, 9 : 9 + GROWN, :] + wide_s[:, EDGE : EDGE + GROWN, :]
    valid = lax.broadcasted_iota(jnp.int32, two.shape, 1) < COLS
    two_ref[...] = jnp.where(valid, two, 0.0).astype(low)


def forward(lat_at, feat_x, conv_near, conv_wide):
    channels = feat_x.shape[2]
    shapes = [
        ((8, GROWN, channels), jnp.bfloat16),
        ((16, 112, channels), jnp.bfloat16),
        ((10, 112, channels), jnp.float32),
        ((8, 112, channels), jnp.float32),
    ]
    return pl.pallas_call(
        forward_block,
        out_shape=[jax.ShapeDtypeStruct(s, t) for s, t in shapes],
        in_specs=[pl.BlockSpec(memory_space=pltpu.SMEM)]
        + [pl.BlockSpec(memory_space=pltpu.VMEM)] * 3,
        out_specs=[pl.BlockSpec(memory_space=pltpu.VMEM)] * 4,
        scratch_shapes=[
            pltpu.VMEM((18, 128, channels), jnp.float32),
            pltpu.VMEM((16, 128, channels), jnp.float32),
            pltpu.VMEM((8, 112, channels), jnp.float32),
        ],
        compiler_params=pltpu.CompilerParams(vmem_limit_bytes=40 * 1024 * 1024),
        cost_estimate=pl.CostEstimate(
            flops=6 * 10**9, bytes_accessed=4 * 10**6, transcendentals=2 * 10**5
        ),
        name="forward_block",
    )(lat_at, feat_x, conv_near, conv_wide)


def backward_block(lat_ref, wide_ref, attn_ref, cot_ref, nslope_ref, one_ref, feat_ref, near_ref,
                   dil_ref, out_ref, term_ref, wide_s, outer_s, slope_s, one_s, feat_s, total_s,
                   near_s, *, factor):
    channels = wide_ref.shape[2]
    low = jnp.bfloat16
    cols = GROWN

    def transposed(ref, tap):
        return jnp.concatenate([ref[tap, i] for i in range(3)], axis=1)

    wide_s[...] = wide_ref[...].astype(jnp.float32)
    outer_s[...] = cot_ref[...].astype(jnp.float32) + attn_ref[...].astype(jnp.float32)
    slope_s[...] = nslope_ref[...]
    one_s[...] = one_ref[...].astype(jnp.float32)
    feat_s[...] = feat_ref[...].astype(jnp.float32)
    wide_3 = three(wide_s, (8, 4, 0), cols)
    total = jnp.zeros((10 * cols, channels), jnp.float32)
    for tap in range(3):
        at = 8 - 4 * tap
        total += lax.dot_general(
            wide_3[at : at + 10].reshape(10 * cols, 3 * channels), transposed(dil_ref, tap),
            (((1,), (1,)), ((), ())), preferred_element_type=jnp.float32,
        )
    near_total = total.reshape(10, cols, channels) + outer_s[:, 4 : 4 + cols, :]
    near_grad = (near_total * slope_s[:, 8 : 8 + cols, :]).astype(low).astype(jnp.float32)
    near_grad = jnp.where(row_inside(lat_ref, near_grad.shape, 1), near_grad, 0.0)
    for ref, value in ((total_s, near_total), (near_s, near_grad)):
        ref[...] = jnp.zeros_like(ref)
        ref[:, :cols, :] = value
    near_3 = three(near_s, (2, 1, 0), cols)
    total = jnp.zeros((8 * cols, channels), jnp.float32)
    for tap in range(3):
        at = 2 - tap
        total += lax.dot_general(
            near_3[at : at + 8].reshape(8 * cols, 3 * channels), transposed(near_ref, tap),
            (((1,), (1,)), ((), ())), preferred_element_type=jnp.float32,
        )
    feature = (total.reshape(8, cols, channels) + total_s[1:9, 1 : 1 + cols, :]).astype(low)
    out_ref[...] = feature[:, :COLS, :]

    valid = lax.broadcasted_iota(jnp.int32, (8, cols, channels), 1) < COLS
    own_near = jnp.where(valid, near_s[1:9, 1 : 1 + cols, :], 0.0)
    own_near = own_near.astype(low).reshape(8 * cols, channels)
    own_wide = jnp.where(valid, wide_s[5:13, EDGE : EDGE + cols, :], 0.0)
    own_wide = own_wide.astype(low).reshape(8 * cols, channels)
    feat_3 = three(feat_s, (9, 10, 11), cols)
    one_3 = three(one_s, (5, 9, 13), cols)
    long = 3 * channels
    for tap in range(3):
        for left, right, at in (
            (feat_3[4 + tap : 12 + tap], own_near, tap * long),
            (one_3[4 * tap : 4 * tap + 8], own_wide, (3 + tap) * long),
        ):
            term = contract_rows(left.reshape(8 * cols, long), right)
            term_ref[at : at + long, :] = (term * factor).astype(low)


def backward(lat_at, wide_all, attn_near, cot_near, near_slope, hidden_one, feat_x, conv_near,
             conv_wide, factor):
    channels = feat_x.shape[2]
    low = jnp.bfloat16
    shapes = [((8, COLS, channels), low), ((18 * channels, channels), low)]
    grown = [(18, 112), (10, 112), (10, 112), (16, 112), (18, 128), (10, 112), (10, 112)]
    return pl.pallas_call(
        functools.partial(backward_block, factor=factor),
        out_shape=[jax.ShapeDtypeStruct(s, t) for s, t in shapes],
        in_specs=[pl.BlockSpec(memory_space=pltpu.SMEM)]
        + [pl.BlockSpec(memory_space=pltpu.VMEM)] * 8,
        out_specs=[pl.BlockSpec(memory_space=pltpu.VMEM)] * 2,
        scratch_shapes=[pltpu.VMEM(g + (channels,), jnp.float32) for g in grown],
        compiler_params=pltpu.CompilerParams(vmem_limit_bytes=44 * 1024 * 1024),
        cost_estimate=pl.CostEstimate(
            flops=6 * 10**9, bytes_accessed=4 * 10**6, transcendentals=0
        ),
        name="backward_block",
    )(lat_at, wide_all, attn_near, cot_near, near_slope, hidden_one, feat_x, conv_near, conv_wide)


def reduce_all(terms):
    rows, channels = terms.shape
    part = rows // 32
    piece = part * channels // 16
    band = lax.all_to_all(
        terms.reshape(32, part, channels), ("x", "y", "core"), 0, 0, tiled=True
    )
    band = band.astype(jnp.float32).sum(0).astype(jnp.bfloat16).reshape(16, piece)
    band = lax.all_to_all(band, ("zh", "zl"), 0, 0, tiled=True)
    band = band.astype(jnp.float32).sum(0).astype(jnp.bfloat16)
    band = lax.all_to_all(
        jnp.broadcast_to(band[None], (16, piece)), ("zh", "zl"), 0, 0, tiled=True
    ).reshape(part, channels)
    return lax.all_to_all(
        jnp.broadcast_to(band[None], (32, part, channels)), ("x", "y", "core"), 0, 0, tiled=True
    ).reshape(rows, channels)


def on_device(
    features, queries, attn_keys, attn_values, cotangent, conv_near, conv_wide, proj_qkv, proj_out
):
    rows, cols, channels = features.shape
    factor = float(rows * cols * 512) ** (-0.5)
    lat_at = lax.axis_index(LAT_AXES).astype(jnp.int32).reshape(1)
    half_at = lax.axis_index("zh")

    def to_rows(*fields):
        grown = [jnp.pad(f, ((0, 0), (0, GROWN - f.shape[1]), (0, 0))) for f in fields]
        return lax.all_to_all(jnp.concatenate(grown, axis=1), PLANE, 0, 0, tiled=True)

    blank = jnp.zeros((rows, 1, channels), features.dtype)
    low, high = exchange_lon(
        jnp.concatenate([features[:, :10], cotangent[:, :EDGE], blank], axis=1),
        jnp.concatenate([features[:, -10:], cotangent[:, -EDGE:], blank], axis=1),
    )
    low, high, attn_keys, attn_values = lax.optimization_barrier(
        (low, high, attn_keys, attn_values)
    )

    side = channels // 2
    own_rows = to_rows(
        jnp.concatenate([attn_keys[..., :side], attn_values[..., :side]], axis=2),
        jnp.concatenate([attn_values[..., side:], attn_keys[..., side:]], axis=2),
        queries,
        cotangent,
    )

    feat_x = jnp.concatenate(
        [low[:, :10], features, high[:, :10], jnp.zeros((rows, 18, channels), features.dtype)],
        axis=1,
    )
    cot_x = jnp.concatenate(
        [low[:, 10:15], cotangent, high[:, 10:15], jnp.zeros((rows, 28, channels), features.dtype)],
        axis=1,
    )
    low, high = exchange_lat(
        jnp.concatenate([feat_x[-5:], cot_x[-1:]], axis=0),
        jnp.concatenate([feat_x[:5], cot_x[:1]], axis=0),
    )
    low, high, own_rows = lax.optimization_barrier((low, high, own_rows))
    far_one = lax.ppermute(own_rows[:, :GROWN], "zh", SWAP)
    far_two = lax.ppermute(own_rows[:, GROWN : 2 * GROWN], "zh", SWAP)
    feat_x = jnp.concatenate([low[:5], feat_x, high[:5]], axis=0)
    cot_near = jnp.concatenate([low[5:], cot_x, high[5:]], axis=0)[:, :112]

    hidden_two, hidden_one, near_slope, wide_slope = forward(lat_at, feat_x, conv_near, conv_wide)
    far_one, hidden_two = lax.optimization_barrier((far_one, hidden_two))

    half = HEADS // 2
    first = attention(own_rows, far_one, proj_out, (0, half))
    first, proj_out, hidden_two = lax.optimization_barrier((first, proj_out, hidden_two))
    hid_far = lax.ppermute(hidden_two, "zh", SWAP)
    own_part, far_edge, sent, out_term, own_qkv, far_kv = attention(
        own_rows, far_two, proj_out, (half, HEADS), first, proj_qkv
    )
    sent, hid_far = lax.optimization_barrier((sent, hid_far))
    hid_rows = to_rows(hidden_two, hid_far)
    from_far = lax.ppermute(sent, "zh", SWAP)
    whole = (own_part + from_far.astype(jnp.float32)).astype(jnp.bfloat16)
    whole = whole.reshape(4, 2, GROWN, channels)
    edge = from_far.reshape(4, 2, GROWN, channels)[:, :, COLS : COLS + EDGE].astype(jnp.float32)
    edge = (edge + far_edge.reshape(4, 2, 8, channels)[:, :, :EDGE]).astype(jnp.bfloat16)
    edge_low, edge_high = edge[:, 0], edge[:, 1]
    left = jnp.where(half_at == 1, edge_high, jnp.roll(edge_high, 1, axis=0))
    right = jnp.where(half_at == 0, edge_low, jnp.roll(edge_low, -1, axis=0))
    left = jnp.stack([left, whole[:, 0, COLS - EDGE : COLS]], axis=1)
    right = jnp.stack([whole[:, 1, :EDGE], right], axis=1)
    blank = jnp.zeros((4, 2, 12, channels), jnp.bfloat16)
    attn_x = jnp.concatenate([left, whole[:, :, :COLS], right, blank], axis=2)
    attn_x = lax.all_to_all(attn_x.reshape(8, 112, channels), PLANE, 0, 0, tiled=True)
    hid_flat = hid_rows[:, :GROWN].reshape(-1, channels)
    far_flat = hid_rows[:, GROWN:].reshape(-1, channels)
    query_term = contract_rows(hid_flat, own_qkv[:, :channels])
    kv_term = contract_rows(hid_flat, own_qkv[:, channels:]) + contract_rows(far_flat, far_kv)

    outer_x = cot_x[:, :112].astype(jnp.float32) + attn_x.astype(jnp.float32)
    wide_x = (outer_x * wide_slope).astype(jnp.bfloat16)
    low, high = exchange_lat(
        jnp.concatenate([wide_x[-5:], attn_x[-1:]], axis=0),
        jnp.concatenate([wide_x[:5], attn_x[:1]], axis=0),
    )
    wide_all = jnp.concatenate([low[:5], wide_x, high[:5]], axis=0)
    attn_near = jnp.concatenate([low[5:], attn_x, high[5:]], axis=0)
    feature_grad, conv_terms = backward(
        lat_at, wide_all, attn_near, cot_near, near_slope, hidden_one, feat_x, conv_near,
        conv_wide, factor,
    )

    others = jnp.concatenate([query_term, kv_term[:, :channels], kv_term[:, channels:], out_term])
    terms = jnp.concatenate([conv_terms, (others * factor).astype(jnp.bfloat16)])
    sums = reduce_all(terms).astype(jnp.float32)
    taps = 9 * channels
    near_sum = sums[:taps].reshape(3, 3, channels, channels)
    wide_sum = sums[taps : 2 * taps].reshape(3, 3, channels, channels)
    qkv_sum = jnp.concatenate(
        [sums[2 * taps + i * channels : 2 * taps + (i + 1) * channels] for i in range(3)], axis=1
    )
    out_sum = sums[2 * taps + 3 * channels :]
    return (feature_grad, near_sum, wide_sum, qkv_sum, out_sum)


def solution(mesh):
    grid = Mesh(mesh.devices.reshape(4, 2, 2, 8, 4), LON_AXES + LAT_AXES)
    field = P(LAT_AXES, LON_AXES, None)
    return jax.shard_map(
        on_device,
        mesh=grid,
        in_specs=(field,) * 5 + (P(),) * 4,
        out_specs=(field, P(), P(), P(), P()),
        check_vma=False,
    )
```
